32 devices in a mesh: side: 2 (over y), grp: 2 (over x), dev: 8 (over z, core).
Axes of the slice: x: 2, y: 2, z: 4, core: 2. Of those that a mesh axis runs over, the one named last changes fastest.
Arguments:
- sources: float32 [2, 8, 4096], P('side', None, ('grp', 'dev')), may hold values from -2500 to 2500
- near_blocks: bfloat16 [2, 512, 128, 128], P('side', ('grp', 'dev')), may hold values from -0.125 to 0.125
- block_rows: int32 [2, 512], P('side', ('grp', 'dev')), may hold values from 0 to 1, as said below
- block_cols: int32 [2, 512], P('side', ('grp', 'dev')), may hold values from 0 to 31, as said below
- mirror: int32 [4096], P(('grp', 'dev')), may hold values from 0 to 127, as said below
Outputs:
- krylov_basis: float32 [4, 2, 8, 4096], P(None, 'side', None, ('grp', 'dev'))
- hessenberg: float32 [8, 4, 3], replicated
The draws below stay inside these ranges and needn't reach their ends.
Inputs may be any that keep to these rules, and one draw needn't show every extreme that they name: `block_rows`: in each device's aligned run of 32 entries, the first 2 are 0 to 1 in order. `block_cols`: in each device's aligned run of 32 entries, the first 2 name that device's own blocks in order, and every entry names a block of an owner at most 4 owners before or after that device (owners of a half counted in the order grp, dev); where such owners exist, some entry names a block of the owner 4 before and some one of the owner 4 after. `mirror`: each aligned run of 128 entries is a permutation of 0 to 127.
All inputs are finite; a program needn't handle non-finite values.
Results may differ from the reference program's by a relative error of at most 0.005.
Values may be sent and summed in bfloat16 or wider, within the bound.
No kernel may reach another device: no remote copies, remote signals or barrier semaphores. Data moves between devices by JAX's collectives and lax.ppermute only.
A program may use at most 64 MiB of HBM per device.

```python
import math
import jax
import jax.numpy as jnp
from jax import lax

BLOCK = 128
BLK_DEV = 2
NEAR = 16
WIN = 4
NRHS = 8
ITERS = 3
NB_DEV = 32
NBH = 32
NH = 4096
NBT = 512
N_GRP = 2
N_DEV = 8


def draw_sources(key, part):
    keys = jax.random.split(jax.random.fold_in(key, 11), 3)
    shape = (2, NRHS, NH)
    position = (jnp.arange(2, dtype=jnp.float32)[:, None, None] * NH + jnp.arange(NH, dtype=jnp.float32)[None, None, :]) / (2.0 * NH)
    row_scale = jnp.exp(jax.random.uniform(keys[1], (2, 1, NH), jnp.float32, 0.0, math.log(10.0)))
    col_scale = jnp.exp(jax.random.uniform(keys[2], (1, NRHS, 1), jnp.float32, 0.0, math.log(10.0)))
    base = jnp.clip(jax.random.normal(keys[0], shape, jnp.float32), -4.0, 4.0)
    ramp = jnp.exp(math.log(3.0) * position)
    return base * row_scale * col_scale * ramp


def draw_block_rows(key, part):
    entry = jnp.arange(NBT, dtype=jnp.int32)
    within = entry % NB_DEV
    random_rows = jax.random.randint(jax.random.fold_in(key, 21), (2, NBT), 0, BLK_DEV, dtype=jnp.int32)
    return jnp.where(within[None, :] < BLK_DEV, within[None, :], random_rows).astype(jnp.int32)


def draw_block_cols(key, part):
    entry = jnp.arange(NBT, dtype=jnp.int32)
    within = entry % NB_DEV
    owner = entry // NB_DEV
    own_block = owner * BLK_DEV + within
    first_reach = (owner - WIN) * BLK_DEV
    last_reach = (owner + WIN + 1) * BLK_DEV - 1
    offsets = jax.random.randint(jax.random.fold_in(key, 31), (2, NBT), -WIN * BLK_DEV, (WIN + 1) * BLK_DEV, dtype=jnp.int32)
    random_cols = owner[None, :] * BLK_DEV + offsets
    chosen = jnp.where(within[None, :] == BLK_DEV, first_reach[None, :], random_cols)
    chosen = jnp.where(within[None, :] == BLK_DEV + 1, last_reach[None, :], chosen)
    chosen = jnp.clip(chosen, 0, NBH - 1)
    return jnp.where(within[None, :] < BLK_DEV, own_block[None, :], chosen).astype(jnp.int32)


def draw_mirror(key, part):
    keys = jax.random.split(jax.random.fold_in(key, 41), NBH)
    perms = jax.vmap(lambda single: jax.random.permutation(single, BLOCK))(keys)
    return perms.reshape(NH).astype(jnp.int32)


def levels(stream_key, extent, cuts, low, largest):
    gain, own = 1.0, jax.random.fold_in(stream_key, 6)
    for axis_at, shards_of in cuts:
        heights = jnp.exp(jax.random.uniform(jax.random.fold_in(own, axis_at), (shards_of,), jnp.float32, low / len(cuts), largest / len(cuts)))
        gain = gain * jnp.repeat(heights, extent[axis_at] // shards_of).reshape([-1 if axis == axis_at else 1 for axis in range(len(extent))])
    return gain


def gaussian(key, dims, scale, most, cuts=(), held_as=jnp.bfloat16):
    factor_of = levels(key, dims, cuts, -0.22, 0.18) if cuts else 1.0
    values = jax.random.normal(key, dims, jnp.float32) * scale * factor_of
    return jnp.minimum(jnp.maximum(values, -most), most).astype(held_as)


def setup_inputs(seed: int = 0) -> dict:
    seeds = jax.random.split(jax.random.key(seed), 6)
    sources = draw_sources(jax.random.fold_in(seeds[5], 71), 0)
    near_blocks = gaussian(seeds[1], (2, NBT, BLOCK, BLOCK), (NEAR * BLOCK) ** -0.5, 0.125, ((0, 2), (1, 16)))
    block_rows = draw_block_rows(jax.random.fold_in(seeds[5], 71), 0)
    block_cols = draw_block_cols(jax.random.fold_in(seeds[5], 71), 0)
    mirror = draw_mirror(jax.random.fold_in(seeds[5], 71), 0)
    return dict(sources=sources, near_blocks=near_blocks, block_rows=block_rows, block_cols=block_cols, mirror=mirror)


epsilon = 1e-06

def reference(sources, near_blocks, block_rows, block_cols, mirror):
    owners = N_GRP * N_DEV
    total_panels = 2.0 * NH
    vectors = sources.shape[1]
    mirror_onehot = (mirror.reshape(NBH, BLOCK)[:, :, None] == jnp.arange(BLOCK, dtype=jnp.int32)[None, None, :]).astype(jnp.float32)

    def mirrored(vector):
        shaped = vector.reshape(vectors, NBH, BLOCK)
        return jnp.einsum('bij,rbj->rbi', mirror_onehot, shaped, precision=lax.Precision.HIGHEST).reshape(vectors, NH)

    def unmirrored(vector):
        shaped = vector.reshape(vectors, NBH, BLOCK)
        return jnp.einsum('bij,rbi->rbj', mirror_onehot, shaped, precision=lax.Precision.HIGHEST).reshape(vectors, NH)

    def near_field(field, half):
        rounded = lax.optimization_barrier(field.astype(jnp.bfloat16)).astype(jnp.float32)
        field_blocks = rounded.reshape(vectors, NBH, BLOCK)
        all_blocks = near_blocks[half].reshape(owners, NB_DEV, BLOCK, BLOCK)
        all_rows = block_rows[half].reshape(owners, NB_DEV)
        all_cols = block_cols[half].reshape(owners, NB_DEV)

        def per_owner(pieces):
            owner_blocks, owner_rows, owner_cols = pieces
            picked = field_blocks[:, owner_cols]
            products = jnp.einsum('rkj,kij->rki', picked, owner_blocks.astype(jnp.float32), precision=lax.Precision.HIGHEST)
            row_onehot = (owner_rows[None, :] == jnp.arange(BLK_DEV, dtype=jnp.int32)[:, None]).astype(jnp.float32)
            return jnp.einsum('bk,rki->rbi', row_onehot, products, precision=lax.Precision.HIGHEST)
        summed = lax.map(per_owner, (all_blocks, all_rows, all_cols))
        summed = jnp.transpose(summed, (1, 0, 2, 3)).reshape(vectors, NH)
        return 0.5 * field + summed

    def operator(vector):
        symmetric = vector[0] + mirrored(vector[1])
        antisym = vector[0] - mirrored(vector[1])
        image_sym = near_field(symmetric, 0)
        image_anti = near_field(antisym, 1)
        return jnp.stack([0.5 * (image_sym + image_anti), unmirrored(0.5 * (image_sym - image_anti))])
    squares = lax.optimization_barrier(jnp.sum(sources * sources, axis=(0, 2))) / total_panels
    length = jnp.sqrt(squares + epsilon)
    vectors_list = [sources / length[None, :, None]]
    hessenberg = jnp.zeros((vectors, ITERS + 1, ITERS), jnp.float32)
    for column in range(ITERS):
        image = operator(vectors_list[column])
        stacked = jnp.stack(vectors_list)
        coeffs = lax.optimization_barrier(jnp.sum(image[None] * stacked, axis=(1, 3))) / total_panels
        remainder = image - jnp.einsum('jr,jsrp->srp', coeffs, stacked, precision=lax.Precision.HIGHEST)
        rem_norm = jnp.sqrt(lax.optimization_barrier(jnp.sum(remainder * remainder, axis=(0, 2))) / total_panels + epsilon)
        vectors_list.append(remainder / rem_norm[None, :, None])
        hessenberg = hessenberg.at[:, :column + 1, column].set(coeffs.T)
        hessenberg = hessenberg.at[:, column + 1, column].set(rem_norm)
    return (jnp.stack(vectors_list), hessenberg)
```

```python
import functools

import jax
import jax.numpy as jnp
from jax import lax
from jax.experimental import pallas as pl
from jax.experimental.pallas import tpu as pltpu
from jax.sharding import PartitionSpec as P

BLOCK = 128
BLK_DEV = 2
ITERS = 3
ROWS = 8
HALF_RHS = 4
EPSILON = 1e-06
AXES = ("side", "grp", "dev")
VMEM_LIMIT = 48 * 2**20


def position():
    side = lax.axis_index("side")
    dev = lax.axis_index("dev")
    owner = lax.axis_index("grp") * lax.axis_size("dev") + dev
    return side, owner, lax.rem(dev, 2)


def per_rhs(tile):
    column = jnp.sum(tile, axis=1, keepdims=True)
    return column + jnp.concatenate([column[HALF_RHS:], column[:HALF_RHS]], axis=0)


def dot(left, right):
    return per_rhs(jnp.sum(left * right, axis=0))


def mirror_onehot(mirror_ref, block):
    rows = lax.broadcasted_iota(jnp.int32, (BLOCK, BLOCK), 0)
    return (rows == mirror_ref[block : block + 1, :]).astype(jnp.float32)


def exact_dot(left, right, dims):
    return lax.dot_general(
        left, right, (dims, ((), ())),
        precision=lax.Precision.HIGHEST, preferred_element_type=jnp.float32,
    )


def start_kernel(sources_ref, mirror_ref, chunk_ref):
    side, _, _ = position()
    pieces = []
    for block in range(BLK_DEV):
        part = sources_ref[:, block * BLOCK : (block + 1) * BLOCK]
        moved = exact_dot(part, mirror_onehot(mirror_ref, block), ((1,), (0,)))
        pieces.append(jnp.where(side == 0, part, moved))
    tiles = [
        jnp.concatenate([piece[HALF_RHS * c : HALF_RHS * (c + 1)] for piece in pieces], axis=0)
        for c in range(2)
    ]
    pairs = chunk_ref.shape[0] // 2

    def store(pair, carry):
        chunk_ref[2 * pair] = tiles[0]
        chunk_ref[2 * pair + 1] = tiles[1]
        return carry

    lax.fori_loop(0, pairs, store, 0, unroll=pairs <= 32)


def near_product(vector_ref, turned_ref, blocks_ref, places_ref):
    half_of_row = lax.broadcasted_iota(jnp.int32, (ROWS, BLOCK), 0) // HALF_RHS
    count = blocks_ref.shape[0]
    sums = [jnp.zeros((ROWS, BLOCK), jnp.float32) for _ in range(4)]
    for entry in range(count):
        row = places_ref[0, entry]
        col = places_ref[1, entry]
        owner = col // 2
        turn = lax.rem(row + col, 2)
        tile = turned_ref[turn, owner]
        tile = jnp.where(half_of_row == row, tile, 0.0).astype(jnp.bfloat16)
        product = lax.dot_general(
            tile, blocks_ref[entry], (((1,), (1,)), ((), ())), preferred_element_type=jnp.float32
        )
        sums[entry % 4] = sums[entry % 4] + product
    return (sums[0] + sums[1]) + (sums[2] + sums[3])


def image(vector_ref, turned_ref, own_ref, other_ref, own_places, other_places):
    side, owner, core = position()
    owners = vector_ref.shape[0] // 2
    first = side * owners

    def fill(index, carry):
        tile = vector_ref[first + index]
        turned_ref[0, index] = tile
        turned_ref[1, index] = jnp.concatenate([tile[HALF_RHS:], tile[:HALF_RHS]], axis=0)
        return carry

    lax.fori_loop(0, owners, fill, 0, unroll=owners <= 32)
    own = near_product(vector_ref, turned_ref, own_ref, own_places)
    other = near_product(vector_ref, turned_ref, other_ref, other_places)
    base = owner - core
    low = jnp.where(core == 0, own, other) + 0.5 * turned_ref[0, base]
    high = jnp.where(core == 0, other, own) + 0.5 * turned_ref[0, base + 1]
    return low, high


def spread(chunk_ref, low, high):
    chips = chunk_ref.shape[0]

    def store(chip, carry):
        chunk_ref[chip, 0] = low
        chunk_ref[chip, 1] = high
        return carry

    lax.fori_loop(0, chips, store, 0, unroll=chips <= 32)


def first_kernel(total, got_ref, own_ref, other_ref, own_places, other_places, chunk_ref,
                 basis_ref, turned_ref):
    owners = got_ref.shape[0] // 2
    port = got_ref[:owners]
    star = got_ref[owners:]
    squares = per_rhs(jnp.sum(port * port + star * star, axis=0))
    scale = 1.0 / jnp.sqrt(squares * (1.0 / total) + EPSILON)
    basis_ref[:owners] = (port + star) * scale
    basis_ref[owners:] = (port - star) * scale
    low, high = image(basis_ref, turned_ref, own_ref, other_ref, own_places, other_places)
    spread(chunk_ref, low, high)


def orthogonalized(total, got, basis_refs):
    inner = 0.5 / total
    coeffs = [dot(got, ref[...]) * inner for ref in basis_refs]
    rest = got
    for coeff, ref in zip(coeffs, basis_refs):
        rest = rest - coeff * ref[...]
    norm = jnp.sqrt(dot(rest, rest) * inner + EPSILON)
    return coeffs, norm, rest * (1.0 / norm)


def columns(values):
    lane = lax.broadcasted_iota(jnp.int32, (ROWS, BLOCK), 1)
    tile = jnp.zeros((ROWS, BLOCK), jnp.float32)
    for index, value in enumerate(values):
        tile = jnp.where(lane == index, value, tile)
    return tile


def middle_kernel(total, got_ref, basis_ref, own_ref, other_ref, own_places, other_places,
                  chunk_ref, next_ref, coeff_ref, turned_ref):
    coeffs, norm, vector = orthogonalized(total, got_ref[...], [basis_ref])
    next_ref[...] = vector
    coeff_ref[...] = columns(coeffs + [norm])
    low, high = image(next_ref, turned_ref, own_ref, other_ref, own_places, other_places)
    spread(chunk_ref, low, high)


def last_kernel(total, got_ref, zero_ref, one_ref, coeff_ref, own_ref, other_ref, own_places,
                other_places, chunk_ref, mine_ref, theirs_ref, two_ref, turned_ref):
    side, owner, core = position()
    owners = got_ref.shape[0] // 2
    inner = 0.5 / total
    coeffs, norm, vector = orthogonalized(total, got_ref[...], [zero_ref, one_ref])
    two_ref[...] = vector
    refs = [zero_ref, one_ref, two_ref]
    gram = [
        dot(refs[i][...], refs[j][...]) * inner for i in range(ITERS) for j in range(i, ITERS)
    ]
    low, high = image(two_ref, turned_ref, own_ref, other_ref, own_places, other_places)
    base = side * owners + owner - core
    partial = [per_rhs(low * ref[base] + high * ref[base + 1]) for ref in refs]
    partial.append(per_rhs(low * low + high * high))
    first = coeff_ref[...]
    sums = columns(partial + [first[:, 0:1], first[:, 1:2]] + coeffs + [norm] + gram)
    chips = chunk_ref.shape[0] // 2

    def store(chip, carry):
        chunk_ref[2 * chip, 0] = low
        chunk_ref[2 * chip, 1] = sums
        chunk_ref[2 * chip + 1, 0] = high
        chunk_ref[2 * chip + 1, 1] = sums
        return carry

    lax.fori_loop(0, chips, store, 0, unroll=chips <= 32)
    for index, ref in enumerate(refs):
        for half in range(2):
            mine_ref[2 * index + half] = ref[half * owners + owner]
            theirs_ref[2 * index + half] = ref[half * owners + owner + 1 - 2 * core]


def final_kernel(total, got_ref, mine_ref, theirs_ref, mirror_ref, basis_ref, hessenberg_ref):
    side, owner, core = position()
    devices = got_ref.shape[0]
    owners = devices // 2
    inner = 0.5 / total
    lane3 = lax.broadcasted_iota(jnp.int32, (ROWS, ITERS), 1)
    entries = []
    halves = []
    for which in range(2):
        sums = got_ref[which, 1]
        for device in range(1, devices // 2):
            sums = sums + got_ref[2 * device + which, 1]
        known = got_ref[which, 1]
        coeffs = [sums[:, j : j + 1] * inner for j in range(ITERS)]
        gram = {}
        place = 9
        for i in range(ITERS):
            for j in range(i, ITERS):
                gram[i, j] = gram[j, i] = known[:, place : place + 1]
                place += 1
        squares = sums[:, ITERS : ITERS + 1] * inner
        for i in range(ITERS):
            weight = -2.0 * coeffs[i]
            for j in range(ITERS):
                weight = weight + coeffs[j] * gram[i, j]
            squares = squares + coeffs[i] * weight
        norm = jnp.sqrt(jnp.maximum(squares, 0.0) + EPSILON)
        entries.append(
            {
                (0, 0): known[:, 4:5], (1, 0): known[:, 5:6],
                (0, 1): known[:, 6:7], (1, 1): known[:, 7:8], (2, 1): known[:, 8:9],
                (0, 2): coeffs[0], (1, 2): coeffs[1], (2, 2): coeffs[2], (3, 2): norm,
            }
        )
        is_mine = core == which
        tiles = [jnp.where(is_mine, mine_ref[n], theirs_ref[n]) for n in range(2 * ITERS)]
        scale = 1.0 / norm
        for half in range(2):
            rest = got_ref[half * owners + owner - core + which, 0]
            for j in range(ITERS):
                rest = rest - coeffs[j] * tiles[2 * j + half]
            tiles.append(rest * scale)
        halves.append(tiles)
    for block in range(BLK_DEV):
        onehot = mirror_onehot(mirror_ref, block)
        rows = slice(block * HALF_RHS, (block + 1) * HALF_RHS)
        stacked = []
        for vector in range(ITERS + 1):
            sym = jnp.concatenate([tiles[2 * vector][rows] for tiles in halves], axis=0)
            anti = jnp.concatenate([tiles[2 * vector + 1][rows] for tiles in halves], axis=0)
            stacked.append((0.5 * (sym + anti), 0.5 * (sym - anti)))
        star = jnp.concatenate([pair[1] for pair in stacked], axis=0)
        back = exact_dot(star, onehot, ((1,), (1,)))
        for vector in range(ITERS + 1):
            basis_ref[vector, :, block * BLOCK : (block + 1) * BLOCK] = jnp.where(
                side == 0, stacked[vector][0], back[vector * ROWS : (vector + 1) * ROWS]
            )
    for j in range(ITERS + 1):
        row = jnp.zeros((ROWS, ITERS), jnp.float32)
        for k in range(ITERS):
            if (j, k) in entries[0]:
                both = jnp.concatenate(
                    [entry[j, k][:HALF_RHS] for entry in entries], axis=0
                )
                row = jnp.where(lane3 == k, both, row)
        hessenberg_ref[:, j, :] = row


VMEM = pl.BlockSpec(memory_space=pltpu.VMEM)
SMEM = pl.BlockSpec(memory_space=pltpu.SMEM)


def call(kernel, outs, specs, scratch=(), name=None):
    return pl.pallas_call(
        kernel,
        out_shape=[jax.ShapeDtypeStruct(shape, jnp.float32) for shape in outs],
        in_specs=specs,
        out_specs=[VMEM] * len(outs),
        scratch_shapes=[pltpu.VMEM(shape, jnp.float32) for shape in scratch],
        compiler_params=pltpu.CompilerParams(vmem_limit_bytes=VMEM_LIMIT),
        name=name,
    )


def on_device(sources, near_blocks, block_rows, block_cols, mirror):
    devices = lax.axis_size(AXES)
    owners = devices // 2
    chips = devices // 2
    panels = sources.shape[2]
    total = 1.0 * panels * devices
    partner = [(i, i ^ 1) for i in range(devices)]
    same_core = [[i for i in range(devices) if i % 2 == core] for core in range(2)]
    mirror_rows = mirror.reshape(BLK_DEV, BLOCK)
    blocks = near_blocks[0]
    places = jnp.concatenate([block_rows, block_cols], axis=0)
    other_blocks = lax.ppermute(blocks, AXES, partner)
    other_places = lax.ppermute(places, AXES, partner)
    near = (blocks, other_blocks, places, other_places)
    near_specs = [VMEM, VMEM, SMEM, SMEM]
    vector = (devices, ROWS, BLOCK)
    chunk = (chips, 2, ROWS, BLOCK)
    turned = (2, owners, ROWS, BLOCK)

    def exchanged(chunks):
        got = lax.all_to_all(chunks, AXES, 0, 0, axis_index_groups=same_core)
        return got.reshape(vector)

    [chunks] = call(start_kernel, [vector], [VMEM, VMEM], name="start")(sources[0], mirror_rows)
    got = lax.all_to_all(chunks, AXES, 0, 0)
    chunks, zero = call(
        functools.partial(first_kernel, total), [chunk, vector], [VMEM] + near_specs, [turned],
        name="first",
    )(got, *near)
    got = exchanged(chunks)
    chunks, one, coeff = call(
        functools.partial(middle_kernel, total), [chunk, vector, (ROWS, BLOCK)],
        [VMEM, VMEM] + near_specs, [turned], name="middle",
    )(got, zero, *near)
    got = exchanged(chunks)
    kept = (2 * ITERS, ROWS, BLOCK)
    chunks, mine, theirs = call(
        functools.partial(last_kernel, total), [(devices, 2, ROWS, BLOCK), kept, kept],
        [VMEM] * 4 + near_specs, [vector, turned], name="last",
    )(got, zero, one, coeff, *near)
    returned = lax.ppermute(theirs, AXES, partner)
    got = lax.all_to_all(chunks, AXES, 0, 0)
    basis, hessenberg = call(
        functools.partial(final_kernel, total),
        [(ITERS + 1, ROWS, panels), (ROWS, ITERS + 1, ITERS)], [VMEM] * 4, name="final",
    )(got, mine, returned, mirror_rows)
    return basis[:, None], hessenberg


def solution(mesh):
    placed = (
        P("side", None, ("grp", "dev")),
        P("side", ("grp", "dev"), None, None),
        P("side", ("grp", "dev")),
        P("side", ("grp", "dev")),
        P(("grp", "dev")),
    )
    return jax.shard_map(
        on_device,
        mesh=mesh,
        in_specs=placed,
        out_specs=(P(None, "side", None, ("grp", "dev")), P()),
        check_vma=False,
    )
```

```python
import functools

import jax
import jax.numpy as jnp
from jax import lax
from jax.experimental import pallas as pl
from jax.experimental.pallas import tpu as pltpu
from jax.sharding import PartitionSpec as P

BLOCK = 128
BLK_DEV = 2
ITERS = 3
ROWS = 8
HALF_RHS = 4
EPSILON = 1e-06
AXES = ("side", "grp", "dev")
VMEM_LIMIT = 48 * 2**20
PAIRS = [(i, j) for i in range(ITERS) for j in range(i, ITERS)]


def position():
    side = lax.axis_index("side")
    dev = lax.axis_index("dev")
    owner = lax.axis_index("grp") * lax.axis_size("dev") + dev
    return side, owner, lax.rem(dev, 2)


def iota(shape, axis):
    return lax.broadcasted_iota(jnp.int32, shape, axis)


def per_rhs(tile):
    column = jnp.sum(tile, axis=1, keepdims=True)
    return column + jnp.concatenate([column[HALF_RHS:], column[:HALF_RHS]], axis=0)


def dot(left, right):
    return per_rhs(jnp.sum(left * right, axis=0))


def columns(values):
    lane = iota((ROWS, BLOCK), 1)
    tile = jnp.zeros((ROWS, BLOCK), jnp.float32)
    for index, value in values.items():
        tile = jnp.where(lane == index, value, tile)
    return tile


def mirror_onehot(mirror_ref, block):
    return (iota((BLOCK, BLOCK), 0) == mirror_ref[block : block + 1, :]).astype(jnp.float32)


def exact_dot(left, right, dims):
    return lax.dot_general(
        left, right, (dims, ((), ())),
        precision=lax.Precision.HIGHEST, preferred_element_type=jnp.float32,
    )


def start_kernel(sources_hbm, mirror_hbm, chunk_ref, sources_ref, mirror_ref, sems):
    copies = [
        pltpu.make_async_copy(sources_hbm, sources_ref, sems.at[0]),
        pltpu.make_async_copy(mirror_hbm, mirror_ref, sems.at[1]),
    ]
    for copy in copies:
        copy.start()
    for copy in copies:
        copy.wait()
    side, _, _ = position()
    pieces = []
    for block in range(BLK_DEV):
        part = sources_ref[:, block * BLOCK : (block + 1) * BLOCK]
        moved = exact_dot(part, mirror_onehot(mirror_ref, block), ((1,), (0,)))
        pieces.append(jnp.where(side == 0, part, moved))
    tiles = [
        jnp.concatenate([piece[HALF_RHS * c : HALF_RHS * (c + 1)] for piece in pieces], axis=0)
        for c in range(2)
    ]
    chips = chunk_ref.shape[0] // 2

    def store(chip, carry):
        chunk_ref[2 * chip] = tiles[0]
        chunk_ref[2 * chip + 1] = tiles[1]
        return carry

    lax.fori_loop(0, chips, store, 0, unroll=chips <= 32)


def prepare_kernel(blocks_hbm, own_places, other_places, blocks_ref, pick_ref, sem):
    copy = pltpu.make_async_copy(blocks_hbm, blocks_ref, sem)
    copy.start()
    width = pick_ref.shape[1]
    half_of_row = iota((ROWS, width), 0) // HALF_RHS
    rhs_of_row = iota((ROWS, width), 0) % HALF_RHS
    lane = iota((ROWS, width), 1)
    for entry in range(blocks_ref.shape[0]):
        picks = []
        for places in (own_places, other_places):
            place = jnp.where(
                half_of_row == places[0, entry], HALF_RHS * places[1, entry] + rhs_of_row, -1
            )
            picks.append((lane == place).astype(jnp.float32))
        first = 2 * ROWS * entry
        pick_ref[first : first + 2 * ROWS, :] = jnp.concatenate(picks, axis=0).astype(jnp.bfloat16)
    copy.wait()


def image(vector_ref, pick_ref, own_ref, other_ref):
    side, owner, core = position()
    owners = vector_ref.shape[0] // 2
    half = vector_ref[pl.ds(side * owners, owners)]
    rounded = half.reshape(owners * ROWS, BLOCK).astype(jnp.bfloat16)
    picked = lax.dot_general(
        pick_ref[...], rounded, (((1,), (0,)), ((), ())), preferred_element_type=jnp.float32
    ).astype(jnp.bfloat16)
    sums = [jnp.zeros((2 * ROWS, 2 * BLOCK), jnp.float32) for _ in range(2)]
    for entry in range(0, own_ref.shape[0], 2):
        first = 2 * ROWS * entry
        left = jnp.concatenate(
            [picked[first : first + 2 * ROWS], picked[first + 2 * ROWS : first + 4 * ROWS]], axis=1
        )
        right = jnp.concatenate(
            [jnp.concatenate([ref[entry], ref[entry + 1]], axis=1) for ref in (own_ref, other_ref)],
            axis=0,
        )
        sums[entry // 2 % 2] += lax.dot_general(
            left, right, (((1,), (1,)), ((), ())), preferred_element_type=jnp.float32
        )
    total = sums[0] + sums[1]
    own = total[:ROWS, :BLOCK]
    other = total[ROWS:, BLOCK:]
    base = side * owners + owner - core
    low = jnp.where(core == 0, own, other) + 0.5 * vector_ref[base]
    high = jnp.where(core == 0, other, own) + 0.5 * vector_ref[base + 1]
    return low, high


def spread(chunk_ref, low, high):
    chips = chunk_ref.shape[0]

    def store(chip, carry):
        chunk_ref[chip, 0] = low
        chunk_ref[chip, 1] = high
        return carry

    lax.fori_loop(0, chips, store, 0, unroll=chips <= 32)


def first_kernel(total, got_ref, pick_ref, own_ref, other_ref, chunk_ref, basis_ref):
    owners = got_ref.shape[0] // 2
    port = got_ref[:owners]
    star = got_ref[owners:]
    squares = per_rhs(jnp.sum(port * port + star * star, axis=0))
    scale = 1.0 / jnp.sqrt(squares * (1.0 / total) + EPSILON)
    basis_ref[:owners] = (port + star) * scale
    basis_ref[owners:] = (port - star) * scale
    spread(chunk_ref, *image(basis_ref, pick_ref, own_ref, other_ref))


def orthogonalized(total, got, basis_refs):
    inner = 0.5 / total
    coeffs = [dot(got, ref[...]) * inner for ref in basis_refs]
    rest = got
    for coeff, ref in zip(coeffs, basis_refs):
        rest = rest - coeff * ref[...]
    norm = jnp.sqrt(dot(rest, rest) * inner + EPSILON)
    return coeffs + [norm], rest * (1.0 / norm)


def middle_kernel(total, got_ref, basis_ref, pick_ref, own_ref, other_ref, chunk_ref, next_ref,
                  coeff_ref):
    coeffs, next_ref[...] = orthogonalized(total, got_ref[...], [basis_ref])
    coeff_ref[...] = columns(dict(enumerate(coeffs)))
    spread(chunk_ref, *image(next_ref, pick_ref, own_ref, other_ref))


def last_kernel(total, got_ref, zero_ref, one_ref, coeff_ref, pick_ref, own_ref, other_ref,
                chunk_ref, mine_ref, theirs_ref, two_ref):
    side, owner, core = position()
    owners = got_ref.shape[0] // 2
    coeffs, two_ref[...] = orthogonalized(total, got_ref[...], [zero_ref, one_ref])
    refs = [zero_ref, one_ref, two_ref]
    tiles = image(two_ref, pick_ref, own_ref, other_ref)
    base = side * owners + owner - core
    basis = [[ref[base], ref[base + 1]] for ref in refs]
    products = [(tiles, part) for part in basis] + [(tiles, tiles)]
    products += [(basis[i], basis[j]) for i, j in PAIRS]
    rhs = iota((ROWS, BLOCK), 0)
    lane = iota((ROWS, BLOCK), 1)
    spots = jnp.zeros((ROWS, BLOCK), jnp.float32)
    for index, (left, right) in enumerate(products):
        value = per_rhs(left[0] * right[0] + left[1] * right[1])
        here = (lane == HALF_RHS * index + rhs) & (rhs < HALF_RHS)
        spots = jnp.where(here, value, spots)
    row = jnp.sum(spots, axis=0, keepdims=True)
    chunk_ref[...] = jnp.broadcast_to(row, chunk_ref.shape)
    known = columns(
        {place + ITERS + 1: value for place, value in enumerate(coeffs)}
    ) + coeff_ref[...]
    for out_ref, which in ((mine_ref, core), (theirs_ref, 1 - core)):
        for index, ref in enumerate(refs):
            for half in range(2):
                out_ref[2 * index + half] = ref[half * owners + owner - core + which]
        out_ref[2 * ITERS] = jnp.where(which == 0, tiles[0], tiles[1])
        out_ref[2 * ITERS + 1] = known


def keep_kernel(mine_ref, theirs_ref, across_ref, flipped_ref, mirror_hbm, kept_ref, known_ref,
                mirror_ref, sem):
    copy = pltpu.make_async_copy(mirror_hbm, mirror_ref, sem)
    copy.start()
    side, _, core = position()

    def both(index):
        mine, theirs = mine_ref[index], theirs_ref[index]
        return [jnp.where(core == 0, mine, theirs), jnp.where(core == 0, theirs, mine)]

    pairs = [(both(2 * index), both(2 * index + 1)) for index in range(ITERS)]
    here = both(2 * ITERS)
    there = [
        jnp.where(core == 0, across_ref[...], flipped_ref[...]),
        jnp.where(core == 0, flipped_ref[...], across_ref[...]),
    ]
    pairs.append(
        (
            [jnp.where(side == 0, h, t) for h, t in zip(here, there)],
            [jnp.where(side == 0, t, h) for h, t in zip(here, there)],
        )
    )
    known = both(2 * ITERS + 1)
    known_ref[...] = jnp.concatenate([tile[:HALF_RHS] for tile in known], axis=0)
    copy.wait()
    for block in range(BLK_DEV):
        rows = slice(block * HALF_RHS, (block + 1) * HALF_RHS)
        ports, stars = [], []
        for sym, anti in pairs:
            sym = jnp.concatenate([tile[rows] for tile in sym], axis=0)
            anti = jnp.concatenate([tile[rows] for tile in anti], axis=0)
            ports.append(0.5 * (sym + anti))
            stars.append(0.5 * (sym - anti))
        back = exact_dot(
            jnp.concatenate(stars, axis=0), mirror_onehot(mirror_ref, block), ((1,), (1,))
        )
        for index, port in enumerate(ports):
            kept_ref[index, :, block * BLOCK : (block + 1) * BLOCK] = jnp.where(
                side == 0, port, back[index * ROWS : (index + 1) * ROWS]
            )


def final_kernel(total, got_ref, kept_ref, known_ref, basis_ref, hessenberg_ref):
    inner = 0.5 / total
    sums = jnp.sum(got_ref[...].reshape(-1, ROWS, BLOCK), axis=0)
    even = iota((ROWS, BLOCK), 0) % 2 == 0
    lower = jnp.sum(jnp.where(even, sums, 0.0), axis=0, keepdims=True)
    upper = jnp.sum(jnp.where(even, 0.0, sums), axis=0, keepdims=True)
    rhs = iota((ROWS, BLOCK), 0)
    lane = iota((ROWS, BLOCK), 1)
    spots = jnp.where(rhs < HALF_RHS, lower, upper) * inner
    values = [
        jnp.sum(
            jnp.where(lane == HALF_RHS * index + rhs % HALF_RHS, spots, 0.0), axis=1, keepdims=True
        )
        for index in range(ITERS + 1 + len(PAIRS))
    ]
    coeffs = values[:ITERS]
    gram = {}
    for (i, j), value in zip(PAIRS, values[ITERS + 1 :]):
        gram[i, j] = gram[j, i] = value
    squares = values[ITERS]
    for i in range(ITERS):
        weight = -2.0 * coeffs[i]
        for j in range(ITERS):
            weight = weight + coeffs[j] * gram[i, j]
        squares = squares + coeffs[i] * weight
    norm = jnp.sqrt(jnp.maximum(squares, 0.0) + EPSILON)
    rest = kept_ref[ITERS]
    for j in range(ITERS):
        rest = rest - coeffs[j] * kept_ref[j]
    basis_ref[:ITERS] = kept_ref[:ITERS]
    basis_ref[ITERS] = rest * (1.0 / norm)
    place = 2 * (ITERS + 1)
    whole = known_ref[...] + columns(
        {place + index: value for index, value in enumerate(coeffs + [norm])}
    )
    turned = whole.T
    for k in range(ITERS):
        hessenberg_ref[k] = turned[k * (ITERS + 1) : (k + 1) * (ITERS + 1), :]


VMEM = pl.BlockSpec(memory_space=pltpu.VMEM)
SMEM = pl.BlockSpec(memory_space=pltpu.SMEM)
HBM = pl.BlockSpec(memory_space=pl.ANY)


def shaped(*shape, dtype=jnp.float32):
    return jax.ShapeDtypeStruct(shape, dtype)


def call(kernel, outs, specs, scratch=(), name=None):
    return pl.pallas_call(
        kernel,
        out_shape=outs,
        in_specs=specs,
        out_specs=[VMEM] * len(outs),
        scratch_shapes=scratch,
        compiler_params=pltpu.CompilerParams(vmem_limit_bytes=VMEM_LIMIT),
        name=name,
    )


def on_device(sources, near_blocks, block_rows, block_cols, mirror):
    devices = lax.axis_size(AXES)
    owners = devices // 2
    chips = devices // 2
    panels = sources.shape[2]
    total = 1.0 * panels * devices
    same_core = [[i for i in range(devices) if i % 2 == core] for core in range(2)]
    mirror_rows = mirror.reshape(BLK_DEV, BLOCK)
    blocks = near_blocks[0]
    vector = shaped(devices, ROWS, BLOCK)
    chunk = shaped(chips, 2, ROWS, BLOCK)
    tile = shaped(ROWS, BLOCK)

    def swapped(value, bits):
        return lax.ppermute(value, AXES, [(i, i ^ bits) for i in range(devices)])

    def exchanged(chunks):
        got = lax.all_to_all(chunks, AXES, 0, 0, axis_index_groups=same_core)
        return got.reshape(vector.shape)

    places = jnp.concatenate([block_rows, block_cols], axis=0)
    other_blocks = swapped(blocks, 1)
    other_places = swapped(places, 1)
    [chunks] = call(
        start_kernel, [vector], [HBM, HBM],
        [
            pltpu.VMEM(sources.shape[1:], jnp.float32),
            pltpu.VMEM(mirror_rows.shape, jnp.int32),
            pltpu.SemaphoreType.DMA((2,)),
        ],
        name="start",
    )(sources[0], mirror_rows)
    got = lax.all_to_all(chunks, AXES, 0, 0)
    own_blocks, pick = call(
        prepare_kernel,
        [
            shaped(*blocks.shape, dtype=blocks.dtype),
            shaped(2 * ROWS * blocks.shape[0], owners * ROWS, dtype=jnp.bfloat16),
        ],
        [HBM, SMEM, SMEM], [pltpu.SemaphoreType.DMA], name="prepare",
    )(blocks, places, other_places)
    near = (pick, own_blocks, other_blocks)
    chunks, zero = call(
        functools.partial(first_kernel, total), [chunk, vector], [VMEM] * 4, name="first"
    )(got, *near)
    got = exchanged(chunks)
    chunks, one, coeff = call(
        functools.partial(middle_kernel, total), [chunk, vector, tile], [VMEM] * 5, name="middle"
    )(got, zero, *near)
    got = exchanged(chunks)
    kept = shaped(2 * ITERS + 2, ROWS, BLOCK)
    chunks, mine, theirs = call(
        functools.partial(last_kernel, total), [shaped(devices, BLOCK), kept, kept], [VMEM] * 7,
        [pltpu.VMEM(vector.shape, jnp.float32)], name="last",
    )(got, zero, one, coeff, *near)
    got = lax.all_to_all(chunks.reshape(devices, 1, BLOCK), AXES, 0, 0)
    partner = swapped(theirs, 1)
    across = swapped(mine[2 * ITERS], devices // 2)
    flipped = swapped(theirs[2 * ITERS], devices // 2 ^ 1)
    kept, known = call(
        keep_kernel, [shaped(ITERS + 1, ROWS, panels), tile], [VMEM] * 4 + [HBM],
        [pltpu.VMEM(mirror_rows.shape, jnp.int32), pltpu.SemaphoreType.DMA], name="keep",
    )(mine, partner, across, flipped, mirror_rows)
    basis, hessenberg = call(
        functools.partial(final_kernel, total),
        [shaped(ITERS + 1, ROWS, panels), shaped(ITERS, ITERS + 1, ROWS)], [VMEM] * 3,
        name="final",
    )(got.reshape(devices, BLOCK), kept, known)
    return basis[:, None], hessenberg.transpose(2, 1, 0)


def solution(mesh):
    placed = (
        P("side", None, ("grp", "dev")),
        P("side", ("grp", "dev"), None, None),
        P("side", ("grp", "dev")),
        P("side", ("grp", "dev")),
        P(("grp", "dev")),
    )
    return jax.shard_map(
        on_device,
        mesh=mesh,
        in_specs=placed,
        out_specs=(P(None, "side", None, ("grp", "dev")), P()),
        check_vma=False,
    )
```

```python
import functools

import jax
import jax.numpy as jnp
from jax import lax
from jax.experimental import pallas as pl
from jax.experimental.pallas import tpu as pltpu
from jax.sharding import PartitionSpec as P

BLOCK = 128
BLK_DEV = 2
ITERS = 3
ROWS = 8
HALF_RHS = 4
EPSILON = 1e-06
AXES = ("side", "grp", "dev")
VMEM_LIMIT = 48 * 2**20
LENGTH_LANE = ITERS * (ITERS + 1)


def position():
    side = lax.axis_index("side")
    dev = lax.axis_index("dev")
    owner = lax.axis_index("grp") * lax.axis_size("dev") + dev
    return side, owner, lax.rem(dev, 2)


def iota(shape, axis):
    return lax.broadcasted_iota(jnp.int32, shape, axis)


def per_rhs(tile):
    column = jnp.sum(tile, axis=1, keepdims=True)
    return column + jnp.concatenate([column[HALF_RHS:], column[:HALF_RHS]], axis=0)


def dot(left, right):
    return per_rhs(jnp.sum(left * right, axis=0))


def columns(values):
    lane = iota((ROWS, BLOCK), 1)
    tile = jnp.zeros((ROWS, BLOCK), jnp.float32)
    for index, value in values.items():
        tile = jnp.where(lane == index, value, tile)
    return tile


def mirror_onehot(mirror_ref, block):
    return (iota((BLOCK, BLOCK), 0) == mirror_ref[block : block + 1, :]).astype(jnp.float32)


def exact_dot(left, right, dims):
    return lax.dot_general(
        left, right, (dims, ((), ())),
        precision=lax.Precision.HIGHEST, preferred_element_type=jnp.float32,
    )


def start_kernel(sources_hbm, mirror_hbm, chunk_ref, sources_ref, mirror_ref, sems):
    copies = [
        pltpu.make_async_copy(sources_hbm, sources_ref, sems.at[0]),
        pltpu.make_async_copy(mirror_hbm, mirror_ref, sems.at[1]),
    ]
    for copy in copies:
        copy.start()
    for copy in copies:
        copy.wait()
    side, _, _ = position()
    pieces = []
    for block in range(BLK_DEV):
        part = sources_ref[:, block * BLOCK : (block + 1) * BLOCK]
        moved = exact_dot(part, mirror_onehot(mirror_ref, block), ((1,), (0,)))
        pieces.append(jnp.where(side == 0, part, moved))
    tiles = [
        jnp.concatenate([piece[HALF_RHS * c : HALF_RHS * (c + 1)] for piece in pieces], axis=0)
        for c in range(2)
    ]
    chips = chunk_ref.shape[0] // 2

    def store(chip, carry):
        chunk_ref[2 * chip] = tiles[0]
        chunk_ref[2 * chip + 1] = tiles[1]
        return carry

    lax.fori_loop(0, chips, store, 0, unroll=chips <= 32)


def prepare_kernel(blocks_hbm, own_rows, own_cols, other_rows, other_cols, blocks_ref, pick_ref,
                   sem):
    copy = pltpu.make_async_copy(blocks_hbm, blocks_ref, sem)
    copy.start()
    width = pick_ref.shape[1]
    half_of_row = iota((ROWS, width), 0) // HALF_RHS
    rhs_of_row = iota((ROWS, width), 0) % HALF_RHS
    lane = iota((ROWS, width), 1)
    for entry in range(blocks_ref.shape[0]):
        picks = []
        for rows, cols in ((own_rows, own_cols), (other_rows, other_cols)):
            place = jnp.where(
                half_of_row == rows[0, entry], HALF_RHS * cols[0, entry] + rhs_of_row, -1
            )
            picks.append((lane == place).astype(jnp.float32))
        first = 2 * ROWS * entry
        pick_ref[first : first + 2 * ROWS, :] = jnp.concatenate(picks, axis=0).astype(jnp.bfloat16)
    copy.wait()


def image(vector_ref, pick_ref, own_ref, other_ref):
    side, owner, core = position()
    owners = vector_ref.shape[0] // 2
    half = vector_ref[pl.ds(side * owners, owners)]
    rounded = half.reshape(owners * ROWS, BLOCK).astype(jnp.bfloat16)
    picked = lax.dot_general(
        pick_ref[...], rounded, (((1,), (0,)), ((), ())), preferred_element_type=jnp.float32
    ).astype(jnp.bfloat16)
    sums = [jnp.zeros((2 * ROWS, 2 * BLOCK), jnp.float32) for _ in range(2)]
    for entry in range(0, own_ref.shape[0], 2):
        first = 2 * ROWS * entry
        left = jnp.concatenate(
            [picked[first : first + 2 * ROWS], picked[first + 2 * ROWS : first + 4 * ROWS]], axis=1
        )
        right = jnp.concatenate(
            [jnp.concatenate([ref[entry], ref[entry + 1]], axis=1) for ref in (own_ref, other_ref)],
            axis=0,
        )
        sums[entry // 2 % 2] += lax.dot_general(
            left, right, (((1,), (1,)), ((), ())), preferred_element_type=jnp.float32
        )
    total = sums[0] + sums[1]
    own = total[:ROWS, :BLOCK]
    other = total[ROWS:, BLOCK:]
    base = side * owners + owner - core
    low = jnp.where(core == 0, own, other) + 0.5 * vector_ref[base]
    high = jnp.where(core == 0, other, own) + 0.5 * vector_ref[base + 1]
    return low, high


def spread(chunk_ref, low, high):
    chips = chunk_ref.shape[0]

    def store(chip, carry):
        chunk_ref[chip, 0] = low
        chunk_ref[chip, 1] = high
        return carry

    lax.fori_loop(0, chips, store, 0, unroll=chips <= 32)


def first_kernel(total, got_ref, pick_ref, own_ref, other_ref, chunk_ref, basis_ref, coeff_ref):
    owners = got_ref.shape[0] // 2
    port = got_ref[:owners]
    star = got_ref[owners:]
    squares = per_rhs(jnp.sum(port * port + star * star, axis=0))
    length = jnp.sqrt(squares * (1.0 / total) + EPSILON)
    scale = 1.0 / length
    coeff_ref[...] = columns({LENGTH_LANE: length})
    basis_ref[:owners] = (port + star) * scale
    basis_ref[owners:] = (port - star) * scale
    spread(chunk_ref, *image(basis_ref, pick_ref, own_ref, other_ref))


def orthogonalized(total, shift, got_ref, basis_refs):
    inner = 0.5 / total
    chips = got_ref.shape[0]
    got = jnp.concatenate([got_ref[chips - shift :], got_ref[: chips - shift]], axis=0)
    got = got.reshape(basis_refs[0].shape)
    coeffs = [dot(got, ref[...]) * inner for ref in basis_refs]
    rest = got
    for coeff, ref in zip(coeffs, basis_refs):
        rest = rest - coeff * ref[...]
    norm = jnp.sqrt(dot(rest, rest) * inner + EPSILON)
    return coeffs + [norm], rest * (1.0 / norm)


def middle_kernel(total, shift, got_ref, basis_ref, known_ref, pick_ref, own_ref, other_ref,
                  chunk_ref, next_ref, coeff_ref):
    coeffs, next_ref[...] = orthogonalized(total, shift, got_ref, [basis_ref])
    coeff_ref[...] = columns(dict(enumerate(coeffs))) + known_ref[...]
    spread(chunk_ref, *image(next_ref, pick_ref, own_ref, other_ref))


def last_kernel(total, shift, got_ref, zero_ref, one_ref, known_ref, pick_ref, own_ref, other_ref,
                chunk_ref, two_ref, coeff_ref, same_ref, flip_ref, theirs_ref):
    side, owner, core = position()
    owners = two_ref.shape[0] // 2
    refs = [zero_ref, one_ref, two_ref]
    coeffs, two_ref[...] = orthogonalized(total, shift, got_ref, refs[:2])
    tiles = image(two_ref, pick_ref, own_ref, other_ref)
    base = side * owners + owner - core
    rhs = iota((ROWS, BLOCK), 0)
    lane = iota((ROWS, BLOCK), 1)
    spots = jnp.zeros((ROWS, BLOCK), jnp.float32)
    for index in range(ITERS + 1):
        if index < ITERS:
            product = tiles[0] * refs[index][base] + tiles[1] * refs[index][base + 1]
        else:
            product = tiles[0] * tiles[0] + tiles[1] * tiles[1]
        here = (lane == HALF_RHS * index + rhs) & (rhs < HALF_RHS)
        spots = jnp.where(here, per_rhs(product), spots)
    row = jnp.sum(spots, axis=0, keepdims=True)
    chunk_ref[...] = jnp.broadcast_to(row, chunk_ref.shape)
    coeffs = columns({place + ITERS + 1: value for place, value in enumerate(coeffs)})
    coeff_ref[...] = coeffs + known_ref[...]
    same_ref[...] = jnp.where(core == 0, tiles[0], tiles[1])
    flip_ref[...] = jnp.where(core == 0, tiles[1], tiles[0])
    for index, ref in enumerate(refs):
        for half in range(2):
            theirs_ref[2 * index + half] = ref[half * owners + owner + 1 - 2 * core]
    theirs_ref[2 * ITERS] = flip_ref[...]
    theirs_ref[2 * ITERS + 1] = coeff_ref[...]


def keep_kernel(zero_ref, one_ref, two_ref, coeff_ref, same_ref, theirs_ref, across_ref,
                flipped_ref, mirror_hbm, kept_ref, known_ref, gram_ref, mirror_ref, sem):
    copy = pltpu.make_async_copy(mirror_hbm, mirror_ref, sem)
    copy.start()
    side, owner, core = position()
    owners = zero_ref.shape[0] // 2

    def by_core(mine, theirs):
        return [jnp.where(core == 0, mine, theirs), jnp.where(core == 0, theirs, mine)]

    pairs = []
    for index, ref in enumerate((zero_ref, one_ref, two_ref)):
        pairs.append(
            [
                by_core(ref[half * owners + owner], theirs_ref[2 * index + half])
                for half in range(2)
            ]
        )
    here = by_core(same_ref[...], theirs_ref[2 * ITERS])
    there = by_core(across_ref[...], flipped_ref[...])
    pairs.append(
        [
            [jnp.where(side == 0, h, t) for h, t in zip(here, there)],
            [jnp.where(side == 0, t, h) for h, t in zip(here, there)],
        ]
    )
    known = by_core(coeff_ref[...], theirs_ref[2 * ITERS + 1])
    known = jnp.concatenate([tile[:HALF_RHS] for tile in known], axis=0)
    known_ref[...] = jnp.where(iota((ROWS, BLOCK), 1) < LENGTH_LANE, known, 0.0)

    def entry(j, k):
        place = k * (ITERS + 1) + j
        return known[:, place : place + 1]

    norms = [known[:, LENGTH_LANE : LENGTH_LANE + 1], entry(1, 0), entry(2, 1)]
    short = [EPSILON / (norm * norm) for norm in norms]
    zero_one = entry(0, 0) * short[0] / norms[1]
    zero_two = (entry(0, 1) * short[0] - entry(1, 1) * zero_one) / norms[2]
    one_two = (entry(1, 1) * short[1] - entry(0, 1) * zero_one) / norms[2]
    gram_ref[...] = columns(dict(enumerate(short + [zero_one, zero_two, one_two])))
    copy.wait()
    for block in range(BLK_DEV):
        rows = slice(block * HALF_RHS, (block + 1) * HALF_RHS)
        ports, stars = [], []
        for sym, anti in pairs:
            sym = jnp.concatenate([tile[rows] for tile in sym], axis=0)
            anti = jnp.concatenate([tile[rows] for tile in anti], axis=0)
            ports.append(0.5 * (sym + anti))
            stars.append(0.5 * (sym - anti))
        back = exact_dot(
            jnp.concatenate(stars, axis=0), mirror_onehot(mirror_ref, block), ((1,), (1,))
        )
        for index, port in enumerate(ports):
            kept_ref[index, :, block * BLOCK : (block + 1) * BLOCK] = jnp.where(
                side == 0, port, back[index * ROWS : (index + 1) * ROWS]
            )


def final_kernel(total, got_ref, kept_ref, known_ref, gram_ref, basis_ref, hessenberg_ref):
    inner = 0.5 / total
    sums = jnp.sum(got_ref[...].reshape(-1, ROWS, BLOCK), axis=0)
    even = iota((ROWS, BLOCK), 0) % 2 == 0
    lower = jnp.sum(jnp.where(even, sums, 0.0), axis=0, keepdims=True)
    upper = jnp.sum(jnp.where(even, 0.0, sums), axis=0, keepdims=True)
    rhs = iota((ROWS, BLOCK), 0)
    lane = iota((ROWS, BLOCK), 1)
    spots = jnp.where(rhs < HALF_RHS, lower, upper) * inner
    values = [
        jnp.sum(
            jnp.where(lane == HALF_RHS * index + rhs % HALF_RHS, spots, 0.0), axis=1, keepdims=True
        )
        for index in range(ITERS + 1)
    ]
    coeffs = values[:ITERS]
    gram = gram_ref[...]
    squares = values[ITERS]
    for j in range(ITERS):
        squares = squares - coeffs[j] * coeffs[j] * (1.0 + gram[:, j : j + 1])
    for place, (i, j) in enumerate(((0, 1), (0, 2), (1, 2))):
        squares = squares + 2.0 * coeffs[i] * coeffs[j] * gram[:, ITERS + place : ITERS + place + 1]
    norm = jnp.sqrt(jnp.maximum(squares, 0.0) + EPSILON)
    rest = kept_ref[ITERS]
    for j in range(ITERS):
        rest = rest - coeffs[j] * kept_ref[j]
    basis_ref[:ITERS] = kept_ref[:ITERS]
    basis_ref[ITERS] = rest * (1.0 / norm)
    place = 2 * (ITERS + 1)
    whole = known_ref[...] + columns(
        {place + index: value for index, value in enumerate(coeffs + [norm])}
    )
    turned = whole.T
    for k in range(ITERS):
        hessenberg_ref[k] = turned[k * (ITERS + 1) : (k + 1) * (ITERS + 1), :]


VMEM = pl.BlockSpec(memory_space=pltpu.VMEM)
SMEM = pl.BlockSpec(memory_space=pltpu.SMEM)
HBM = pl.BlockSpec(memory_space=pltpu.HBM)


def shaped(*shape, dtype=jnp.float32):
    return jax.ShapeDtypeStruct(shape, dtype)


def call(kernel, outs, specs, scratch=(), name=None):
    return pl.pallas_call(
        kernel,
        out_shape=outs,
        in_specs=specs,
        out_specs=[VMEM] * len(outs),
        scratch_shapes=scratch,
        compiler_params=pltpu.CompilerParams(vmem_limit_bytes=VMEM_LIMIT),
        name=name,
    )


def on_device(sources, near_blocks, block_rows, block_cols, mirror):
    devices = lax.axis_size(AXES)
    owners = devices // 2
    chips = devices // 2
    panels = sources.shape[2]
    total = 1.0 * panels * devices
    dev = lax.axis_size("dev")
    shift = (dev + dev // 2) // 2 % chips
    same_core = [
        [(2 * (chip + shift) + core) % devices for chip in range(chips)] for core in range(2)
    ]
    mirror_rows = mirror.reshape(BLK_DEV, BLOCK)
    blocks = near_blocks[0]
    vector = shaped(devices, ROWS, BLOCK)
    chunk = shaped(chips, 2, ROWS, BLOCK)
    tile = shaped(ROWS, BLOCK)

    def swapped(value, bits):
        return lax.ppermute(value, AXES, [(i, i ^ bits) for i in range(devices)])

    def exchanged(chunks):
        return lax.all_to_all(chunks, AXES, 0, 0, axis_index_groups=same_core)

    [chunks] = call(
        start_kernel, [vector], [HBM, HBM],
        [
            pltpu.VMEM(sources.shape[1:], jnp.float32),
            pltpu.VMEM(mirror_rows.shape, jnp.int32),
            pltpu.SemaphoreType.DMA((2,)),
        ],
        name="start",
    )(sources[0], mirror_rows)
    chunks, blocks, block_rows, block_cols = lax.optimization_barrier(
        (chunks, blocks, block_rows, block_cols)
    )
    got = lax.all_to_all(chunks, AXES, 0, 0)
    other_blocks = swapped(blocks, 1)
    own_blocks, pick = call(
        prepare_kernel,
        [
            shaped(*blocks.shape, dtype=blocks.dtype),
            shaped(2 * ROWS * blocks.shape[0], owners * ROWS, dtype=jnp.bfloat16),
        ],
        [HBM] + [SMEM] * 4, [pltpu.SemaphoreType.DMA], name="prepare",
    )(blocks, block_rows, block_cols, swapped(block_rows, 1), swapped(block_cols, 1))
    near = (pick, own_blocks, other_blocks)
    chunks, zero, coeff = call(
        functools.partial(first_kernel, total), [chunk, vector, tile], [VMEM] * 4, name="first"
    )(got, *near)
    got = exchanged(chunks)
    chunks, one, coeff = call(
        functools.partial(middle_kernel, total, shift), [chunk, vector, tile], [VMEM] * 6,
        name="middle",
    )(got, zero, coeff, *near)
    got = exchanged(chunks)
    theirs = shaped(2 * ITERS + 2, ROWS, BLOCK)
    chunks, two, coeff, same, flip, theirs = call(
        functools.partial(last_kernel, total, shift),
        [shaped(devices, BLOCK), vector, tile, tile, tile, theirs], [VMEM] * 7, name="last",
    )(got, zero, one, coeff, *near)
    got = lax.all_to_all(chunks.reshape(devices, 1, BLOCK), AXES, 0, 0)
    kept, known, gram = call(
        keep_kernel, [shaped(ITERS + 1, ROWS, panels), tile, tile], [VMEM] * 8 + [HBM],
        [pltpu.VMEM(mirror_rows.shape, jnp.int32), pltpu.SemaphoreType.DMA], name="keep",
    )(
        zero, one, two, coeff, same, swapped(theirs, 1), swapped(same, devices // 2),
        swapped(flip, devices // 2 ^ 1), mirror_rows,
    )
    basis, hessenberg = call(
        functools.partial(final_kernel, total),
        [shaped(ITERS + 1, ROWS, panels), shaped(ITERS, ITERS + 1, ROWS)], [VMEM] * 4,
        name="final",
    )(got.reshape(devices, BLOCK), kept, known, gram)
    return basis[:, None], hessenberg.transpose(2, 1, 0)


def solution(mesh):
    placed = (
        P("side", None, ("grp", "dev")),
        P("side", ("grp", "dev"), None, None),
        P("side", ("grp", "dev")),
        P("side", ("grp", "dev")),
        P(("grp", "dev")),
    )
    return jax.shard_map(
        on_device,
        mesh=mesh,
        in_specs=placed,
        out_specs=(P(None, "side", None, ("grp", "dev")), P()),
        check_vma=False,
    )
```

```python
import functools

import jax
import jax.numpy as jnp
from jax import lax
from jax.experimental import pallas as pl
from jax.experimental.pallas import tpu as pltpu
from jax.sharding import PartitionSpec as P

BLOCK = 128
BLK_DEV = 2
ITERS = 3
ROWS = 8
HALF_RHS = 4
EPSILON = 1e-06
AXES = ("side", "grp", "dev")
VMEM_LIMIT = 48 * 2**20
LENGTH_LANE = ITERS * (ITERS + 1)


def position():
    side = lax.axis_index("side")
    dev = lax.axis_index("dev")
    owner = lax.axis_index("grp") * lax.axis_size("dev") + dev
    return side, owner, lax.rem(dev, 2)


def iota(shape, axis):
    return lax.broadcasted_iota(jnp.int32, shape, axis)


def per_rhs(tile):
    column = jnp.sum(tile, axis=1, keepdims=True)
    return column + jnp.concatenate([column[HALF_RHS:], column[:HALF_RHS]], axis=0)


def dot(left, right):
    return per_rhs(jnp.sum(left * right, axis=0))


def columns(values):
    lane = iota((ROWS, BLOCK), 1)
    tile = jnp.zeros((ROWS, BLOCK), jnp.float32)
    for index, value in values.items():
        tile = jnp.where(lane == index, value, tile)
    return tile


def mirror_onehot(mirror_ref, block):
    return (iota((BLOCK, BLOCK), 0) == mirror_ref[block : block + 1, :]).astype(jnp.float32)


def exact_dot(left, right, dims):
    return lax.dot_general(
        left, right, (dims, ((), ())),
        precision=lax.Precision.HIGHEST, preferred_element_type=jnp.float32,
    )


def start_kernel(sources_hbm, mirror_hbm, chunk_ref, sources_ref, mirror_ref, sems):
    copies = [
        pltpu.make_async_copy(sources_hbm, sources_ref, sems.at[0]),
        pltpu.make_async_copy(mirror_hbm, mirror_ref, sems.at[1]),
    ]
    for copy in copies:
        copy.start()
    for copy in copies:
        copy.wait()
    side, _, _ = position()
    pieces = []
    for block in range(BLK_DEV):
        part = sources_ref[:, block * BLOCK : (block + 1) * BLOCK]
        moved = exact_dot(part, mirror_onehot(mirror_ref, block), ((1,), (0,)))
        pieces.append(jnp.where(side == 0, part, moved))
    tiles = [
        jnp.concatenate([piece[HALF_RHS * c : HALF_RHS * (c + 1)] for piece in pieces], axis=0)
        for c in range(2)
    ]
    chips = chunk_ref.shape[0] // 2

    def store(chip, carry):
        chunk_ref[2 * chip] = tiles[0]
        chunk_ref[2 * chip + 1] = tiles[1]
        return carry

    lax.fori_loop(0, chips, store, 0, unroll=chips <= 32)


def prepare_kernel(blocks_hbm, own_rows, own_cols, other_rows, other_cols, blocks_ref, pick_ref,
                   sem):
    copy = pltpu.make_async_copy(blocks_hbm, blocks_ref, sem)
    copy.start()
    width = pick_ref.shape[1]
    half_of_row = iota((ROWS, width), 0) // HALF_RHS
    rhs_of_row = iota((ROWS, width), 0) % HALF_RHS
    lane = iota((ROWS, width), 1)
    for entry in range(blocks_ref.shape[0]):
        picks = []
        for rows, cols in ((own_rows, own_cols), (other_rows, other_cols)):
            place = jnp.where(
                half_of_row == rows[0, entry], HALF_RHS * cols[0, entry] + rhs_of_row, -1
            )
            picks.append((lane == place).astype(jnp.float32))
        first = 2 * ROWS * entry
        pick_ref[first : first + 2 * ROWS, :] = jnp.concatenate(picks, axis=0).astype(jnp.bfloat16)
    copy.wait()


def image(vector_ref, pick_ref, own_ref, other_ref):
    side, owner, core = position()
    owners = vector_ref.shape[0] // 2
    half = vector_ref[pl.ds(side * owners, owners)]
    rounded = half.reshape(owners * ROWS, BLOCK).astype(jnp.bfloat16)
    picked = lax.dot_general(
        pick_ref[...], rounded, (((1,), (0,)), ((), ())), preferred_element_type=jnp.float32
    ).astype(jnp.bfloat16)
    sums = [jnp.zeros((2 * ROWS, 2 * BLOCK), jnp.float32) for _ in range(2)]
    for entry in range(0, own_ref.shape[0], 2):
        first = 2 * ROWS * entry
        left = jnp.concatenate(
            [picked[first : first + 2 * ROWS], picked[first + 2 * ROWS : first + 4 * ROWS]], axis=1
        )
        right = jnp.concatenate(
            [jnp.concatenate([ref[entry], ref[entry + 1]], axis=1) for ref in (own_ref, other_ref)],
            axis=0,
        )
        sums[entry // 2 % 2] += lax.dot_general(
            left, right, (((1,), (1,)), ((), ())), preferred_element_type=jnp.float32
        )
    total = sums[0] + sums[1]
    own = total[:ROWS, :BLOCK]
    other = total[ROWS:, BLOCK:]
    base = side * owners + owner - core
    low = jnp.where(core == 0, own, other) + 0.5 * vector_ref[base]
    high = jnp.where(core == 0, other, own) + 0.5 * vector_ref[base + 1]
    return low, high


def spread(chunk_ref, low, high):
    chips = chunk_ref.shape[0]

    def store(chip, carry):
        chunk_ref[chip, 0] = low
        chunk_ref[chip, 1] = high
        return carry

    lax.fori_loop(0, chips, store, 0, unroll=chips <= 32)


def first_kernel(total, got_ref, pick_ref, own_ref, other_ref, chunk_ref, basis_ref, coeff_ref):
    owners = got_ref.shape[0] // 2
    port = got_ref[:owners]
    star = got_ref[owners:]
    squares = per_rhs(jnp.sum(port * port + star * star, axis=0))
    squares = squares * (1.0 / total) + EPSILON
    scale = lax.rsqrt(squares)
    coeff_ref[...] = columns({LENGTH_LANE: jnp.sqrt(squares)})
    basis_ref[:owners] = (port + star) * scale
    basis_ref[owners:] = (port - star) * scale
    spread(chunk_ref, *image(basis_ref, pick_ref, own_ref, other_ref))


def orthogonalized(total, shift, got_ref, basis_refs):
    inner = 0.5 / total
    chips = got_ref.shape[0]
    got = jnp.concatenate([got_ref[chips - shift :], got_ref[: chips - shift]], axis=0)
    got = got.reshape(basis_refs[0].shape)
    coeffs = [dot(got, ref[...]) * inner for ref in basis_refs]
    rest = got
    for coeff, ref in zip(coeffs, basis_refs):
        rest = rest - coeff * ref[...]
    squares = dot(rest, rest) * inner + EPSILON
    return coeffs + [jnp.sqrt(squares)], rest * lax.rsqrt(squares)


def middle_kernel(total, shift, got_ref, basis_ref, known_ref, pick_ref, own_ref, other_ref,
                  chunk_ref, next_ref, coeff_ref):
    coeffs, next_ref[...] = orthogonalized(total, shift, got_ref, [basis_ref])
    coeff_ref[...] = columns(dict(enumerate(coeffs))) + known_ref[...]
    spread(chunk_ref, *image(next_ref, pick_ref, own_ref, other_ref))


def last_kernel(total, shift, got_ref, zero_ref, one_ref, known_ref, pick_ref, own_ref, other_ref,
                chunk_ref, two_ref, coeff_ref, same_ref, flip_ref):
    side, owner, core = position()
    owners = two_ref.shape[0] // 2
    refs = [zero_ref, one_ref, two_ref]
    coeffs, two_ref[...] = orthogonalized(total, shift, got_ref, refs[:2])
    tiles = image(two_ref, pick_ref, own_ref, other_ref)
    base = side * owners + owner - core
    rhs = iota((ROWS, BLOCK), 0)
    lane = iota((ROWS, BLOCK), 1)
    spots = jnp.zeros((ROWS, BLOCK), jnp.float32)
    for index in range(ITERS + 1):
        if index < ITERS:
            product = tiles[0] * refs[index][base] + tiles[1] * refs[index][base + 1]
        else:
            product = tiles[0] * tiles[0] + tiles[1] * tiles[1]
        here = (lane == HALF_RHS * index + rhs) & (rhs < HALF_RHS)
        spots = jnp.where(here, per_rhs(product), spots)
    row = jnp.sum(spots, axis=0, keepdims=True)
    chunk_ref[...] = jnp.broadcast_to(row, chunk_ref.shape)
    coeffs = columns({place + ITERS + 1: value for place, value in enumerate(coeffs)})
    coeff_ref[...] = coeffs + known_ref[...]
    same_ref[...] = jnp.where(core == 0, tiles[0], tiles[1])
    flip_ref[...] = jnp.where(core == 0, tiles[1], tiles[0])


def pack_kernel(zero_ref, one_ref, two_ref, coeff_ref, flip_ref, theirs_ref):
    _, owner, core = position()
    owners = zero_ref.shape[0] // 2
    for index, ref in enumerate((zero_ref, one_ref, two_ref)):
        for half in range(2):
            theirs_ref[2 * index + half] = ref[half * owners + owner + 1 - 2 * core]
    theirs_ref[2 * ITERS] = flip_ref[...]
    theirs_ref[2 * ITERS + 1] = coeff_ref[...]


def keep_kernel(zero_ref, one_ref, two_ref, coeff_ref, same_ref, theirs_ref, across_ref,
                flipped_ref, mirror_hbm, kept_ref, known_ref, gram_ref, mirror_ref, sem):
    copy = pltpu.make_async_copy(mirror_hbm, mirror_ref, sem)
    copy.start()
    side, owner, core = position()
    owners = zero_ref.shape[0] // 2

    def by_core(mine, theirs):
        return [jnp.where(core == 0, mine, theirs), jnp.where(core == 0, theirs, mine)]

    pairs = []
    for index, ref in enumerate((zero_ref, one_ref, two_ref)):
        pairs.append(
            [
                by_core(ref[half * owners + owner], theirs_ref[2 * index + half])
                for half in range(2)
            ]
        )
    here = by_core(same_ref[...], theirs_ref[2 * ITERS])
    there = by_core(across_ref[...], flipped_ref[...])
    pairs.append(
        [
            [jnp.where(side == 0, h, t) for h, t in zip(here, there)],
            [jnp.where(side == 0, t, h) for h, t in zip(here, there)],
        ]
    )
    known = by_core(coeff_ref[...], theirs_ref[2 * ITERS + 1])
    known = jnp.concatenate([tile[:HALF_RHS] for tile in known], axis=0)
    known_ref[...] = jnp.where(iota((ROWS, BLOCK), 1) < LENGTH_LANE, known, 0.0)

    def entry(j, k):
        place = k * (ITERS + 1) + j
        return known[:, place : place + 1]

    norms = [known[:, LENGTH_LANE : LENGTH_LANE + 1], entry(1, 0), entry(2, 1)]
    short = [EPSILON / (norm * norm) for norm in norms]
    zero_one = entry(0, 0) * short[0] / norms[1]
    zero_two = (entry(0, 1) * short[0] - entry(1, 1) * zero_one) / norms[2]
    one_two = (entry(1, 1) * short[1] - entry(0, 1) * zero_one) / norms[2]
    gram_ref[...] = columns(dict(enumerate(short + [zero_one, zero_two, one_two])))
    copy.wait()
    for block in range(BLK_DEV):
        rows = slice(block * HALF_RHS, (block + 1) * HALF_RHS)
        ports, stars = [], []
        for sym, anti in pairs:
            sym = jnp.concatenate([tile[rows] for tile in sym], axis=0)
            anti = jnp.concatenate([tile[rows] for tile in anti], axis=0)
            ports.append(0.5 * (sym + anti))
            stars.append(0.5 * (sym - anti))
        back = exact_dot(
            jnp.concatenate(stars, axis=0), mirror_onehot(mirror_ref, block), ((1,), (1,))
        )
        for index, port in enumerate(ports):
            kept_ref[index, :, block * BLOCK : (block + 1) * BLOCK] = jnp.where(
                side == 0, port, back[index * ROWS : (index + 1) * ROWS]
            )


def final_kernel(total, got_ref, kept_ref, known_ref, gram_ref, basis_ref, hessenberg_ref):
    inner = 0.5 / total
    sums = jnp.sum(got_ref[...].reshape(-1, ROWS, BLOCK), axis=0)
    even = iota((ROWS, BLOCK), 0) % 2 == 0
    lower = jnp.sum(jnp.where(even, sums, 0.0), axis=0, keepdims=True)
    upper = jnp.sum(jnp.where(even, 0.0, sums), axis=0, keepdims=True)
    rhs = iota((ROWS, BLOCK), 0)
    lane = iota((ROWS, BLOCK), 1)
    spots = jnp.where(rhs < HALF_RHS, lower, upper) * inner
    values = [
        jnp.sum(
            jnp.where(lane == HALF_RHS * index + rhs % HALF_RHS, spots, 0.0), axis=1, keepdims=True
        )
        for index in range(ITERS + 1)
    ]
    coeffs = values[:ITERS]
    gram = gram_ref[...]
    squares = values[ITERS]
    for j in range(ITERS):
        squares = squares - coeffs[j] * coeffs[j] * (1.0 + gram[:, j : j + 1])
    for place, (i, j) in enumerate(((0, 1), (0, 2), (1, 2))):
        squares = squares + 2.0 * coeffs[i] * coeffs[j] * gram[:, ITERS + place : ITERS + place + 1]
    squares = jnp.maximum(squares, 0.0) + EPSILON
    norm = jnp.sqrt(squares)
    rest = kept_ref[ITERS]
    for j in range(ITERS):
        rest = rest - coeffs[j] * kept_ref[j]
    basis_ref[:ITERS] = kept_ref[:ITERS]
    basis_ref[ITERS] = rest * lax.rsqrt(squares)
    place = 2 * (ITERS + 1)
    whole = known_ref[...] + columns(
        {place + index: value for index, value in enumerate(coeffs + [norm])}
    )
    turned = whole.T
    for k in range(ITERS):
        hessenberg_ref[k] = turned[k * (ITERS + 1) : (k + 1) * (ITERS + 1), :]


VMEM = pl.BlockSpec(memory_space=pltpu.VMEM)
SMEM = pl.BlockSpec(memory_space=pltpu.SMEM)
HBM = pl.BlockSpec(memory_space=pltpu.HBM)


def shaped(*shape, dtype=jnp.float32):
    return jax.ShapeDtypeStruct(shape, dtype)


def in_hbm(value):
    return pltpu.with_memory_space_constraint(value, pltpu.HBM)


def call(kernel, outs, specs, scratch=(), name=None):
    return pl.pallas_call(
        kernel,
        out_shape=outs,
        in_specs=specs,
        out_specs=[VMEM] * len(outs),
        scratch_shapes=scratch,
        compiler_params=pltpu.CompilerParams(vmem_limit_bytes=VMEM_LIMIT),
        name=name,
    )


def on_device(sources, near_blocks, block_rows, block_cols, mirror):
    devices = lax.axis_size(AXES)
    owners = devices // 2
    chips = devices // 2
    panels = sources.shape[2]
    total = 1.0 * panels * devices
    dev = lax.axis_size("dev")
    shift = (dev + dev // 2) // 2 % chips
    same_core = [
        [(2 * (chip + shift) + core) % devices for chip in range(chips)] for core in range(2)
    ]
    mirror_rows = mirror.reshape(BLK_DEV, BLOCK)
    blocks = near_blocks[0]
    vector = shaped(devices, ROWS, BLOCK)
    chunk = shaped(chips, 2, ROWS, BLOCK)
    tile = shaped(ROWS, BLOCK)

    def swapped(value, bits):
        return lax.ppermute(value, AXES, [(i, i ^ bits) for i in range(devices)])

    def exchanged(chunks):
        return lax.all_to_all(chunks, AXES, 0, 0, axis_index_groups=same_core)

    [chunks] = call(
        start_kernel, [pltpu.VMEM(vector.shape, jnp.float32)], [HBM, HBM],
        [
            pltpu.VMEM(sources.shape[1:], jnp.float32),
            pltpu.VMEM(mirror_rows.shape, jnp.int32),
            pltpu.SemaphoreType.DMA((2,)),
        ],
        name="start",
    )(in_hbm(sources[0]), in_hbm(mirror_rows))
    chunks, blocks, block_rows, block_cols = lax.optimization_barrier(
        (chunks, blocks, block_rows, block_cols)
    )
    got = lax.all_to_all(chunks, AXES, 0, 0)
    other_blocks = swapped(blocks, 1)
    own_blocks, pick = call(
        prepare_kernel,
        [
            shaped(*blocks.shape, dtype=blocks.dtype),
            shaped(2 * ROWS * blocks.shape[0], owners * ROWS, dtype=jnp.bfloat16),
        ],
        [HBM] + [SMEM] * 4, [pltpu.SemaphoreType.DMA], name="prepare",
    )(in_hbm(blocks), block_rows, block_cols, swapped(block_rows, 1), swapped(block_cols, 1))
    near = (pick, own_blocks, other_blocks)
    chunks, zero, coeff = call(
        functools.partial(first_kernel, total), [chunk, vector, tile], [VMEM] * 4, name="first"
    )(got, *near)
    got = exchanged(chunks)
    chunks, one, coeff = call(
        functools.partial(middle_kernel, total, shift), [chunk, vector, tile], [VMEM] * 6,
        name="middle",
    )(got, zero, coeff, *near)
    got = exchanged(chunks)
    chunks, two, coeff, same, flip = call(
        functools.partial(last_kernel, total, shift),
        [pltpu.VMEM((devices, BLOCK), jnp.float32), vector, tile, tile, tile], [VMEM] * 7,
        name="last",
    )(got, zero, one, coeff, *near)
    got = lax.all_to_all(chunks.reshape(devices, 1, BLOCK), AXES, 0, 0)
    [theirs] = call(
        pack_kernel, [shaped(2 * ITERS + 2, ROWS, BLOCK)], [VMEM] * 5, name="pack"
    )(zero, one, two, coeff, flip)
    kept, known, gram = call(
        keep_kernel, [shaped(ITERS + 1, ROWS, panels), tile, tile], [VMEM] * 8 + [HBM],
        [pltpu.VMEM(mirror_rows.shape, jnp.int32), pltpu.SemaphoreType.DMA], name="keep",
    )(
        zero, one, two, coeff, same, swapped(theirs, 1), swapped(same, devices // 2),
        swapped(flip, devices // 2 ^ 1), in_hbm(mirror_rows),
    )
    basis, hessenberg = call(
        functools.partial(final_kernel, total),
        [shaped(ITERS + 1, ROWS, panels), shaped(ITERS, ITERS + 1, ROWS)], [VMEM] * 4,
        name="final",
    )(got.reshape(devices, BLOCK), kept, known, gram)
    return basis[:, None], hessenberg.transpose(2, 1, 0)


def solution(mesh):
    placed = (
        P("side", None, ("grp", "dev")),
        P("side", ("grp", "dev"), None, None),
        P("side", ("grp", "dev")),
        P("side", ("grp", "dev")),
        P(("grp", "dev")),
    )
    return jax.shard_map(
        on_device,
        mesh=mesh,
        in_specs=placed,
        out_specs=(P(None, "side", None, ("grp", "dev")), P()),
        check_vma=False,
    )
```

```python
import functools

import jax
import jax.numpy as jnp
from jax import lax
from jax.experimental import pallas as pl
from jax.experimental.pallas import tpu as pltpu
from jax.sharding import PartitionSpec as P

BLOCK = 128
BLK_DEV = 2
ITERS = 3
ROWS = 8
HALF_RHS = 4
EPSILON = 1e-06
AXES = ("side", "grp", "dev")
VMEM_LIMIT = 48 * 2**20
LENGTH_LANE = ITERS * (ITERS + 1)


def position():
    side = lax.axis_index("side")
    dev = lax.axis_index("dev")
    owner = lax.axis_index("grp") * lax.axis_size("dev") + dev
    return side, owner, lax.rem(dev, 2)


def iota(shape, axis):
    return lax.broadcasted_iota(jnp.int32, shape, axis)


def per_rhs(tile):
    column = jnp.sum(tile, axis=1, keepdims=True)
    return column + jnp.concatenate([column[HALF_RHS:], column[:HALF_RHS]], axis=0)


def dot(left, right):
    return per_rhs(jnp.sum(left * right, axis=0))


def columns(values):
    lane = iota((ROWS, BLOCK), 1)
    tile = jnp.zeros((ROWS, BLOCK), jnp.float32)
    for index, value in values.items():
        tile = jnp.where(lane == index, value, tile)
    return tile


def mirror_onehot(mirror_ref, block):
    return (iota((BLOCK, BLOCK), 0) == mirror_ref[block : block + 1, :]).astype(jnp.float32)


def exact_dot(left, right, dims):
    return lax.dot_general(
        left, right, (dims, ((), ())),
        precision=lax.Precision.HIGHEST, preferred_element_type=jnp.float32,
    )


def start_kernel(sources_hbm, mirror_hbm, chunk_ref, mirror_ref, sources_ref, sems):
    copies = [
        pltpu.make_async_copy(sources_hbm, sources_ref, sems.at[0]),
        pltpu.make_async_copy(mirror_hbm, mirror_ref, sems.at[1]),
    ]
    for copy in copies:
        copy.start()
    for copy in copies:
        copy.wait()
    side, _, _ = position()
    pieces = []
    for block in range(BLK_DEV):
        part = sources_ref[:, block * BLOCK : (block + 1) * BLOCK]
        places = jnp.broadcast_to(mirror_ref[block : block + 1, :], part.shape)
        moved = jnp.take_along_axis(part, places, axis=1, mode="promise_in_bounds")
        pieces.append(jnp.where(side == 0, part, moved))
    tiles = [
        jnp.concatenate([piece[HALF_RHS * c : HALF_RHS * (c + 1)] for piece in pieces], axis=0)
        for c in range(2)
    ]
    chips = chunk_ref.shape[0] // 2

    def store(chip, carry):
        chunk_ref[2 * chip] = tiles[0]
        chunk_ref[2 * chip + 1] = tiles[1]
        return carry

    lax.fori_loop(0, chips, store, 0, unroll=chips <= 32)


def prepare_kernel(blocks_hbm, own_rows, own_cols, other_rows, other_cols, blocks_ref, pick_ref,
                   sem):
    copy = pltpu.make_async_copy(blocks_hbm, blocks_ref, sem)
    copy.start()
    width = pick_ref.shape[1]
    half_of_row = iota((ROWS, width), 0) // HALF_RHS
    rhs_of_row = iota((ROWS, width), 0) % HALF_RHS
    lane = iota((ROWS, width), 1)
    for entry in range(blocks_ref.shape[0]):
        picks = []
        for rows, cols in ((own_rows, own_cols), (other_rows, other_cols)):
            place = jnp.where(
                half_of_row == rows[0, entry], HALF_RHS * cols[0, entry] + rhs_of_row, -1
            )
            picks.append((lane == place).astype(jnp.float32))
        first = 2 * ROWS * entry
        pick_ref[first : first + 2 * ROWS, :] = jnp.concatenate(picks, axis=0).astype(jnp.bfloat16)
    copy.wait()


def image(vector_ref, pick_ref, own_ref, other_ref):
    side, owner, core = position()
    owners = vector_ref.shape[0] // 2
    half = vector_ref[pl.ds(side * owners, owners)]
    rounded = half.reshape(owners * ROWS, BLOCK).astype(jnp.bfloat16)
    picked = lax.dot_general(
        pick_ref[...], rounded, (((1,), (0,)), ((), ())), preferred_element_type=jnp.float32
    ).astype(jnp.bfloat16)
    sums = [jnp.zeros((2 * ROWS, 2 * BLOCK), jnp.float32) for _ in range(2)]
    for entry in range(0, own_ref.shape[0], 2):
        first = 2 * ROWS * entry
        left = jnp.concatenate(
            [picked[first : first + 2 * ROWS], picked[first + 2 * ROWS : first + 4 * ROWS]], axis=1
        )
        right = jnp.concatenate(
            [jnp.concatenate([ref[entry], ref[entry + 1]], axis=1) for ref in (own_ref, other_ref)],
            axis=0,
        )
        sums[entry // 2 % 2] += lax.dot_general(
            left, right, (((1,), (1,)), ((), ())), preferred_element_type=jnp.float32
        )
    total = sums[0] + sums[1]
    own = total[:ROWS, :BLOCK]
    other = total[ROWS:, BLOCK:]
    base = side * owners + owner - core
    low = jnp.where(core == 0, own, other) + 0.5 * vector_ref[base]
    high = jnp.where(core == 0, other, own) + 0.5 * vector_ref[base + 1]
    return low, high


def spread(chunk_ref, low, high):
    chips = chunk_ref.shape[0]

    def store(chip, carry):
        chunk_ref[chip, 0] = low
        chunk_ref[chip, 1] = high
        return carry

    lax.fori_loop(0, chips, store, 0, unroll=chips <= 32)


def first_kernel(total, got_ref, pick_ref, own_ref, other_ref, chunk_ref, basis_ref, coeff_ref):
    owners = got_ref.shape[0] // 2
    port = got_ref[:owners]
    star = got_ref[owners:]
    squares = per_rhs(jnp.sum(port * port + star * star, axis=0))
    squares = squares * (1.0 / total) + EPSILON
    scale = lax.rsqrt(squares)
    coeff_ref[...] = columns({LENGTH_LANE: jnp.sqrt(squares)})
    basis_ref[:owners] = (port + star) * scale
    basis_ref[owners:] = (port - star) * scale
    spread(chunk_ref, *image(basis_ref, pick_ref, own_ref, other_ref))


def orthogonalized(total, shift, got_ref, basis_refs):
    inner = 0.5 / total
    chips = got_ref.shape[0]
    got = jnp.concatenate([got_ref[chips - shift :], got_ref[: chips - shift]], axis=0)
    got = got.reshape(basis_refs[0].shape)
    coeffs = [dot(got, ref[...]) * inner for ref in basis_refs]
    rest = got
    for coeff, ref in zip(coeffs, basis_refs):
        rest = rest - coeff * ref[...]
    squares = dot(rest, rest) * inner + EPSILON
    return coeffs + [jnp.sqrt(squares)], rest * lax.rsqrt(squares)


def middle_kernel(total, shift, got_ref, basis_ref, known_ref, pick_ref, own_ref, other_ref,
                  chunk_ref, next_ref, coeff_ref):
    coeffs, next_ref[...] = orthogonalized(total, shift, got_ref, [basis_ref])
    coeff_ref[...] = columns(dict(enumerate(coeffs))) + known_ref[...]
    spread(chunk_ref, *image(next_ref, pick_ref, own_ref, other_ref))


def last_kernel(total, shift, got_ref, zero_ref, one_ref, known_ref, pick_ref, own_ref, other_ref,
                chunk_ref, two_ref, coeff_ref, same_ref, flip_ref):
    side, owner, core = position()
    owners = two_ref.shape[0] // 2
    refs = [zero_ref, one_ref, two_ref]
    coeffs, two_ref[...] = orthogonalized(total, shift, got_ref, refs[:2])
    tiles = image(two_ref, pick_ref, own_ref, other_ref)
    base = side * owners + owner - core
    rhs = iota((ROWS, BLOCK), 0)
    lane = iota((ROWS, BLOCK), 1)
    spots = jnp.zeros((ROWS, BLOCK), jnp.float32)
    for index in range(ITERS + 1):
        if index < ITERS:
            product = tiles[0] * refs[index][base] + tiles[1] * refs[index][base + 1]
        else:
            product = tiles[0] * tiles[0] + tiles[1] * tiles[1]
        column = jnp.sum(product, axis=1, keepdims=True)
        spots = jnp.where(lane == ROWS * index + rhs, column, spots)
    row = jnp.sum(spots, axis=0, keepdims=True)
    chunk_ref[...] = jnp.broadcast_to(row, chunk_ref.shape)
    coeffs = columns({place + ITERS + 1: value for place, value in enumerate(coeffs)})
    coeff_ref[...] = coeffs + known_ref[...]
    same_ref[...] = jnp.where(core == 0, tiles[0], tiles[1])
    flip_ref[...] = jnp.where(core == 0, tiles[1], tiles[0])


def pack_kernel(zero_ref, one_ref, two_ref, coeff_ref, flip_ref, theirs_ref):
    _, owner, core = position()
    owners = zero_ref.shape[0] // 2
    for index, ref in enumerate((zero_ref, one_ref, two_ref)):
        for half in range(2):
            theirs_ref[2 * index + half] = ref[half * owners + owner + 1 - 2 * core]
    theirs_ref[2 * ITERS] = flip_ref[...]
    theirs_ref[2 * ITERS + 1] = coeff_ref[...]


def keep_kernel(zero_ref, one_ref, two_ref, coeff_ref, same_ref, theirs_ref, across_ref,
                flipped_ref, mirror_ref, kept_ref, known_ref, gram_ref):
    side, owner, core = position()
    owners = zero_ref.shape[0] // 2

    def by_core(mine, theirs):
        return [jnp.where(core == 0, mine, theirs), jnp.where(core == 0, theirs, mine)]

    pairs = []
    for index, ref in enumerate((zero_ref, one_ref, two_ref)):
        pairs.append(
            [
                by_core(ref[half * owners + owner], theirs_ref[2 * index + half])
                for half in range(2)
            ]
        )
    here = by_core(same_ref[...], theirs_ref[2 * ITERS])
    there = by_core(across_ref[...], flipped_ref[...])
    pairs.append(
        [
            [jnp.where(side == 0, h, t) for h, t in zip(here, there)],
            [jnp.where(side == 0, t, h) for h, t in zip(here, there)],
        ]
    )
    known = by_core(coeff_ref[...], theirs_ref[2 * ITERS + 1])
    known = jnp.concatenate([tile[:HALF_RHS] for tile in known], axis=0)
    known_ref[...] = jnp.where(iota((ROWS, BLOCK), 1) < LENGTH_LANE, known, 0.0)

    def entry(j, k):
        place = k * (ITERS + 1) + j
        return known[:, place : place + 1]

    norms = [known[:, LENGTH_LANE : LENGTH_LANE + 1], entry(1, 0), entry(2, 1)]
    short = [EPSILON / (norm * norm) for norm in norms]
    zero_one = entry(0, 0) * short[0] / norms[1]
    zero_two = (entry(0, 1) * short[0] - entry(1, 1) * zero_one) / norms[2]
    one_two = (entry(1, 1) * short[1] - entry(0, 1) * zero_one) / norms[2]
    gram_ref[...] = columns(dict(enumerate(short + [zero_one, zero_two, one_two])))
    for block in range(BLK_DEV):
        rows = slice(block * HALF_RHS, (block + 1) * HALF_RHS)
        ports, stars = [], []
        for sym, anti in pairs:
            sym = jnp.concatenate([tile[rows] for tile in sym], axis=0)
            anti = jnp.concatenate([tile[rows] for tile in anti], axis=0)
            ports.append(0.5 * (sym + anti))
            stars.append(0.5 * (sym - anti))
        back = exact_dot(
            jnp.concatenate(stars, axis=0), mirror_onehot(mirror_ref, block), ((1,), (1,))
        )
        for index, port in enumerate(ports):
            kept_ref[index, :, block * BLOCK : (block + 1) * BLOCK] = jnp.where(
                side == 0, port, back[index * ROWS : (index + 1) * ROWS]
            )


def final_kernel(total, got_ref, kept_ref, known_ref, gram_ref, basis_ref, hessenberg_ref):
    inner = 0.5 / total
    sums = jnp.sum(got_ref[...].reshape(-1, ROWS, BLOCK), axis=0)
    even = iota((ROWS, BLOCK), 0) % 2 == 0
    lower = jnp.sum(jnp.where(even, sums, 0.0), axis=0, keepdims=True)
    upper = jnp.sum(jnp.where(even, 0.0, sums), axis=0, keepdims=True)
    rhs = iota((ROWS, BLOCK), 0)
    lane = iota((ROWS, BLOCK), 1)
    spots = jnp.where(rhs < HALF_RHS, lower, upper) * inner
    values = [
        jnp.sum(
            jnp.where((lane // ROWS == index) & (lane % HALF_RHS == rhs % HALF_RHS), spots, 0.0),
            axis=1,
            keepdims=True,
        )
        for index in range(ITERS + 1)
    ]
    coeffs = values[:ITERS]
    gram = gram_ref[...]
    squares = values[ITERS]
    for j in range(ITERS):
        squares = squares - coeffs[j] * coeffs[j] * (1.0 + gram[:, j : j + 1])
    for place, (i, j) in enumerate(((0, 1), (0, 2), (1, 2))):
        squares = squares + 2.0 * coeffs[i] * coeffs[j] * gram[:, ITERS + place : ITERS + place + 1]
    squares = jnp.maximum(squares, 0.0) + EPSILON
    norm = jnp.sqrt(squares)
    rest = kept_ref[ITERS]
    for j in range(ITERS):
        rest = rest - coeffs[j] * kept_ref[j]
    basis_ref[:ITERS] = kept_ref[:ITERS]
    basis_ref[ITERS] = rest * lax.rsqrt(squares)
    place = 2 * (ITERS + 1)
    whole = known_ref[...] + columns(
        {place + index: value for index, value in enumerate(coeffs + [norm])}
    )
    turned = whole.T
    for k in range(ITERS):
        hessenberg_ref[k] = turned[k * (ITERS + 1) : (k + 1) * (ITERS + 1), :]


VMEM = pl.BlockSpec(memory_space=pltpu.VMEM)
SMEM = pl.BlockSpec(memory_space=pltpu.SMEM)
HBM = pl.BlockSpec(memory_space=pltpu.HBM)


def shaped(*shape, dtype=jnp.float32):
    return jax.ShapeDtypeStruct(shape, dtype)


def in_hbm(value):
    return pltpu.with_memory_space_constraint(value, pltpu.HBM)


def call(kernel, outs, specs, scratch=(), name=None):
    return pl.pallas_call(
        kernel,
        out_shape=outs,
        in_specs=specs,
        out_specs=[VMEM] * len(outs),
        scratch_shapes=scratch,
        compiler_params=pltpu.CompilerParams(vmem_limit_bytes=VMEM_LIMIT),
        name=name,
    )


def on_device(sources, near_blocks, block_rows, block_cols, mirror):
    devices = lax.axis_size(AXES)
    owners = devices // 2
    chips = devices // 2
    panels = sources.shape[2]
    total = 1.0 * panels * devices
    shift = 1
    same_core = [
        [(2 * (chip + shift) + core) % devices for chip in range(chips)] for core in range(2)
    ]
    mirror_rows = mirror.reshape(BLK_DEV, BLOCK)
    blocks = near_blocks[0]
    vector = shaped(devices, ROWS, BLOCK)
    chunk = shaped(chips, 2, ROWS, BLOCK)
    tile = shaped(ROWS, BLOCK)

    def swapped(value, bits):
        return lax.ppermute(value, AXES, [(i, i ^ bits) for i in range(devices)])

    def exchanged(chunks):
        return lax.all_to_all(chunks, AXES, 0, 0, axis_index_groups=same_core)

    chunks, mirror_rows = call(
        start_kernel,
        [pltpu.VMEM(vector.shape, jnp.float32), shaped(*mirror_rows.shape, dtype=jnp.int32)],
        [HBM, HBM],
        [pltpu.VMEM(sources.shape[1:], jnp.float32), pltpu.SemaphoreType.DMA((2,))],
        name="start",
    )(in_hbm(sources[0]), in_hbm(mirror_rows))
    chunks, blocks, block_rows, block_cols = lax.optimization_barrier(
        (chunks, blocks, block_rows, block_cols)
    )
    got = lax.all_to_all(chunks, AXES, 0, 0)
    other_blocks = swapped(blocks, 1)
    own_blocks, pick = call(
        prepare_kernel,
        [
            shaped(*blocks.shape, dtype=blocks.dtype),
            shaped(2 * ROWS * blocks.shape[0], owners * ROWS, dtype=jnp.bfloat16),
        ],
        [HBM] + [SMEM] * 4, [pltpu.SemaphoreType.DMA], name="prepare",
    )(in_hbm(blocks), block_rows, block_cols, swapped(block_rows, 1), swapped(block_cols, 1))
    near = (pick, own_blocks, other_blocks)
    chunks, zero, coeff = call(
        functools.partial(first_kernel, total), [chunk, vector, tile], [VMEM] * 4, name="first"
    )(got, *near)
    got = exchanged(chunks)
    chunks, one, coeff = call(
        functools.partial(middle_kernel, total, shift), [chunk, vector, tile], [VMEM] * 6,
        name="middle",
    )(got, zero, coeff, *near)
    got = exchanged(chunks)
    chunks, two, coeff, same, flip = call(
        functools.partial(last_kernel, total, shift),
        [pltpu.VMEM((devices, BLOCK), jnp.float32), vector, tile, tile, tile], [VMEM] * 7,
        name="last",
    )(got, zero, one, coeff, *near)
    got = lax.all_to_all(chunks.reshape(devices, 1, BLOCK), AXES, 0, 0)
    [theirs] = call(
        pack_kernel, [shaped(2 * ITERS + 2, ROWS, BLOCK)], [VMEM] * 5, name="pack"
    )(zero, one, two, coeff, flip)
    kept, known, gram = call(
        keep_kernel, [shaped(ITERS + 1, ROWS, panels), tile, tile], [VMEM] * 9, name="keep"
    )(
        zero, one, two, coeff, same, swapped(theirs, 1), swapped(same, devices // 2),
        swapped(flip, devices // 2 ^ 1), mirror_rows,
    )
    basis, hessenberg = call(
        functools.partial(final_kernel, total),
        [shaped(ITERS + 1, ROWS, panels), shaped(ITERS, ITERS + 1, ROWS)], [VMEM] * 4,
        name="final",
    )(got.reshape(devices, BLOCK), kept, known, gram)
    return basis[:, None], hessenberg.transpose(2, 1, 0)


def solution(mesh):
    placed = (
        P("side", None, ("grp", "dev")),
        P("side", ("grp", "dev"), None, None),
        P("side", ("grp", "dev")),
        P("side", ("grp", "dev")),
        P(("grp", "dev")),
    )
    return jax.shard_map(
        on_device,
        mesh=mesh,
        in_specs=placed,
        out_specs=(P(None, "side", None, ("grp", "dev")), P()),
        check_vma=False,
    )
```

```python
import functools

import jax
import jax.numpy as jnp
from jax import lax
from jax.experimental import pallas as pl
from jax.experimental.pallas import tpu as pltpu
from jax.sharding import PartitionSpec as P

BLOCK = 128
BLK_DEV = 2
ITERS = 3
ROWS = 8
HALF_RHS = 4
EPSILON = 1e-06
AXES = ("side", "grp", "dev")
VMEM_LIMIT = 48 * 2**20
LENGTH_LANE = ITERS * (ITERS + 1)


def position():
    side = lax.axis_index("side")
    dev = lax.axis_index("dev")
    owner = lax.axis_index("grp") * lax.axis_size("dev") + dev
    return side, owner, lax.rem(dev, 2)


def iota(shape, axis):
    return lax.broadcasted_iota(jnp.int32, shape, axis)


def per_rhs(tile):
    column = jnp.sum(tile, axis=1, keepdims=True)
    return column + jnp.concatenate([column[HALF_RHS:], column[:HALF_RHS]], axis=0)


def dot(left, right):
    return per_rhs(jnp.sum(left * right, axis=0))


def columns(values):
    lane = iota((ROWS, BLOCK), 1)
    tile = jnp.zeros((ROWS, BLOCK), jnp.float32)
    for index, value in values.items():
        tile = jnp.where(lane == index, value, tile)
    return tile


def mirror_onehot(mirror_ref, block):
    return (iota((BLOCK, BLOCK), 0) == mirror_ref[block : block + 1, :]).astype(jnp.float32)


def exact_dot(left, right, dims):
    return lax.dot_general(
        left, right, (dims, ((), ())),
        precision=lax.Precision.HIGHEST, preferred_element_type=jnp.float32,
    )


def start_kernel(sources_hbm, mirror_hbm, chunk_ref, mirror_ref, sources_ref, sems):
    copies = [
        pltpu.make_async_copy(sources_hbm, sources_ref, sems.at[0]),
        pltpu.make_async_copy(mirror_hbm, mirror_ref, sems.at[1]),
    ]
    for copy in copies:
        copy.start()
    for copy in copies:
        copy.wait()
    side, _, _ = position()
    pieces = []
    for block in range(BLK_DEV):
        part = sources_ref[:, block * BLOCK : (block + 1) * BLOCK]
        places = jnp.broadcast_to(mirror_ref[block : block + 1, :], part.shape)
        moved = jnp.take_along_axis(part, places, axis=1, mode="promise_in_bounds")
        pieces.append(jnp.where(side == 0, part, moved))
    tiles = [
        jnp.concatenate([piece[HALF_RHS * c : HALF_RHS * (c + 1)] for piece in pieces], axis=0)
        for c in range(2)
    ]
    chips = chunk_ref.shape[0] // 2

    def store(chip, carry):
        chunk_ref[2 * chip] = tiles[0]
        chunk_ref[2 * chip + 1] = tiles[1]
        return carry

    lax.fori_loop(0, chips, store, 0, unroll=chips <= 32)


def prepare_kernel(blocks_hbm, own_rows, own_cols, other_rows, other_cols, blocks_ref, pick_ref,
                   sem):
    copy = pltpu.make_async_copy(blocks_hbm, blocks_ref, sem)
    copy.start()
    width = pick_ref.shape[1]
    half_of_row = iota((ROWS, width), 0) // HALF_RHS
    rhs_of_row = iota((ROWS, width), 0) % HALF_RHS
    lane = iota((ROWS, width), 1)
    for entry in range(blocks_ref.shape[0]):
        picks = []
        for rows, cols in ((own_rows, own_cols), (other_rows, other_cols)):
            place = jnp.where(
                half_of_row == rows[0, entry], HALF_RHS * cols[0, entry] + rhs_of_row, -1
            )
            picks.append((lane == place).astype(jnp.float32))
        first = 2 * ROWS * entry
        pick_ref[first : first + 2 * ROWS, :] = jnp.concatenate(picks, axis=0).astype(jnp.bfloat16)
    copy.wait()


def near(half, pick_ref, own_ref, other_ref):
    flat = half.reshape(-1, BLOCK)
    coarse = flat.astype(jnp.bfloat16)
    fine = (flat - coarse.astype(jnp.float32)).astype(jnp.bfloat16)
    picked = lax.dot_general(
        pick_ref[...], jnp.concatenate([coarse, fine], axis=1), (((1,), (0,)), ((), ())),
        preferred_element_type=jnp.float32,
    ).astype(jnp.bfloat16)
    sums = [jnp.zeros((4 * ROWS, 2 * BLOCK), jnp.float32) for _ in range(2)]
    for entry in range(0, own_ref.shape[0], 2):
        rows = [slice(2 * ROWS * place, 2 * ROWS * (place + 1)) for place in (entry, entry + 1)]
        left = jnp.concatenate(
            [
                jnp.concatenate([picked[rows[0], part], picked[rows[1], part]], axis=1)
                for part in (slice(0, BLOCK), slice(BLOCK, 2 * BLOCK))
            ],
            axis=0,
        )
        right = jnp.concatenate(
            [jnp.concatenate([ref[entry], ref[entry + 1]], axis=1) for ref in (own_ref, other_ref)],
            axis=0,
        )
        sums[entry // 2 % 2] += lax.dot_general(
            left, right, (((1,), (1,)), ((), ())), preferred_element_type=jnp.float32
        )
    total = sums[0] + sums[1]
    total = total[: 2 * ROWS] + total[2 * ROWS :]
    _, _, core = position()
    own = total[:ROWS, :BLOCK]
    other = total[ROWS:, BLOCK:]
    return jnp.where(core == 0, own, other), jnp.where(core == 0, other, own)


def spread(chunk_ref, low, high):
    chips = chunk_ref.shape[0]

    def store(chip, carry):
        chunk_ref[chip, 0] = low
        chunk_ref[chip, 1] = high
        return carry

    lax.fori_loop(0, chips, store, 0, unroll=chips <= 32)


def first_kernel(total, got_ref, pick_ref, own_ref, other_ref, chunk_ref, basis_ref, coeff_ref):
    side, owner, core = position()
    owners = got_ref.shape[0] // 2
    base = owner - core
    port = got_ref[:owners]
    star = got_ref[owners:]
    sym = port + star
    anti = port - star
    tiles = near(jnp.where(side == 0, sym, anti), pick_ref, own_ref, other_ref)
    squares = per_rhs(jnp.sum(port * port + star * star, axis=0)) * (1.0 / total) + EPSILON
    scale = lax.rsqrt(squares)
    coeff_ref[...] = columns({LENGTH_LANE: jnp.sqrt(squares)})
    basis_ref[:owners] = sym * scale
    basis_ref[owners:] = anti * scale
    images = []
    for place, tile in enumerate(tiles):
        here, there = got_ref[base + place], got_ref[owners + base + place]
        images.append((tile + 0.5 * jnp.where(side == 0, here + there, here - there)) * scale)
    spread(chunk_ref, *images)


def in_order(got_ref, shift):
    chips = got_ref.shape[0]
    return jnp.concatenate([got_ref[chips - shift :], got_ref[: chips - shift]], axis=0)


def own_tiles(got_ref, shift):
    side, owner, _ = position()
    chips = got_ref.shape[0]
    chip = lax.rem(side * (chips // 2) + owner // 2 + chips - shift, chips)
    return got_ref[chip, 0], got_ref[chip, 1]


def advanced(total, shift, got_refs, basis_refs, pick_ref, own_ref, other_ref):
    side, _, _ = position()
    got = in_order(got_refs[-1], shift)
    half = got.shape[0] // 2
    tiles = near(jnp.where(side == 0, got[:half], got[half:]), pick_ref, own_ref, other_ref)
    got = got.reshape(basis_refs[0].shape)
    inner = 0.5 / total
    coeffs = [dot(got, ref[...]) * inner for ref in basis_refs]
    rest = got
    for coeff, ref in zip(coeffs, basis_refs):
        rest = rest - coeff * ref[...]
    squares = dot(rest, rest) * inner + EPSILON
    scale = lax.rsqrt(squares)
    owned = [own_tiles(ref, shift) for ref in got_refs]
    images = []
    for place, tile in enumerate(tiles):
        value = tile + 0.5 * owned[-1][place]
        for coeff, earlier in zip(coeffs, owned):
            value = value - coeff * earlier[place]
        images.append(value * scale)
    return coeffs + [jnp.sqrt(squares)], rest * scale, images


def middle_kernel(total, shift, got_ref, basis_ref, known_ref, pick_ref, own_ref, other_ref,
                  chunk_ref, next_ref, coeff_ref):
    coeffs, next_ref[...], images = advanced(
        total, shift, [got_ref], [basis_ref], pick_ref, own_ref, other_ref
    )
    coeff_ref[...] = columns(dict(enumerate(coeffs))) + known_ref[...]
    spread(chunk_ref, *images)


def last_kernel(total, shift, first_got_ref, got_ref, zero_ref, one_ref, known_ref, pick_ref,
                own_ref, other_ref, chunk_ref, two_ref, coeff_ref, same_ref, flip_ref):
    side, owner, core = position()
    owners = two_ref.shape[0] // 2
    refs = [zero_ref, one_ref, two_ref]
    coeffs, two_ref[...], tiles = advanced(
        total, shift, [first_got_ref, got_ref], refs[:2], pick_ref, own_ref, other_ref
    )
    base = side * owners + owner - core
    rhs = iota((ROWS, BLOCK), 0)
    lane = iota((ROWS, BLOCK), 1)
    spots = jnp.zeros((ROWS, BLOCK), jnp.float32)
    for index in range(ITERS + 1):
        if index < ITERS:
            product = tiles[0] * refs[index][base] + tiles[1] * refs[index][base + 1]
        else:
            product = tiles[0] * tiles[0] + tiles[1] * tiles[1]
        column = jnp.sum(product, axis=1, keepdims=True)
        spots = jnp.where(lane == ROWS * index + rhs, column, spots)
    row = jnp.sum(spots, axis=0, keepdims=True)
    chunk_ref[...] = jnp.broadcast_to(row, chunk_ref.shape)
    coeffs = columns({place + ITERS + 1: value for place, value in enumerate(coeffs)})
    coeff_ref[...] = coeffs + known_ref[...]
    same_ref[...] = jnp.where(core == 0, tiles[0], tiles[1])
    flip_ref[...] = jnp.where(core == 0, tiles[1], tiles[0])


def pack_kernel(zero_ref, one_ref, two_ref, coeff_ref, flip_ref, theirs_ref):
    _, owner, core = position()
    owners = zero_ref.shape[0] // 2
    for index, ref in enumerate((zero_ref, one_ref, two_ref)):
        for half in range(2):
            theirs_ref[2 * index + half] = ref[half * owners + owner + 1 - 2 * core]
    theirs_ref[2 * ITERS] = flip_ref[...]
    theirs_ref[2 * ITERS + 1] = coeff_ref[...]


def keep_kernel(zero_ref, one_ref, two_ref, coeff_ref, same_ref, theirs_ref, across_ref,
                flipped_ref, mirror_ref, kept_ref, known_ref, gram_ref):
    side, owner, core = position()
    owners = zero_ref.shape[0] // 2

    def by_core(mine, theirs):
        return [jnp.where(core == 0, mine, theirs), jnp.where(core == 0, theirs, mine)]

    pairs = []
    for index, ref in enumerate((zero_ref, one_ref, two_ref)):
        pairs.append(
            [
                by_core(ref[half * owners + owner], theirs_ref[2 * index + half])
                for half in range(2)
            ]
        )
    here = by_core(same_ref[...], theirs_ref[2 * ITERS])
    there = by_core(across_ref[...], flipped_ref[...])
    pairs.append(
        [
            [jnp.where(side == 0, h, t) for h, t in zip(here, there)],
            [jnp.where(side == 0, t, h) for h, t in zip(here, there)],
        ]
    )
    known = by_core(coeff_ref[...], theirs_ref[2 * ITERS + 1])
    known = jnp.concatenate([tile[:HALF_RHS] for tile in known], axis=0)
    known_ref[...] = jnp.where(iota((ROWS, BLOCK), 1) < LENGTH_LANE, known, 0.0)

    def entry(j, k):
        place = k * (ITERS + 1) + j
        return known[:, place : place + 1]

    norms = [known[:, LENGTH_LANE : LENGTH_LANE + 1], entry(1, 0), entry(2, 1)]
    short = [EPSILON / (norm * norm) for norm in norms]
    zero_one = entry(0, 0) * short[0] / norms[1]
    zero_two = (entry(0, 1) * short[0] - entry(1, 1) * zero_one) / norms[2]
    one_two = (entry(1, 1) * short[1] - entry(0, 1) * zero_one) / norms[2]
    gram_ref[...] = columns(dict(enumerate(short + [zero_one, zero_two, one_two])))
    for block in range(BLK_DEV):
        rows = slice(block * HALF_RHS, (block + 1) * HALF_RHS)
        ports, stars = [], []
        for sym, anti in pairs:
            sym = jnp.concatenate([tile[rows] for tile in sym], axis=0)
            anti = jnp.concatenate([tile[rows] for tile in anti], axis=0)
            ports.append(0.5 * (sym + anti))
            stars.append(0.5 * (sym - anti))
        back = exact_dot(
            jnp.concatenate(stars, axis=0), mirror_onehot(mirror_ref, block), ((1,), (1,))
        )
        for index, port in enumerate(ports):
            kept_ref[index, :, block * BLOCK : (block + 1) * BLOCK] = jnp.where(
                side == 0, port, back[index * ROWS : (index + 1) * ROWS]
            )


def final_kernel(total, got_ref, kept_ref, known_ref, gram_ref, basis_ref, hessenberg_ref):
    inner = 0.5 / total
    sums = jnp.sum(got_ref[...].reshape(-1, ROWS, BLOCK), axis=0)
    even = iota((ROWS, BLOCK), 0) % 2 == 0
    lower = jnp.sum(jnp.where(even, sums, 0.0), axis=0, keepdims=True)
    upper = jnp.sum(jnp.where(even, 0.0, sums), axis=0, keepdims=True)
    rhs = iota((ROWS, BLOCK), 0)
    lane = iota((ROWS, BLOCK), 1)
    spots = jnp.where(rhs < HALF_RHS, lower, upper) * inner
    values = [
        jnp.sum(
            jnp.where((lane // ROWS == index) & (lane % HALF_RHS == rhs % HALF_RHS), spots, 0.0),
            axis=1,
            keepdims=True,
        )
        for index in range(ITERS + 1)
    ]
    coeffs = values[:ITERS]
    gram = gram_ref[...]
    squares = values[ITERS]
    for j in range(ITERS):
        squares = squares - coeffs[j] * coeffs[j] * (1.0 + gram[:, j : j + 1])
    for place, (i, j) in enumerate(((0, 1), (0, 2), (1, 2))):
        squares = squares + 2.0 * coeffs[i] * coeffs[j] * gram[:, ITERS + place : ITERS + place + 1]
    squares = jnp.maximum(squares, 0.0) + EPSILON
    norm = jnp.sqrt(squares)
    rest = kept_ref[ITERS]
    for j in range(ITERS):
        rest = rest - coeffs[j] * kept_ref[j]
    basis_ref[:ITERS] = kept_ref[:ITERS]
    basis_ref[ITERS] = rest * lax.rsqrt(squares)
    place = 2 * (ITERS + 1)
    whole = known_ref[...] + columns(
        {place + index: value for index, value in enumerate(coeffs + [norm])}
    )
    turned = whole.T
    for k in range(ITERS):
        hessenberg_ref[k] = turned[k * (ITERS + 1) : (k + 1) * (ITERS + 1), :]


VMEM = pl.BlockSpec(memory_space=pltpu.VMEM)
SMEM = pl.BlockSpec(memory_space=pltpu.SMEM)
HBM = pl.BlockSpec(memory_space=pltpu.HBM)


def shaped(*shape, dtype=jnp.float32):
    return jax.ShapeDtypeStruct(shape, dtype)


def in_hbm(value):
    return pltpu.with_memory_space_constraint(value, pltpu.HBM)


def call(kernel, outs, specs, scratch=(), name=None):
    return pl.pallas_call(
        kernel,
        out_shape=outs,
        in_specs=specs,
        out_specs=[VMEM] * len(outs),
        scratch_shapes=scratch,
        compiler_params=pltpu.CompilerParams(vmem_limit_bytes=VMEM_LIMIT),
        name=name,
    )


def on_device(sources, near_blocks, block_rows, block_cols, mirror):
    devices = lax.axis_size(AXES)
    owners = devices // 2
    chips = devices // 2
    panels = sources.shape[2]
    total = 1.0 * panels * devices
    shift = 1
    same_core = [
        [(2 * (chip + shift) + core) % devices for chip in range(chips)] for core in range(2)
    ]
    mirror_rows = mirror.reshape(BLK_DEV, BLOCK)
    blocks = near_blocks[0]
    vector = shaped(devices, ROWS, BLOCK)
    chunk = shaped(chips, 2, ROWS, BLOCK)
    tile = shaped(ROWS, BLOCK)

    def swapped(value, bits):
        return lax.ppermute(value, AXES, [(i, i ^ bits) for i in range(devices)])

    def exchanged(chunks):
        return lax.all_to_all(chunks, AXES, 0, 0, axis_index_groups=same_core)

    chunks, mirror_rows = call(
        start_kernel,
        [pltpu.VMEM(vector.shape, jnp.float32), shaped(*mirror_rows.shape, dtype=jnp.int32)],
        [HBM, HBM],
        [pltpu.VMEM(sources.shape[1:], jnp.float32), pltpu.SemaphoreType.DMA((2,))],
        name="start",
    )(in_hbm(sources[0]), in_hbm(mirror_rows))
    chunks, blocks, block_rows, block_cols = lax.optimization_barrier(
        (chunks, blocks, block_rows, block_cols)
    )
    got = lax.all_to_all(chunks, AXES, 0, 0)
    other_blocks = swapped(blocks, 1)
    own_blocks, pick = call(
        prepare_kernel,
        [
            shaped(*blocks.shape, dtype=blocks.dtype),
            shaped(2 * ROWS * blocks.shape[0], owners * ROWS, dtype=jnp.bfloat16),
        ],
        [HBM] + [SMEM] * 4, [pltpu.SemaphoreType.DMA], name="prepare",
    )(in_hbm(blocks), block_rows, block_cols, swapped(block_rows, 1), swapped(block_cols, 1))
    near_args = (pick, own_blocks, other_blocks)
    chunks, zero, coeff = call(
        functools.partial(first_kernel, total), [chunk, vector, tile], [VMEM] * 4, name="first"
    )(got, *near_args)
    got = exchanged(chunks)
    chunks, one, coeff = call(
        functools.partial(middle_kernel, total, shift), [chunk, vector, tile], [VMEM] * 6,
        name="middle",
    )(got, zero, coeff, *near_args)
    first_got, got = got, exchanged(chunks)
    chunks, two, coeff, same, flip = call(
        functools.partial(last_kernel, total, shift),
        [pltpu.VMEM((devices, BLOCK), jnp.float32), vector, tile, tile, tile], [VMEM] * 8,
        name="last",
    )(first_got, got, zero, one, coeff, *near_args)
    got = lax.all_to_all(chunks.reshape(devices, 1, BLOCK), AXES, 0, 0)
    [theirs] = call(
        pack_kernel, [shaped(2 * ITERS + 2, ROWS, BLOCK)], [VMEM] * 5, name="pack"
    )(zero, one, two, coeff, flip)
    kept, known, gram = call(
        keep_kernel, [shaped(ITERS + 1, ROWS, panels), tile, tile], [VMEM] * 9, name="keep"
    )(
        zero, one, two, coeff, same, swapped(theirs, 1), swapped(same, devices // 2),
        swapped(flip, devices // 2 ^ 1), mirror_rows,
    )
    basis, hessenberg = call(
        functools.partial(final_kernel, total),
        [shaped(ITERS + 1, ROWS, panels), shaped(ITERS, ITERS + 1, ROWS)], [VMEM] * 4,
        name="final",
    )(got.reshape(devices, BLOCK), kept, known, gram)
    return basis[:, None], hessenberg.transpose(2, 1, 0)


def solution(mesh):
    placed = (
        P("side", None, ("grp", "dev")),
        P("side", ("grp", "dev"), None, None),
        P("side", ("grp", "dev")),
        P("side", ("grp", "dev")),
        P(("grp", "dev")),
    )
    return jax.shard_map(
        on_device,
        mesh=mesh,
        in_specs=placed,
        out_specs=(P(None, "side", None, ("grp", "dev")), P()),
        check_vma=False,
    )
```

```python
import functools

import jax
import jax.numpy as jnp
from jax import lax
from jax.experimental import pallas as pl
from jax.experimental.pallas import tpu as pltpu
from jax.sharding import PartitionSpec as P

BLOCK = 128
BLK_DEV = 2
ITERS = 3
ROWS = 8
HALF_RHS = 4
EPSILON = 1e-06
AXES = ("side", "grp", "dev")
VMEM_LIMIT = 48 * 2**20
LENGTH_LANE = ITERS * (ITERS + 1)


def position():
    side = lax.axis_index("side")
    dev = lax.axis_index("dev")
    owner = lax.axis_index("grp") * lax.axis_size("dev") + dev
    return side, owner, lax.rem(dev, 2)


def iota(shape, axis):
    return lax.broadcasted_iota(jnp.int32, shape, axis)


def per_rhs(tile):
    column = jnp.sum(tile, axis=1, keepdims=True)
    return column + jnp.concatenate([column[HALF_RHS:], column[:HALF_RHS]], axis=0)


def dot(left, right):
    return per_rhs(jnp.sum(left * right, axis=0))


def columns(values):
    lane = iota((ROWS, BLOCK), 1)
    tile = jnp.zeros((ROWS, BLOCK), jnp.float32)
    for index, value in values.items():
        tile = jnp.where(lane == index, value, tile)
    return tile


def mirror_onehot(mirror_ref, block):
    return (iota((BLOCK, BLOCK), 0) == mirror_ref[block : block + 1, :]).astype(jnp.float32)


def exact_dot(left, right, dims):
    return lax.dot_general(
        left, right, (dims, ((), ())),
        precision=lax.Precision.HIGHEST, preferred_element_type=jnp.float32,
    )


def start_kernel(sources_hbm, mirror_hbm, rows_hbm, cols_hbm, chunk_ref, mirror_ref, places_ref,
                 sources_ref, sems):
    copies = [
        pltpu.make_async_copy(sources_hbm, sources_ref, sems.at[0]),
        pltpu.make_async_copy(mirror_hbm, mirror_ref, sems.at[1]),
        pltpu.make_async_copy(rows_hbm, places_ref.at[0], sems.at[2]),
        pltpu.make_async_copy(cols_hbm, places_ref.at[1], sems.at[3]),
    ]
    for copy in copies:
        copy.start()
    for copy in copies:
        copy.wait()
    side, _, _ = position()
    pieces = []
    for block in range(BLK_DEV):
        part = sources_ref[:, block * BLOCK : (block + 1) * BLOCK]
        places = jnp.broadcast_to(mirror_ref[block : block + 1, :], part.shape)
        moved = jnp.take_along_axis(part, places, axis=1, mode="promise_in_bounds")
        pieces.append(jnp.where(side == 0, part, moved))
    tiles = [
        jnp.concatenate([piece[HALF_RHS * c : HALF_RHS * (c + 1)] for piece in pieces], axis=0)
        for c in range(2)
    ]
    chips = chunk_ref.shape[0] // 2

    def store(chip, carry):
        chunk_ref[2 * chip] = tiles[0]
        chunk_ref[2 * chip + 1] = tiles[1]
        return carry

    lax.fori_loop(0, chips, store, 0, unroll=chips <= 32)


def prepare_kernel(own_hbm, other_ref, own_places, other_places, weights_ref, pick_ref, own_ref,
                   sem):
    copy = pltpu.make_async_copy(own_hbm, own_ref, sem)
    copy.start()
    width = pick_ref.shape[1]
    half_of_row = iota((ROWS, width), 0) // HALF_RHS
    rhs_of_row = iota((ROWS, width), 0) % HALF_RHS
    lane = iota((ROWS, width), 1)
    for entry in range(own_ref.shape[0]):
        picks = []
        for places in (own_places, other_places):
            place = jnp.where(
                half_of_row == places[0, 0, entry], HALF_RHS * places[1, 0, entry] + rhs_of_row, -1
            )
            picks.append((lane == place).astype(jnp.float32))
        first = 2 * ROWS * entry
        pick_ref[first : first + 2 * ROWS, :] = jnp.concatenate(picks, axis=0).astype(jnp.bfloat16)
    for side, ref in ((1, other_ref), (0, own_ref)):
        if side == 0:
            copy.wait()
        for entry in range(own_ref.shape[0]):
            first = entry % 2 * BLOCK
            weights_ref[
                entry // 2, first : first + BLOCK, side * BLOCK : (side + 1) * BLOCK
            ] = ref[entry].T


def near(half, pick_ref, weights_ref):
    flat = half.reshape(-1, BLOCK)
    coarse = flat.astype(jnp.bfloat16)
    fine = (flat - coarse.astype(jnp.float32)).astype(jnp.bfloat16)
    picked = lax.dot_general(
        pick_ref[...], jnp.concatenate([coarse, fine], axis=1), (((1,), (0,)), ((), ())),
        preferred_element_type=jnp.float32,
    ).astype(jnp.bfloat16)
    sums = [jnp.zeros((4 * ROWS, 2 * BLOCK), jnp.float32) for _ in range(2)]
    for group in range(weights_ref.shape[0]):
        rows = [
            slice(2 * ROWS * place, 2 * ROWS * (place + 1)) for place in (2 * group, 2 * group + 1)
        ]
        left = jnp.concatenate(
            [
                jnp.concatenate([picked[rows[0], part], picked[rows[1], part]], axis=1)
                for part in (slice(0, BLOCK), slice(BLOCK, 2 * BLOCK))
            ],
            axis=0,
        )
        sums[group % 2] += lax.dot_general(
            left, weights_ref[group], (((1,), (0,)), ((), ())), preferred_element_type=jnp.float32
        )
    total = sums[0] + sums[1]
    total = total[: 2 * ROWS] + total[2 * ROWS :]
    _, _, core = position()
    own = total[:ROWS, :BLOCK]
    other = total[ROWS:, BLOCK:]
    return jnp.where(core == 0, own, other), jnp.where(core == 0, other, own)


def spread(chunk_ref, low, high):
    chips = chunk_ref.shape[0]

    def store(chip, carry):
        chunk_ref[chip, 0] = low
        chunk_ref[chip, 1] = high
        return carry

    lax.fori_loop(0, chips, store, 0, unroll=chips <= 32)


def first_kernel(total, got_ref, pick_ref, weights_ref, chunk_ref, basis_ref, coeff_ref):
    side, owner, core = position()
    owners = got_ref.shape[0] // 2
    base = owner - core
    port = got_ref[:owners]
    star = got_ref[owners:]
    sym = port + star
    anti = port - star
    tiles = near(jnp.where(side == 0, sym, anti), pick_ref, weights_ref)
    squares = per_rhs(jnp.sum(port * port + star * star, axis=0)) * (1.0 / total) + EPSILON
    scale = lax.rsqrt(squares)
    coeff_ref[...] = columns({LENGTH_LANE: jnp.sqrt(squares)})
    basis_ref[:owners] = sym * scale
    basis_ref[owners:] = anti * scale
    images = []
    for place, tile in enumerate(tiles):
        here, there = got_ref[base + place], got_ref[owners + base + place]
        images.append((tile + 0.5 * jnp.where(side == 0, here + there, here - there)) * scale)
    spread(chunk_ref, *images)


def in_order(got_ref, shift):
    chips = got_ref.shape[0]
    return jnp.concatenate([got_ref[chips - shift :], got_ref[: chips - shift]], axis=0)


def own_tiles(got_ref, shift):
    side, owner, _ = position()
    chips = got_ref.shape[0]
    chip = lax.rem(side * (chips // 2) + owner // 2 + chips - shift, chips)
    return got_ref[chip, 0], got_ref[chip, 1]


def advanced(total, shift, got_refs, basis_refs, pick_ref, weights_ref):
    side, _, _ = position()
    got = in_order(got_refs[-1], shift)
    half = got.shape[0] // 2
    tiles = near(jnp.where(side == 0, got[:half], got[half:]), pick_ref, weights_ref)
    got = got.reshape(basis_refs[0].shape)
    inner = 0.5 / total
    coeffs = [dot(got, ref[...]) * inner for ref in basis_refs]
    rest = got
    for coeff, ref in zip(coeffs, basis_refs):
        rest = rest - coeff * ref[...]
    squares = dot(rest, rest) * inner + EPSILON
    scale = lax.rsqrt(squares)
    owned = [own_tiles(ref, shift) for ref in got_refs]
    images = []
    for place, tile in enumerate(tiles):
        value = tile + 0.5 * owned[-1][place]
        for coeff, earlier in zip(coeffs, owned):
            value = value - coeff * earlier[place]
        images.append(value * scale)
    return coeffs + [jnp.sqrt(squares)], rest * scale, images


def middle_kernel(total, shift, got_ref, basis_ref, known_ref, pick_ref, weights_ref,
                  chunk_ref, next_ref, coeff_ref):
    coeffs, next_ref[...], images = advanced(
        total, shift, [got_ref], [basis_ref], pick_ref, weights_ref
    )
    coeff_ref[...] = columns(dict(enumerate(coeffs))) + known_ref[...]
    spread(chunk_ref, *images)


def last_kernel(total, shift, first_got_ref, got_ref, zero_ref, one_ref, known_ref, pick_ref,
                weights_ref, chunk_ref, two_ref, coeff_ref, same_ref, flip_ref):
    side, owner, core = position()
    owners = two_ref.shape[0] // 2
    refs = [zero_ref, one_ref, two_ref]
    coeffs, two_ref[...], tiles = advanced(
        total, shift, [first_got_ref, got_ref], refs[:2], pick_ref, weights_ref
    )
    base = side * owners + owner - core
    rhs = iota((ROWS, BLOCK), 0)
    lane = iota((ROWS, BLOCK), 1)
    spots = jnp.zeros((ROWS, BLOCK), jnp.float32)
    for index in range(ITERS + 1):
        if index < ITERS:
            product = tiles[0] * refs[index][base] + tiles[1] * refs[index][base + 1]
        else:
            product = tiles[0] * tiles[0] + tiles[1] * tiles[1]
        column = jnp.sum(product, axis=1, keepdims=True)
        spots = jnp.where(lane == ROWS * index + rhs, column, spots)
    row = jnp.sum(spots, axis=0, keepdims=True)
    chunk_ref[...] = jnp.broadcast_to(row, chunk_ref.shape)
    coeffs = columns({place + ITERS + 1: value for place, value in enumerate(coeffs)})
    coeff_ref[...] = coeffs + known_ref[...]
    same_ref[...] = jnp.where(core == 0, tiles[0], tiles[1])
    flip_ref[...] = jnp.where(core == 0, tiles[1], tiles[0])


def pack_kernel(zero_ref, one_ref, two_ref, coeff_ref, flip_ref, theirs_ref):
    _, owner, core = position()
    owners = zero_ref.shape[0] // 2
    for index, ref in enumerate((zero_ref, one_ref, two_ref)):
        for half in range(2):
            theirs_ref[2 * index + half] = ref[half * owners + owner + 1 - 2 * core]
    theirs_ref[2 * ITERS] = flip_ref[...]
    theirs_ref[2 * ITERS + 1] = coeff_ref[...]


def keep_kernel(zero_ref, one_ref, two_ref, coeff_ref, same_ref, theirs_ref, across_ref,
                flipped_ref, mirror_ref, kept_ref, known_ref, gram_ref):
    side, owner, core = position()
    owners = zero_ref.shape[0] // 2

    def by_core(mine, theirs):
        return [jnp.where(core == 0, mine, theirs), jnp.where(core == 0, theirs, mine)]

    pairs = []
    for index, ref in enumerate((zero_ref, one_ref, two_ref)):
        pairs.append(
            [
                by_core(ref[half * owners + owner], theirs_ref[2 * index + half])
                for half in range(2)
            ]
        )
    here = by_core(same_ref[...], theirs_ref[2 * ITERS])
    there = by_core(across_ref[...], flipped_ref[...])
    pairs.append(
        [
            [jnp.where(side == 0, h, t) for h, t in zip(here, there)],
            [jnp.where(side == 0, t, h) for h, t in zip(here, there)],
        ]
    )
    known = by_core(coeff_ref[...], theirs_ref[2 * ITERS + 1])
    known = jnp.concatenate([tile[:HALF_RHS] for tile in known], axis=0)
    known_ref[...] = jnp.where(iota((ROWS, BLOCK), 1) < LENGTH_LANE, known, 0.0)

    def entry(j, k):
        place = k * (ITERS + 1) + j
        return known[:, place : place + 1]

    norms = [known[:, LENGTH_LANE : LENGTH_LANE + 1], entry(1, 0), entry(2, 1)]
    short = [EPSILON / (norm * norm) for norm in norms]
    zero_one = entry(0, 0) * short[0] / norms[1]
    zero_two = (entry(0, 1) * short[0] - entry(1, 1) * zero_one) / norms[2]
    one_two = (entry(1, 1) * short[1] - entry(0, 1) * zero_one) / norms[2]
    gram_ref[...] = columns(dict(enumerate(short + [zero_one, zero_two, one_two])))
    for block in range(BLK_DEV):
        rows = slice(block * HALF_RHS, (block + 1) * HALF_RHS)
        ports, stars = [], []
        for sym, anti in pairs:
            sym = jnp.concatenate([tile[rows] for tile in sym], axis=0)
            anti = jnp.concatenate([tile[rows] for tile in anti], axis=0)
            ports.append(0.5 * (sym + anti))
            stars.append(0.5 * (sym - anti))
        back = exact_dot(
            jnp.concatenate(stars, axis=0), mirror_onehot(mirror_ref, block), ((1,), (1,))
        )
        for index, port in enumerate(ports):
            kept_ref[index, :, block * BLOCK : (block + 1) * BLOCK] = jnp.where(
                side == 0, port, back[index * ROWS : (index + 1) * ROWS]
            )


def final_kernel(total, got_ref, kept_ref, known_ref, gram_ref, basis_ref, hessenberg_ref):
    inner = 0.5 / total
    sums = jnp.sum(got_ref[...].reshape(-1, ROWS, BLOCK), axis=0)
    even = iota((ROWS, BLOCK), 0) % 2 == 0
    lower = jnp.sum(jnp.where(even, sums, 0.0), axis=0, keepdims=True)
    upper = jnp.sum(jnp.where(even, 0.0, sums), axis=0, keepdims=True)
    rhs = iota((ROWS, BLOCK), 0)
    lane = iota((ROWS, BLOCK), 1)
    spots = jnp.where(rhs < HALF_RHS, lower, upper) * inner
    values = [
        jnp.sum(
            jnp.where((lane // ROWS == index) & (lane % HALF_RHS == rhs % HALF_RHS), spots, 0.0),
            axis=1,
            keepdims=True,
        )
        for index in range(ITERS + 1)
    ]
    coeffs = values[:ITERS]
    gram = gram_ref[...]
    squares = values[ITERS]
    for j in range(ITERS):
        squares = squares - coeffs[j] * coeffs[j] * (1.0 + gram[:, j : j + 1])
    for place, (i, j) in enumerate(((0, 1), (0, 2), (1, 2))):
        squares = squares + 2.0 * coeffs[i] * coeffs[j] * gram[:, ITERS + place : ITERS + place + 1]
    squares = jnp.maximum(squares, 0.0) + EPSILON
    norm = jnp.sqrt(squares)
    rest = kept_ref[ITERS]
    for j in range(ITERS):
        rest = rest - coeffs[j] * kept_ref[j]
    basis_ref[:ITERS] = kept_ref[:ITERS]
    basis_ref[ITERS] = rest * lax.rsqrt(squares)
    place = 2 * (ITERS + 1)
    whole = known_ref[...] + columns(
        {place + index: value for index, value in enumerate(coeffs + [norm])}
    )
    turned = whole.T
    for k in range(ITERS):
        hessenberg_ref[k] = turned[k * (ITERS + 1) : (k + 1) * (ITERS + 1), :]


VMEM = pl.BlockSpec(memory_space=pltpu.VMEM)
SMEM = pl.BlockSpec(memory_space=pltpu.SMEM)
HBM = pl.BlockSpec(memory_space=pltpu.HBM)


def shaped(*shape, dtype=jnp.float32):
    return jax.ShapeDtypeStruct(shape, dtype)


def in_hbm(value):
    return pltpu.with_memory_space_constraint(value, pltpu.HBM)


def call(kernel, outs, specs, scratch=(), name=None):
    return pl.pallas_call(
        kernel,
        out_shape=outs,
        in_specs=specs,
        out_specs=[VMEM] * len(outs),
        scratch_shapes=scratch,
        compiler_params=pltpu.CompilerParams(vmem_limit_bytes=VMEM_LIMIT),
        name=name,
    )


def on_device(sources, near_blocks, block_rows, block_cols, mirror):
    devices = lax.axis_size(AXES)
    owners = devices // 2
    chips = devices // 2
    panels = sources.shape[2]
    total = 1.0 * panels * devices
    shift = 1
    same_core = [
        [(2 * (chip + shift) + core) % devices for chip in range(chips)] for core in range(2)
    ]
    mirror_rows = mirror.reshape(BLK_DEV, BLOCK)
    blocks = near_blocks[0]
    vector = shaped(devices, ROWS, BLOCK)
    chunk = shaped(chips, 2, ROWS, BLOCK)
    tile = shaped(ROWS, BLOCK)

    def swapped(value, bits):
        return lax.ppermute(value, AXES, [(i, i ^ bits) for i in range(devices)])

    def exchanged(chunks):
        return lax.all_to_all(chunks, AXES, 0, 0, axis_index_groups=same_core)

    chunks, mirror_rows, places = call(
        start_kernel,
        [
            vector,
            shaped(*mirror_rows.shape, dtype=jnp.int32),
            shaped(2, *block_rows.shape, dtype=jnp.int32),
        ],
        [HBM] * 4,
        [pltpu.VMEM(sources.shape[1:], jnp.float32), pltpu.SemaphoreType.DMA((4,))],
        name="start",
    )(in_hbm(sources[0]), in_hbm(mirror_rows), in_hbm(block_rows), in_hbm(block_cols))
    chunks, blocks = lax.optimization_barrier((chunks, blocks))
    got = lax.all_to_all(chunks, AXES, 0, 0)
    other_blocks = swapped(blocks, 1)
    weights, pick = call(
        prepare_kernel,
        [
            shaped(blocks.shape[0] // 2, 2 * BLOCK, 2 * BLOCK, dtype=blocks.dtype),
            shaped(2 * ROWS * blocks.shape[0], owners * ROWS, dtype=jnp.bfloat16),
        ],
        [HBM, VMEM, SMEM, SMEM],
        [pltpu.VMEM(blocks.shape, blocks.dtype), pltpu.SemaphoreType.DMA],
        name="prepare",
    )(in_hbm(blocks), other_blocks, places, swapped(places, 1))
    near_args = (pick, weights)
    chunks, zero, coeff = call(
        functools.partial(first_kernel, total), [chunk, vector, tile], [VMEM] * 3, name="first"
    )(got, *near_args)
    got = exchanged(chunks)
    chunks, one, coeff = call(
        functools.partial(middle_kernel, total, shift), [chunk, vector, tile], [VMEM] * 5,
        name="middle",
    )(got, zero, coeff, *near_args)
    first_got, got = got, exchanged(chunks)
    chunks, two, coeff, same, flip = call(
        functools.partial(last_kernel, total, shift),
        [shaped(devices, BLOCK), vector, tile, tile, tile], [VMEM] * 7,
        name="last",
    )(first_got, got, zero, one, coeff, *near_args)
    got = lax.all_to_all(chunks.reshape(devices, 1, BLOCK), AXES, 0, 0)
    [theirs] = call(
        pack_kernel, [shaped(2 * ITERS + 2, ROWS, BLOCK)], [VMEM] * 5, name="pack"
    )(zero, one, two, coeff, flip)
    kept, known, gram = call(
        keep_kernel, [shaped(ITERS + 1, ROWS, panels), tile, tile], [VMEM] * 9, name="keep"
    )(
        zero, one, two, coeff, same, swapped(theirs, 1), swapped(same, devices // 2),
        swapped(flip, devices // 2 ^ 1), mirror_rows,
    )
    basis, hessenberg = call(
        functools.partial(final_kernel, total),
        [shaped(ITERS + 1, ROWS, panels), shaped(ITERS, ITERS + 1, ROWS)], [VMEM] * 4,
        name="final",
    )(got.reshape(devices, BLOCK), kept, known, gram)
    return basis[:, None], hessenberg.transpose(2, 1, 0)


def solution(mesh):
    placed = (
        P("side", None, ("grp", "dev")),
        P("side", ("grp", "dev"), None, None),
        P("side", ("grp", "dev")),
        P("side", ("grp", "dev")),
        P(("grp", "dev")),
    )
    return jax.shard_map(
        on_device,
        mesh=mesh,
        in_specs=placed,
        out_specs=(P(None, "side", None, ("grp", "dev")), P()),
        check_vma=False,
    )
```

```python
import functools

import jax
import jax.numpy as jnp
from jax import lax
from jax.experimental import pallas as pl
from jax.experimental.pallas import tpu as pltpu
from jax.sharding import PartitionSpec as P

BLOCK = 128
BLK_DEV = 2
ITERS = 3
ROWS = 8
HALF_RHS = 4
EPSILON = 1e-06
AXES = ("side", "grp", "dev")
VMEM_LIMIT = 48 * 2**20
LENGTH_LANE = ITERS * (ITERS + 1)
CROSSED = [(0, 1), (0, 2), (1, 2)]


def position():
    side = lax.axis_index("side")
    dev = lax.axis_index("dev")
    owner = lax.axis_index("grp") * lax.axis_size("dev") + dev
    return side, owner, lax.rem(dev, 2)


def iota(shape, axis):
    return lax.broadcasted_iota(jnp.int32, shape, axis)


def per_rhs(tile):
    column = jnp.sum(tile, axis=1, keepdims=True)
    return column + jnp.concatenate([column[HALF_RHS:], column[:HALF_RHS]], axis=0)


def dot(left, right):
    return per_rhs(jnp.sum(left * right, axis=0))


def columns(values):
    lane = iota((ROWS, BLOCK), 1)
    tile = jnp.zeros((ROWS, BLOCK), jnp.float32)
    for index, value in values.items():
        tile = jnp.where(lane == index, value, tile)
    return tile


def mirror_onehot(mirror_ref, block):
    return (iota((BLOCK, BLOCK), 0) == mirror_ref[block : block + 1, :]).astype(jnp.float32)


def exact_dot(left, right, dims):
    return lax.dot_general(
        left, right, (dims, ((), ())),
        precision=lax.Precision.HIGHEST, preferred_element_type=jnp.float32,
    )


def start_kernel(sources_hbm, mirror_hbm, rows_hbm, cols_hbm, chunk_ref, mirror_ref, places_ref,
                 sources_ref, sems):
    copies = [
        pltpu.make_async_copy(sources_hbm, sources_ref, sems.at[0]),
        pltpu.make_async_copy(mirror_hbm, mirror_ref, sems.at[1]),
        pltpu.make_async_copy(rows_hbm, places_ref.at[0], sems.at[2]),
        pltpu.make_async_copy(cols_hbm, places_ref.at[1], sems.at[3]),
    ]
    for copy in copies:
        copy.start()
    for copy in copies:
        copy.wait()
    side, _, _ = position()
    pieces = []
    for block in range(BLK_DEV):
        part = sources_ref[:, block * BLOCK : (block + 1) * BLOCK]
        places = jnp.broadcast_to(mirror_ref[block : block + 1, :], part.shape)
        moved = jnp.take_along_axis(part, places, axis=1, mode="promise_in_bounds")
        pieces.append(jnp.where(side == 0, part, moved))
    tiles = [
        jnp.concatenate([piece[HALF_RHS * c : HALF_RHS * (c + 1)] for piece in pieces], axis=0)
        for c in range(2)
    ]
    chips = chunk_ref.shape[0] // 2

    def store(chip, carry):
        chunk_ref[2 * chip] = tiles[0]
        chunk_ref[2 * chip + 1] = tiles[1]
        return carry

    lax.fori_loop(0, chips, store, 0, unroll=chips <= 32)


def prepare_kernel(own_hbm, other_ref, own_places, other_places, weights_ref, pick_ref, own_ref,
                   sem):
    copy = pltpu.make_async_copy(own_hbm, own_ref, sem)
    copy.start()
    width = pick_ref.shape[1]
    half_of_row = iota((ROWS, width), 0) // HALF_RHS
    rhs_of_row = iota((ROWS, width), 0) % HALF_RHS
    lane = iota((ROWS, width), 1)
    for entry in range(own_ref.shape[0]):
        picks = []
        for places in (own_places, other_places):
            place = jnp.where(
                half_of_row == places[0, 0, entry], HALF_RHS * places[1, 0, entry] + rhs_of_row, -1
            )
            picks.append((lane == place).astype(jnp.float32))
        first = 2 * ROWS * entry
        pick_ref[first : first + 2 * ROWS, :] = jnp.concatenate(picks, axis=0).astype(jnp.bfloat16)
    for side, ref in ((1, other_ref), (0, own_ref)):
        if side == 0:
            copy.wait()
        for entry in range(own_ref.shape[0]):
            first = entry % 2 * BLOCK
            weights_ref[
                entry // 2, first : first + BLOCK, side * BLOCK : (side + 1) * BLOCK
            ] = ref[entry].T


def near(half, pick_ref, weights_ref):
    flat = half.reshape(-1, BLOCK)
    coarse = flat.astype(jnp.bfloat16)
    fine = (flat - coarse.astype(jnp.float32)).astype(jnp.bfloat16)
    picked = lax.dot_general(
        pick_ref[...], jnp.concatenate([coarse, fine], axis=1), (((1,), (0,)), ((), ())),
        preferred_element_type=jnp.float32,
    ).astype(jnp.bfloat16)
    sums = [jnp.zeros((4 * ROWS, 2 * BLOCK), jnp.float32) for _ in range(2)]
    for group in range(weights_ref.shape[0]):
        rows = [
            slice(2 * ROWS * place, 2 * ROWS * (place + 1)) for place in (2 * group, 2 * group + 1)
        ]
        left = jnp.concatenate(
            [
                jnp.concatenate([picked[rows[0], part], picked[rows[1], part]], axis=1)
                for part in (slice(0, BLOCK), slice(BLOCK, 2 * BLOCK))
            ],
            axis=0,
        )
        sums[group % 2] += lax.dot_general(
            left, weights_ref[group], (((1,), (0,)), ((), ())), preferred_element_type=jnp.float32
        )
    total = sums[0] + sums[1]
    total = total[: 2 * ROWS] + total[2 * ROWS :]
    _, _, core = position()
    own = total[:ROWS, :BLOCK]
    other = total[ROWS:, BLOCK:]
    return jnp.where(core == 0, own, other), jnp.where(core == 0, other, own)


def spread(chunk_ref, low, high):
    chips = chunk_ref.shape[0]

    def store(chip, carry):
        chunk_ref[chip, 0] = low
        chunk_ref[chip, 1] = high
        return carry

    lax.fori_loop(0, chips, store, 0, unroll=chips <= 32)


def first_kernel(total, got_ref, pick_ref, weights_ref, chunk_ref, basis_ref, coeff_ref):
    side, _, _ = position()
    owners = got_ref.shape[0] // 2
    port = got_ref[:owners]
    star = got_ref[owners:]
    sym = port + star
    anti = port - star
    tiles = near(jnp.where(side == 0, sym, anti), pick_ref, weights_ref)
    squares = per_rhs(jnp.sum(port * port + star * star, axis=0)) * (1.0 / total) + EPSILON
    scale = lax.rsqrt(squares)
    coeff_ref[...] = columns({LENGTH_LANE: jnp.sqrt(squares)})
    basis_ref[:owners] = sym * scale
    basis_ref[owners:] = anti * scale
    spread(chunk_ref, *[tile * scale for tile in tiles])


def in_order(got_ref, shift):
    chips = got_ref.shape[0]
    return jnp.concatenate([got_ref[chips - shift :], got_ref[: chips - shift]], axis=0)


def own_tiles(got_ref, shift):
    side, owner, _ = position()
    chips = got_ref.shape[0]
    chip = lax.rem(side * (chips // 2) + owner // 2 + chips - shift, chips)
    return got_ref[chip, 0], got_ref[chip, 1]


def advanced(total, shift, got_refs, basis_refs, overlaps, pick_ref, weights_ref):
    side, _, _ = position()
    got = in_order(got_refs[-1], shift)
    half = got.shape[0] // 2
    tiles = near(jnp.where(side == 0, got[:half], got[half:]), pick_ref, weights_ref)
    got = got.reshape(basis_refs[0].shape)
    inner = 0.5 / total
    multiples = [
        dot(got, ref[...]) * inner + 0.5 * overlap for ref, overlap in zip(basis_refs, overlaps)
    ]
    rest = got
    for multiple, ref in zip(multiples, basis_refs):
        rest = rest - multiple * ref[...]
    squares = dot(rest, rest) * inner + EPSILON
    scale = lax.rsqrt(squares)
    owned = [own_tiles(ref, shift) for ref in got_refs]
    parts = []
    for place, value in enumerate(tiles):
        for multiple, earlier in zip(multiples, owned):
            value = value - multiple * earlier[place]
        parts.append(value * scale)
    coeffs = multiples[:-1] + [multiples[-1] + 0.5, jnp.sqrt(squares)]
    return coeffs, rest * scale, parts


def middle_kernel(total, shift, got_ref, basis_ref, known_ref, pick_ref, weights_ref,
                  chunk_ref, next_ref, coeff_ref):
    known = known_ref[...]
    length = known[:, LENGTH_LANE : LENGTH_LANE + 1]
    coeffs, next_ref[...], parts = advanced(
        total, shift, [got_ref], [basis_ref], [-EPSILON / (length * length)], pick_ref, weights_ref
    )
    coeff_ref[...] = columns(dict(enumerate(coeffs))) + known
    spread(chunk_ref, *parts)


def last_kernel(total, shift, first_got_ref, got_ref, zero_ref, one_ref, known_ref, pick_ref,
                weights_ref, chunk_ref, two_ref, coeff_ref, same_ref, flip_ref):
    side, owner, core = position()
    owners = two_ref.shape[0] // 2
    refs = [zero_ref, one_ref, two_ref]
    known = known_ref[...]
    length = known[:, LENGTH_LANE : LENGTH_LANE + 1]
    coeff, norm = known[:, 0:1], known[:, 1:2]
    overlaps = [coeff * EPSILON / (length * length * norm), -EPSILON / (norm * norm)]
    coeffs, two_ref[...], tiles = advanced(
        total, shift, [first_got_ref, got_ref], refs[:2], overlaps, pick_ref, weights_ref
    )
    base = side * owners + owner - core
    rhs = iota((ROWS, BLOCK), 0)
    lane = iota((ROWS, BLOCK), 1)
    spots = jnp.zeros((ROWS, BLOCK), jnp.float32)
    for index in range(ITERS + 1):
        if index < ITERS:
            product = tiles[0] * refs[index][base] + tiles[1] * refs[index][base + 1]
        else:
            product = tiles[0] * tiles[0] + tiles[1] * tiles[1]
        column = jnp.sum(product, axis=1, keepdims=True)
        spots = jnp.where(lane == ROWS * index + rhs, column, spots)
    row = jnp.sum(spots, axis=0, keepdims=True)
    chunk_ref[...] = jnp.broadcast_to(row, chunk_ref.shape)
    coeffs = columns({place + ITERS + 1: value for place, value in enumerate(coeffs)})
    coeff_ref[...] = coeffs + known
    same_ref[...] = jnp.where(core == 0, tiles[0], tiles[1])
    flip_ref[...] = jnp.where(core == 0, tiles[1], tiles[0])


def early_kernel(zero_ref, one_ref, theirs_ref):
    _, owner, core = position()
    owners = zero_ref.shape[0] // 2
    for index, ref in enumerate((zero_ref, one_ref)):
        for half in range(2):
            theirs_ref[2 * index + half] = ref[half * owners + owner + 1 - 2 * core]


def pack_kernel(two_ref, coeff_ref, flip_ref, theirs_ref):
    _, owner, core = position()
    owners = two_ref.shape[0] // 2
    for half in range(2):
        theirs_ref[half] = two_ref[half * owners + owner + 1 - 2 * core]
    theirs_ref[2] = flip_ref[...]
    theirs_ref[3] = coeff_ref[...]


def keep_kernel(zero_ref, one_ref, two_ref, coeff_ref, same_ref, early_ref, theirs_ref, across_ref,
                flipped_ref, mirror_ref, kept_ref, known_ref, gram_ref):
    side, owner, core = position()
    owners = zero_ref.shape[0] // 2

    def by_core(mine, theirs):
        return [jnp.where(core == 0, mine, theirs), jnp.where(core == 0, theirs, mine)]

    pairs = []
    for index, ref in enumerate((zero_ref, one_ref, two_ref)):
        pairs.append(
            [
                by_core(
                    ref[half * owners + owner],
                    early_ref[2 * index + half] if index < 2 else theirs_ref[half],
                )
                for half in range(2)
            ]
        )
    here = by_core(same_ref[...], theirs_ref[2])
    there = by_core(across_ref[...], flipped_ref[...])
    pairs.append(
        [
            [jnp.where(side == 0, h, t) for h, t in zip(here, there)],
            [jnp.where(side == 0, t, h) for h, t in zip(here, there)],
        ]
    )
    known = by_core(coeff_ref[...], theirs_ref[3])
    known = jnp.concatenate([tile[:HALF_RHS] for tile in known], axis=0)
    known_ref[...] = jnp.where(iota((ROWS, BLOCK), 1) < LENGTH_LANE, known, 0.0)

    def entry(j, k):
        place = k * (ITERS + 1) + j
        return known[:, place : place + 1]

    norms = [known[:, LENGTH_LANE : LENGTH_LANE + 1], entry(1, 0), entry(2, 1)]
    short = [EPSILON / (norm * norm) for norm in norms]
    zero_one = entry(0, 0) * short[0] / norms[1]
    zero_two = (entry(0, 1) * short[0] - entry(1, 1) * zero_one) / norms[2]
    one_two = (entry(1, 1) * short[1] - entry(0, 1) * zero_one) / norms[2]
    gram_ref[...] = columns(dict(enumerate(short + [zero_one, zero_two, one_two])))
    for block in range(BLK_DEV):
        rows = slice(block * HALF_RHS, (block + 1) * HALF_RHS)
        ports, stars = [], []
        for sym, anti in pairs:
            sym = jnp.concatenate([tile[rows] for tile in sym], axis=0)
            anti = jnp.concatenate([tile[rows] for tile in anti], axis=0)
            ports.append(0.5 * (sym + anti))
            stars.append(0.5 * (sym - anti))
        back = exact_dot(
            jnp.concatenate(stars, axis=0), mirror_onehot(mirror_ref, block), ((1,), (1,))
        )
        for index, port in enumerate(ports):
            kept_ref[index, :, block * BLOCK : (block + 1) * BLOCK] = jnp.where(
                side == 0, port, back[index * ROWS : (index + 1) * ROWS]
            )


def final_kernel(total, got_ref, kept_ref, known_ref, gram_ref, basis_ref, hessenberg_ref):
    inner = 0.5 / total
    sums = jnp.sum(got_ref[...].reshape(-1, ROWS, BLOCK), axis=0)
    even = iota((ROWS, BLOCK), 0) % 2 == 0
    lower = jnp.sum(jnp.where(even, sums, 0.0), axis=0, keepdims=True)
    upper = jnp.sum(jnp.where(even, 0.0, sums), axis=0, keepdims=True)
    rhs = iota((ROWS, BLOCK), 0)
    lane = iota((ROWS, BLOCK), 1)
    spots = jnp.where(rhs < HALF_RHS, lower, upper) * inner
    values = [
        jnp.sum(
            jnp.where((lane // ROWS == index) & (lane % HALF_RHS == rhs % HALF_RHS), spots, 0.0),
            axis=1,
            keepdims=True,
        )
        for index in range(ITERS + 1)
    ]
    dots = values[:ITERS]
    short = [gram_ref[:, j : j + 1] for j in range(ITERS)]
    crossed = dict(
        zip(CROSSED, [gram_ref[:, ITERS + j : ITERS + j + 1] for j in range(len(CROSSED))])
    )
    multiples = [
        dots[0] + 0.5 * crossed[0, 2], dots[1] + 0.5 * crossed[1, 2], dots[2] - 0.5 * short[2]
    ]
    squares = values[ITERS]
    for j in range(ITERS):
        squares = squares - multiples[j] * (2.0 * dots[j] - multiples[j] * (1.0 - short[j]))
    for (i, j), value in crossed.items():
        squares = squares + 2.0 * multiples[i] * multiples[j] * value
    squares = jnp.maximum(squares, 0.0) + EPSILON
    norm = jnp.sqrt(squares)
    rest = kept_ref[ITERS]
    for j in range(ITERS):
        rest = rest - multiples[j] * kept_ref[j]
    basis_ref[:ITERS] = kept_ref[:ITERS]
    basis_ref[ITERS] = rest * lax.rsqrt(squares)
    coeffs = multiples[:-1] + [multiples[-1] + 0.5]
    place = 2 * (ITERS + 1)
    whole = known_ref[...] + columns(
        {place + index: value for index, value in enumerate(coeffs + [norm])}
    )
    turned = whole.T
    for k in range(ITERS):
        hessenberg_ref[k] = turned[k * (ITERS + 1) : (k + 1) * (ITERS + 1), :]


VMEM = pl.BlockSpec(memory_space=pltpu.VMEM)
SMEM = pl.BlockSpec(memory_space=pltpu.SMEM)
HBM = pl.BlockSpec(memory_space=pltpu.HBM)


def shaped(*shape, dtype=jnp.float32):
    return jax.ShapeDtypeStruct(shape, dtype)


def in_hbm(value):
    return pltpu.with_memory_space_constraint(value, pltpu.HBM)


def call(kernel, outs, specs, scratch=(), name=None):
    return pl.pallas_call(
        kernel,
        out_shape=outs,
        in_specs=specs,
        out_specs=[VMEM] * len(outs),
        scratch_shapes=scratch,
        compiler_params=pltpu.CompilerParams(vmem_limit_bytes=VMEM_LIMIT),
        name=name,
    )


def on_device(sources, near_blocks, block_rows, block_cols, mirror):
    devices = lax.axis_size(AXES)
    owners = devices // 2
    chips = devices // 2
    panels = sources.shape[2]
    total = 1.0 * panels * devices
    shift = 1
    same_core = [
        [(2 * (chip + shift) + core) % devices for chip in range(chips)] for core in range(2)
    ]
    mirror_rows = mirror.reshape(BLK_DEV, BLOCK)
    blocks = near_blocks[0]
    vector = shaped(devices, ROWS, BLOCK)
    chunk = shaped(chips, 2, ROWS, BLOCK)
    tile = shaped(ROWS, BLOCK)

    def swapped(value, bits):
        return lax.ppermute(value, AXES, [(i, i ^ bits) for i in range(devices)])

    def exchanged(chunks):
        return lax.all_to_all(chunks, AXES, 0, 0, axis_index_groups=same_core)

    chunks, mirror_rows, places = call(
        start_kernel,
        [
            vector,
            shaped(*mirror_rows.shape, dtype=jnp.int32),
            shaped(2, *block_rows.shape, dtype=jnp.int32),
        ],
        [HBM] * 4,
        [pltpu.VMEM(sources.shape[1:], jnp.float32), pltpu.SemaphoreType.DMA((4,))],
        name="start",
    )(in_hbm(sources[0]), in_hbm(mirror_rows), in_hbm(block_rows), in_hbm(block_cols))
    chunks, blocks = lax.optimization_barrier((chunks, blocks))
    got = lax.all_to_all(chunks, AXES, 0, 0)
    other_blocks = swapped(blocks, 1)
    weights, pick = call(
        prepare_kernel,
        [
            shaped(blocks.shape[0] // 2, 2 * BLOCK, 2 * BLOCK, dtype=blocks.dtype),
            shaped(2 * ROWS * blocks.shape[0], owners * ROWS, dtype=jnp.bfloat16),
        ],
        [HBM, VMEM, SMEM, SMEM],
        [pltpu.VMEM(blocks.shape, blocks.dtype), pltpu.SemaphoreType.DMA],
        name="prepare",
    )(in_hbm(blocks), other_blocks, places, swapped(places, 1))
    near_args = (pick, weights)
    chunks, zero, coeff = call(
        functools.partial(first_kernel, total), [chunk, vector, tile], [VMEM] * 3, name="first"
    )(got, *near_args)
    got = exchanged(chunks)
    chunks, one, coeff = call(
        functools.partial(middle_kernel, total, shift), [chunk, vector, tile], [VMEM] * 5,
        name="middle",
    )(got, zero, coeff, *near_args)
    [early] = call(early_kernel, [shaped(4, ROWS, BLOCK)], [VMEM] * 2, name="early")(zero, one)
    early = swapped(early, 1)
    first_got, got = got, exchanged(chunks)
    chunks, two, coeff, same, flip = call(
        functools.partial(last_kernel, total, shift),
        [shaped(devices, BLOCK), vector, tile, tile, tile], [VMEM] * 7,
        name="last",
    )(first_got, got, zero, one, coeff, *near_args)
    got = lax.all_to_all(chunks.reshape(devices, 1, BLOCK), AXES, 0, 0)
    [theirs] = call(pack_kernel, [shaped(4, ROWS, BLOCK)], [VMEM] * 3, name="pack")(
        two, coeff, flip
    )
    kept, known, gram = call(
        keep_kernel, [shaped(ITERS + 1, ROWS, panels), tile, tile], [VMEM] * 10, name="keep"
    )(
        zero, one, two, coeff, same, early, swapped(theirs, 1), swapped(same, devices // 2),
        swapped(flip, devices // 2 ^ 1), mirror_rows,
    )
    basis, hessenberg = call(
        functools.partial(final_kernel, total),
        [shaped(ITERS + 1, ROWS, panels), shaped(ITERS, ITERS + 1, ROWS)], [VMEM] * 4,
        name="final",
    )(got.reshape(devices, BLOCK), kept, known, gram)
    return basis[:, None], hessenberg.transpose(2, 1, 0)


def solution(mesh):
    placed = (
        P("side", None, ("grp", "dev")),
        P("side", ("grp", "dev"), None, None),
        P("side", ("grp", "dev")),
        P("side", ("grp", "dev")),
        P(("grp", "dev")),
    )
    return jax.shard_map(
        on_device,
        mesh=mesh,
        in_specs=placed,
        out_specs=(P(None, "side", None, ("grp", "dev")), P()),
        check_vma=False,
    )
```

```python
import functools

import jax
import jax.numpy as jnp
from jax import lax
from jax.experimental import pallas as pl
from jax.experimental.pallas import tpu as pltpu
from jax.sharding import PartitionSpec as P

BLOCK = 128
BLK_DEV = 2
ITERS = 3
ROWS = 8
HALF_RHS = 4
EPSILON = 1e-06
AXES = ("side", "grp", "dev")
VMEM_LIMIT = 48 * 2**20
LENGTH_LANE = ITERS * (ITERS + 1)
START_LANE = LENGTH_LANE + 1
PACKED = ITERS + 2
TINY = 1e-30


def position():
    side = lax.axis_index("side")
    dev = lax.axis_index("dev")
    owner = lax.axis_index("grp") * lax.axis_size("dev") + dev
    return side, owner, lax.rem(dev, 2)


def iota(shape, axis):
    return lax.broadcasted_iota(jnp.int32, shape, axis)


def per_rhs(tile):
    column = jnp.sum(tile, axis=1, keepdims=True)
    return column + jnp.concatenate([column[HALF_RHS:], column[:HALF_RHS]], axis=0)


def dot(left, right):
    return per_rhs(jnp.sum(left * right, axis=0))


def columns(values):
    lane = iota((ROWS, BLOCK), 1)
    tile = jnp.zeros((ROWS, BLOCK), jnp.float32)
    for index, value in values.items():
        tile = jnp.where(lane == index, value, tile)
    return tile


def mirror_onehot(mirror_ref, block):
    return (iota((BLOCK, BLOCK), 0) == mirror_ref[block : block + 1, :]).astype(jnp.float32)


def exact_dot(left, right, dims):
    return lax.dot_general(
        left, right, (dims, ((), ())),
        precision=lax.Precision.HIGHEST, preferred_element_type=jnp.float32,
    )


def start_kernel(sources_hbm, mirror_hbm, rows_hbm, cols_hbm, chunk_ref, mirror_ref, places_ref,
                 sources_ref, sems):
    copies = [
        pltpu.make_async_copy(sources_hbm, sources_ref, sems.at[0]),
        pltpu.make_async_copy(mirror_hbm, mirror_ref, sems.at[1]),
        pltpu.make_async_copy(rows_hbm, places_ref.at[0], sems.at[2]),
        pltpu.make_async_copy(cols_hbm, places_ref.at[1], sems.at[3]),
    ]
    for copy in copies:
        copy.start()
    for copy in copies:
        copy.wait()
    side, _, _ = position()
    pieces = []
    for block in range(BLK_DEV):
        part = sources_ref[:, block * BLOCK : (block + 1) * BLOCK]
        places = jnp.broadcast_to(mirror_ref[block : block + 1, :], part.shape)
        moved = jnp.take_along_axis(part, places, axis=1, mode="promise_in_bounds")
        pieces.append(jnp.where(side == 0, part, moved))
    tiles = [
        jnp.concatenate([piece[HALF_RHS * c : HALF_RHS * (c + 1)] for piece in pieces], axis=0)
        for c in range(2)
    ]
    chips = chunk_ref.shape[0] // 2

    def store(chip, carry):
        chunk_ref[2 * chip] = tiles[0]
        chunk_ref[2 * chip + 1] = tiles[1]
        return carry

    lax.fori_loop(0, chips, store, 0, unroll=chips <= 32)


def prepare_kernel(own_hbm, other_ref, own_places, other_places, weights_ref, pick_ref, own_ref,
                   sem):
    copy = pltpu.make_async_copy(own_hbm, own_ref, sem)
    copy.start()
    width = pick_ref.shape[1]
    half_of_row = iota((ROWS, width), 0) // HALF_RHS
    rhs_of_row = iota((ROWS, width), 0) % HALF_RHS
    lane = iota((ROWS, width), 1)
    for entry in range(own_ref.shape[0]):
        picks = []
        for places in (own_places, other_places):
            place = jnp.where(
                half_of_row == places[0, 0, entry], HALF_RHS * places[1, 0, entry] + rhs_of_row, -1
            )
            picks.append((lane == place).astype(jnp.float32))
        first = 2 * ROWS * entry
        pick_ref[first : first + 2 * ROWS, :] = jnp.concatenate(picks, axis=0).astype(jnp.bfloat16)
    for side, ref in ((1, other_ref), (0, own_ref)):
        if side == 0:
            copy.wait()
        for entry in range(own_ref.shape[0]):
            first = entry % 2 * BLOCK
            weights_ref[
                entry // 2, first : first + BLOCK, side * BLOCK : (side + 1) * BLOCK
            ] = ref[entry].T


def near(half, pick_ref, weights_ref):
    flat = half.reshape(-1, BLOCK)
    coarse = flat.astype(jnp.bfloat16)
    fine = (flat - coarse.astype(jnp.float32)).astype(jnp.bfloat16)
    picked = lax.dot_general(
        pick_ref[...], jnp.concatenate([coarse, fine], axis=1), (((1,), (0,)), ((), ())),
        preferred_element_type=jnp.float32,
    ).astype(jnp.bfloat16)
    sums = [jnp.zeros((4 * ROWS, 2 * BLOCK), jnp.float32) for _ in range(2)]
    for group in range(weights_ref.shape[0]):
        rows = [
            slice(2 * ROWS * place, 2 * ROWS * (place + 1)) for place in (2 * group, 2 * group + 1)
        ]
        left = jnp.concatenate(
            [
                jnp.concatenate([picked[rows[0], part], picked[rows[1], part]], axis=1)
                for part in (slice(0, BLOCK), slice(BLOCK, 2 * BLOCK))
            ],
            axis=0,
        )
        sums[group % 2] += lax.dot_general(
            left, weights_ref[group], (((1,), (0,)), ((), ())), preferred_element_type=jnp.float32
        )
    total = sums[0] + sums[1]
    total = total[: 2 * ROWS] + total[2 * ROWS :]
    _, _, core = position()
    own = total[:ROWS, :BLOCK]
    other = total[ROWS:, BLOCK:]
    return jnp.where(core == 0, own, other), jnp.where(core == 0, other, own)


def spread(chunk_ref, low, high):
    chips = chunk_ref.shape[0]

    def store(chip, carry):
        chunk_ref[chip, 0] = low
        chunk_ref[chip, 1] = high
        return carry

    lax.fori_loop(0, chips, store, 0, unroll=chips <= 32)


def first_kernel(total, got_ref, pick_ref, weights_ref, chunk_ref, basis_ref, coeff_ref):
    side, _, _ = position()
    owners = got_ref.shape[0] // 2
    port = got_ref[:owners]
    star = got_ref[owners:]
    half = jnp.where(side == 0, port + star, port - star)
    tiles = near(half, pick_ref, weights_ref)
    squares = per_rhs(jnp.sum(port * port + star * star, axis=0)) * (1.0 / total) + EPSILON
    own = dot(half, half) * (0.5 / total)
    scale = lax.rsqrt(jnp.maximum(own, TINY))
    coeff_ref[...] = columns(
        {LENGTH_LANE: jnp.sqrt(squares), START_LANE: jnp.sqrt(own) * lax.rsqrt(squares)}
    )
    basis_ref[...] = half * scale
    spread(chunk_ref, *[tile * scale for tile in tiles])


def in_order(got_ref, shift):
    chips = got_ref.shape[0]
    return jnp.concatenate([got_ref[chips - shift :], got_ref[: chips - shift]], axis=0)


def own_tiles(got_ref, shift):
    _, owner, _ = position()
    chips = got_ref.shape[0]
    chip = lax.rem(owner // 2 + chips - shift, chips)
    return got_ref[chip, 0], got_ref[chip, 1]


def advanced(total, shift, got_refs, basis_refs, pick_ref, weights_ref):
    got = in_order(got_refs[-1], shift).reshape(basis_refs[0].shape)
    tiles = near(got, pick_ref, weights_ref)
    inner = 0.5 / total
    coeffs = [dot(got, ref[...]) * inner for ref in basis_refs]
    rest = got
    for coeff, ref in zip(coeffs, basis_refs):
        rest = rest - coeff * ref[...]
    squares = dot(rest, rest) * inner
    scale = lax.rsqrt(jnp.maximum(squares, TINY))
    owned = [own_tiles(ref, shift) for ref in got_refs]
    parts = []
    for place, value in enumerate(tiles):
        for coeff, earlier in zip(coeffs, owned):
            value = value - coeff * earlier[place]
        parts.append(value * scale)
    return coeffs + [jnp.sqrt(squares)], rest * scale, parts


def middle_kernel(total, shift, got_ref, basis_ref, known_ref, pick_ref, weights_ref,
                  chunk_ref, next_ref, coeff_ref):
    coeffs, next_ref[...], parts = advanced(
        total, shift, [got_ref], [basis_ref], pick_ref, weights_ref
    )
    coeff_ref[...] = columns(dict(enumerate(coeffs))) + known_ref[...]
    spread(chunk_ref, *parts)


def last_kernel(total, shift, first_got_ref, got_ref, zero_ref, one_ref, known_ref, pick_ref,
                weights_ref, chunk_ref, two_ref, coeff_ref, low_ref, high_ref):
    _, owner, core = position()
    refs = [zero_ref, one_ref, two_ref]
    coeffs, two_ref[...], tiles = advanced(
        total, shift, [first_got_ref, got_ref], refs[:2], pick_ref, weights_ref
    )
    base = owner - core
    rhs = iota((ROWS, BLOCK), 0)
    lane = iota((ROWS, BLOCK), 1)
    spots = jnp.zeros((ROWS, BLOCK), jnp.float32)
    for index in range(ITERS + 1):
        if index < ITERS:
            product = tiles[0] * refs[index][base] + tiles[1] * refs[index][base + 1]
        else:
            product = tiles[0] * tiles[0] + tiles[1] * tiles[1]
        column = jnp.sum(product, axis=1, keepdims=True)
        spots = jnp.where(lane == ROWS * index + rhs, column, spots)
    row = jnp.sum(spots, axis=0, keepdims=True)
    chunk_ref[...] = jnp.broadcast_to(row, chunk_ref.shape)
    coeffs = columns({place + ITERS + 1: value for place, value in enumerate(coeffs)})
    coeff_ref[...] = coeffs + known_ref[...]
    low_ref[...] = tiles[0]
    high_ref[...] = tiles[1]


def pack_kernel(zero_ref, one_ref, two_ref, coeff_ref, low_ref, high_ref, mine_ref, theirs_ref):
    _, owner, core = position()
    for out_ref, which in ((mine_ref, core), (theirs_ref, 1 - core)):
        for index, ref in enumerate((zero_ref, one_ref, two_ref)):
            out_ref[index] = ref[owner - core + which]
        out_ref[ITERS] = jnp.where(which == 0, low_ref[...], high_ref[...])
        out_ref[ITERS + 1] = coeff_ref[...]


def over_halves(products):
    return sum(one * other for one, other in products)


def keep_kernel(mine_ref, partner_ref, across_ref, flipped_ref, mirror_ref, kept_ref, known_ref,
                terms_ref):
    side, _, core = position()
    packed = []
    for index in range(PACKED):
        mine, partner = mine_ref[index], partner_ref[index]
        across, flipped = across_ref[index], flipped_ref[index]
        here = [jnp.where(core == 0, mine, partner), jnp.where(core == 0, partner, mine)]
        there = [jnp.where(core == 0, across, flipped), jnp.where(core == 0, flipped, across)]
        packed.append(
            [
                [jnp.where(side == 0, h, t) for h, t in zip(here, there)],
                [jnp.where(side == 0, t, h) for h, t in zip(here, there)],
            ]
        )
    known = [
        jnp.concatenate([tile[:HALF_RHS] for tile in packed[ITERS + 1][half]], axis=0)
        for half in range(2)
    ]

    def entry(half, j, k):
        place = k * (ITERS + 1) + j
        return known[half][:, place : place + 1]

    halves = range(2)
    length = known[0][:, LENGTH_LANE : LENGTH_LANE + 1]
    start = [known[half][:, START_LANE : START_LANE + 1] for half in halves]
    zero = [[start[half]] for half in halves]
    ahead = [[entry(half, 0, 0) * zero[half][0], entry(half, 1, 0) * zero[half][0]] for half in halves]
    short = [EPSILON / (length * length)]
    multiple = over_halves([(ahead[half][0], zero[half][0]) for half in halves]) - 0.5 * short[0]
    rest = [[ahead[half][0] - multiple * zero[half][0], ahead[half][1]] for half in halves]
    squares = over_halves([(value, value) for half in halves for value in rest[half]]) + EPSILON
    norms = [jnp.sqrt(squares)]
    one = [[value * lax.rsqrt(squares) for value in rest[half]] for half in halves]
    heads = {(0, 0): multiple + 0.5, (1, 0): norms[0]}
    short.append(EPSILON / squares)
    cross = heads[0, 0] * short[0] / norms[0]
    ahead = [
        [
            entry(half, 0, 0) * one[half][0] + entry(half, 0, 1) * one[half][1],
            entry(half, 1, 0) * one[half][0] + entry(half, 1, 1) * one[half][1],
            entry(half, 2, 1) * one[half][1],
        ]
        for half in halves
    ]
    multiples = [
        over_halves([(ahead[half][0], zero[half][0]) for half in halves]) + 0.5 * cross,
        over_halves([pair for half in halves for pair in zip(ahead[half], one[half])])
        - 0.5 * short[1],
    ]
    rest = [
        [
            ahead[half][0] - multiples[0] * zero[half][0] - multiples[1] * one[half][0],
            ahead[half][1] - multiples[1] * one[half][1],
            ahead[half][2],
        ]
        for half in halves
    ]
    squares = over_halves([(value, value) for half in halves for value in rest[half]]) + EPSILON
    norms.append(jnp.sqrt(squares))
    two = [[value * lax.rsqrt(squares) for value in rest[half]] for half in halves]
    heads.update({(0, 1): multiples[0], (1, 1): multiples[1] + 0.5, (2, 1): norms[1]})
    short.append(EPSILON / squares)
    crosses = [
        (heads[0, 1] * short[0] - heads[1, 1] * cross) / norms[1],
        (heads[1, 1] * short[1] - heads[0, 1] * cross) / norms[1],
    ]
    ahead = [
        [
            entry(half, 0, 0) * two[half][0] + entry(half, 0, 1) * two[half][1],
            entry(half, 1, 0) * two[half][0] + entry(half, 1, 1) * two[half][1],
            entry(half, 2, 1) * two[half][1],
        ]
        for half in halves
    ]
    known_ref[...] = columns({k * (ITERS + 1) + j: value for (j, k), value in heads.items()})
    terms = [0.5 * crosses[0], 0.5 * crosses[1], -0.5 * short[2]]
    for half in halves:
        terms += zero[half] + one[half] + two[half] + ahead[half]
    for index, value in enumerate(terms):
        terms_ref[index] = jnp.broadcast_to(value, (ROWS, BLOCK))
    for block in range(BLK_DEV):
        rows = slice(block * HALF_RHS, (block + 1) * HALF_RHS)
        vectors = []
        for half in halves:
            parts = [
                jnp.concatenate([tile[rows] for tile in packed[index][half]], axis=0)
                for index in range(ITERS + 1)
            ]
            vectors.append(
                [
                    over_halves(zip(weights, parts))
                    for weights in (
                        zero[half], one[half], two[half], ahead[half] + [two[half][2]]
                    )
                ]
            )
        ports = [0.5 * (sym + anti) for sym, anti in zip(*vectors)]
        stars = [0.5 * (sym - anti) for sym, anti in zip(*vectors)]
        back = exact_dot(
            jnp.concatenate(stars, axis=0), mirror_onehot(mirror_ref, block), ((1,), (1,))
        )
        for index, port in enumerate(ports):
            kept_ref[index, :, block * BLOCK : (block + 1) * BLOCK] = jnp.where(
                side == 0, port, back[index * ROWS : (index + 1) * ROWS]
            )


TERMS = 3 + 2 * 9


def final_kernel(total, got_ref, kept_ref, known_ref, terms_ref, basis_ref, hessenberg_ref):
    inner = 0.5 / total
    got = got_ref[...]
    devices = got.shape[0]
    even = iota((ROWS, BLOCK), 0) % 2 == 0
    rhs = iota((ROWS, BLOCK), 0)
    lane = iota((ROWS, BLOCK), 1)
    halves = range(2)
    values = []
    for half in halves:
        rows = got[half * devices // 2 : (half + 1) * devices // 2]
        sums = jnp.sum(rows.reshape(-1, ROWS, BLOCK), axis=0)
        lower = jnp.sum(jnp.where(even, sums, 0.0), axis=0, keepdims=True)
        upper = jnp.sum(jnp.where(even, 0.0, sums), axis=0, keepdims=True)
        spots = jnp.where(rhs < HALF_RHS, lower, upper) * inner
        values.append(
            [
                jnp.sum(
                    jnp.where(
                        (lane // ROWS == index) & (lane % HALF_RHS == rhs % HALF_RHS), spots, 0.0
                    ),
                    axis=1,
                    keepdims=True,
                )
                for index in range(ITERS + 1)
            ]
        )
    terms = [terms_ref[index] for index in range(TERMS)]
    zero, one, two, ahead = [], [], [], []
    for half in halves:
        own = terms[3 + 9 * half : 12 + 9 * half]
        zero.append(own[0:1])
        one.append(own[1:3])
        two.append(own[3:6])
        ahead.append(
            [known + own[5] * value for known, value in zip(own[6:9], values[half][:ITERS])]
        )
    multiples = [
        over_halves([pair for half in halves for pair in zip(ahead[half], vector[half])]) + term
        for vector, term in zip((zero, one, two), terms[:3])
    ]
    squares = jnp.full((ROWS, BLOCK), EPSILON, jnp.float32)
    for half in halves:
        beyond = values[half][ITERS]
        for value in values[half][:ITERS]:
            beyond = beyond - value * value
        squares = squares + jnp.maximum(beyond, 0.0) * two[half][2] * two[half][2]
        for index in range(ITERS):
            value = ahead[half][index]
            for multiple, vector in zip(multiples, (zero, one, two)):
                if index < len(vector[half]):
                    value = value - multiple * vector[half][index]
            squares = squares + value * value
    scale = lax.rsqrt(squares)
    basis_ref[:ITERS] = kept_ref[:ITERS]
    for block in range(BLK_DEV):
        span = slice(block * BLOCK, (block + 1) * BLOCK)
        rest = kept_ref[ITERS, :, span]
        for j in range(ITERS):
            rest = rest - multiples[j] * kept_ref[j, :, span]
        basis_ref[ITERS, :, span] = rest * scale
    place = 2 * (ITERS + 1)
    coeffs = multiples[:-1] + [multiples[-1] + 0.5, jnp.sqrt(squares)]
    whole = known_ref[...] + columns({place + index: value for index, value in enumerate(coeffs)})
    turned = whole.T
    for k in range(ITERS):
        hessenberg_ref[k] = turned[k * (ITERS + 1) : (k + 1) * (ITERS + 1), :]


VMEM = pl.BlockSpec(memory_space=pltpu.VMEM)
SMEM = pl.BlockSpec(memory_space=pltpu.SMEM)
HBM = pl.BlockSpec(memory_space=pltpu.HBM)


def shaped(*shape, dtype=jnp.float32):
    return jax.ShapeDtypeStruct(shape, dtype)


def in_hbm(value):
    return pltpu.with_memory_space_constraint(value, pltpu.HBM)


def call(kernel, outs, specs, scratch=(), name=None):
    return pl.pallas_call(
        kernel,
        out_shape=outs,
        in_specs=specs,
        out_specs=[VMEM] * len(outs),
        scratch_shapes=scratch,
        compiler_params=pltpu.CompilerParams(vmem_limit_bytes=VMEM_LIMIT),
        name=name,
    )


def on_device(sources, near_blocks, block_rows, block_cols, mirror):
    devices = lax.axis_size(AXES)
    owners = devices // 2
    chips = devices // 2
    panels = sources.shape[2]
    total = 1.0 * panels * devices
    shift = 5 % (chips // 2)
    groups = [
        [
            2 * (side * (chips // 2) + (chip + shift) % (chips // 2)) + core
            for chip in range(chips // 2)
        ]
        for side in range(2)
        for core in range(2)
    ]
    mirror_rows = mirror.reshape(BLK_DEV, BLOCK)
    blocks = near_blocks[0]
    everything = shaped(devices, ROWS, BLOCK)
    vector = shaped(owners, ROWS, BLOCK)
    chunk = shaped(chips // 2, 2, ROWS, BLOCK)
    tile = shaped(ROWS, BLOCK)

    def swapped(value, bits):
        return lax.ppermute(value, AXES, [(i, i ^ bits) for i in range(devices)])

    def exchanged(chunks):
        return lax.all_to_all(chunks, AXES, 0, 0, axis_index_groups=groups)

    chunks, mirror_rows, places = call(
        start_kernel,
        [
            everything,
            shaped(*mirror_rows.shape, dtype=jnp.int32),
            shaped(2, *block_rows.shape, dtype=jnp.int32),
        ],
        [HBM] * 4,
        [pltpu.VMEM(sources.shape[1:], jnp.float32), pltpu.SemaphoreType.DMA((4,))],
        name="start",
    )(in_hbm(sources[0]), in_hbm(mirror_rows), in_hbm(block_rows), in_hbm(block_cols))
    chunks, blocks = lax.optimization_barrier((chunks, blocks))
    got = lax.all_to_all(chunks, AXES, 0, 0)
    other_blocks = swapped(blocks, 1)
    weights, pick = call(
        prepare_kernel,
        [
            shaped(blocks.shape[0] // 2, 2 * BLOCK, 2 * BLOCK, dtype=blocks.dtype),
            shaped(2 * ROWS * blocks.shape[0], owners * ROWS, dtype=jnp.bfloat16),
        ],
        [HBM, VMEM, SMEM, SMEM],
        [pltpu.VMEM(blocks.shape, blocks.dtype), pltpu.SemaphoreType.DMA],
        name="prepare",
    )(in_hbm(blocks), other_blocks, places, swapped(places, 1))
    near_args = (pick, weights)
    chunks, zero, coeff = call(
        functools.partial(first_kernel, total), [chunk, vector, tile], [VMEM] * 3, name="first"
    )(got, *near_args)
    got = exchanged(chunks)
    chunks, one, coeff = call(
        functools.partial(middle_kernel, total, shift), [chunk, vector, tile], [VMEM] * 5,
        name="middle",
    )(got, zero, coeff, *near_args)
    first_got, got = got, exchanged(chunks)
    chunks, two, coeff, low, high = call(
        functools.partial(last_kernel, total, shift),
        [shaped(devices, BLOCK), vector, tile, tile, tile], [VMEM] * 7, name="last",
    )(first_got, got, zero, one, coeff, *near_args)
    got = lax.all_to_all(chunks.reshape(devices, 1, BLOCK), AXES, 0, 0)
    packed = shaped(PACKED, ROWS, BLOCK)
    mine, theirs = call(pack_kernel, [packed, packed], [VMEM] * 6, name="pack")(
        zero, one, two, coeff, low, high
    )
    kept, known, terms = call(
        keep_kernel,
        [shaped(ITERS + 1, ROWS, panels), tile, shaped(TERMS, ROWS, BLOCK)], [VMEM] * 5,
        name="keep",
    )(
        mine, swapped(theirs, 1), swapped(mine, devices // 2), swapped(theirs, devices // 2 ^ 1),
        mirror_rows,
    )
    basis, hessenberg = call(
        functools.partial(final_kernel, total),
        [shaped(ITERS + 1, ROWS, panels), shaped(ITERS, ITERS + 1, ROWS)], [VMEM] * 4,
        name="final",
    )(got.reshape(devices, BLOCK), kept, known, terms)
    return basis[:, None], hessenberg.transpose(2, 1, 0)


def solution(mesh):
    placed = (
        P("side", None, ("grp", "dev")),
        P("side", ("grp", "dev"), None, None),
        P("side", ("grp", "dev")),
        P("side", ("grp", "dev")),
        P(("grp", "dev")),
    )
    return jax.shard_map(
        on_device,
        mesh=mesh,
        in_specs=placed,
        out_specs=(P(None, "side", None, ("grp", "dev")), P()),
        check_vma=False,
    )
```

```python
import functools

import jax
import jax.numpy as jnp
from jax import lax
from jax.experimental import pallas as pl
from jax.experimental.pallas import tpu as pltpu
from jax.sharding import PartitionSpec as P

BLOCK = 128
BLK_DEV = 2
ITERS = 3
ROWS = 8
HALF_RHS = 4
EPSILON = 1e-06
AXES = ("side", "grp", "dev")
VMEM_LIMIT = 48 * 2**20
LENGTH_LANE = ITERS * (ITERS + 1)
START_LANE = LENGTH_LANE + 1
PACKED = ITERS + 2
TINY = 1e-30


def position():
    side = lax.axis_index("side")
    dev = lax.axis_index("dev")
    owner = lax.axis_index("grp") * lax.axis_size("dev") + dev
    return side, owner, lax.rem(dev, 2)


def iota(shape, axis):
    return lax.broadcasted_iota(jnp.int32, shape, axis)


def per_rhs(tile):
    column = jnp.sum(tile, axis=1, keepdims=True)
    return column + jnp.concatenate([column[HALF_RHS:], column[:HALF_RHS]], axis=0)


def dot(left, right):
    return per_rhs(jnp.sum(left * right, axis=0))


def columns(values):
    lane = iota((ROWS, BLOCK), 1)
    tile = jnp.zeros((ROWS, BLOCK), jnp.float32)
    for index, value in values.items():
        tile = jnp.where(lane == index, value, tile)
    return tile


def mirror_onehot(mirror_ref, block):
    return (iota((BLOCK, BLOCK), 0) == mirror_ref[block : block + 1, :]).astype(jnp.float32)


def exact_dot(left, right, dims):
    return lax.dot_general(
        left, right, (dims, ((), ())),
        precision=lax.Precision.HIGHEST, preferred_element_type=jnp.float32,
    )


def start_kernel(sources_hbm, mirror_hbm, rows_hbm, cols_hbm, chunk_ref, mirror_ref, places_ref,
                 sources_ref, sems):
    copies = [
        pltpu.make_async_copy(sources_hbm, sources_ref, sems.at[0]),
        pltpu.make_async_copy(mirror_hbm, mirror_ref, sems.at[1]),
        pltpu.make_async_copy(rows_hbm, places_ref.at[0], sems.at[2]),
        pltpu.make_async_copy(cols_hbm, places_ref.at[1], sems.at[3]),
    ]
    for copy in copies:
        copy.start()
    for copy in copies:
        copy.wait()
    side, _, _ = position()
    pieces = []
    for block in range(BLK_DEV):
        part = sources_ref[:, block * BLOCK : (block + 1) * BLOCK]
        places = jnp.broadcast_to(mirror_ref[block : block + 1, :], part.shape)
        moved = jnp.take_along_axis(part, places, axis=1, mode="promise_in_bounds")
        pieces.append(jnp.where(side == 0, part, moved))
    tiles = [
        jnp.concatenate([piece[HALF_RHS * c : HALF_RHS * (c + 1)] for piece in pieces], axis=0)
        for c in range(2)
    ]
    chips = chunk_ref.shape[0] // 2

    def store(chip, carry):
        chunk_ref[2 * chip] = tiles[0]
        chunk_ref[2 * chip + 1] = tiles[1]
        return carry

    lax.fori_loop(0, chips, store, 0, unroll=chips <= 32)


def prepare_kernel(own_hbm, other_ref, own_places, other_places, weights_ref, pick_ref, own_ref,
                   sem):
    copy = pltpu.make_async_copy(own_hbm, own_ref, sem)
    copy.start()
    width = pick_ref.shape[1]
    half_of_row = iota((ROWS, width), 0) // HALF_RHS
    rhs_of_row = iota((ROWS, width), 0) % HALF_RHS
    lane = iota((ROWS, width), 1)
    for entry in range(own_ref.shape[0]):
        picks = []
        for places in (own_places, other_places):
            place = jnp.where(
                half_of_row == places[0, 0, entry], HALF_RHS * places[1, 0, entry] + rhs_of_row, -1
            )
            picks.append((lane == place).astype(jnp.float32))
        first = 2 * ROWS * entry
        pick_ref[first : first + 2 * ROWS, :] = jnp.concatenate(picks, axis=0).astype(jnp.bfloat16)
    for side, ref in ((1, other_ref), (0, own_ref)):
        if side == 0:
            copy.wait()
        for entry in range(own_ref.shape[0]):
            first = entry % 2 * BLOCK
            weights_ref[
                entry // 2, first : first + BLOCK, side * BLOCK : (side + 1) * BLOCK
            ] = ref[entry].T


def near(half, pick_ref, weights_ref):
    flat = half.reshape(-1, BLOCK)
    coarse = flat.astype(jnp.bfloat16)
    fine = (flat - coarse.astype(jnp.float32)).astype(jnp.bfloat16)
    picked = lax.dot_general(
        pick_ref[...], jnp.concatenate([coarse, fine], axis=1), (((1,), (0,)), ((), ())),
        preferred_element_type=jnp.float32,
    ).astype(jnp.bfloat16)
    sums = [jnp.zeros((4 * ROWS, 2 * BLOCK), jnp.float32) for _ in range(2)]
    for group in range(weights_ref.shape[0]):
        rows = [
            slice(2 * ROWS * place, 2 * ROWS * (place + 1)) for place in (2 * group, 2 * group + 1)
        ]
        left = jnp.concatenate(
            [
                jnp.concatenate([picked[rows[0], part], picked[rows[1], part]], axis=1)
                for part in (slice(0, BLOCK), slice(BLOCK, 2 * BLOCK))
            ],
            axis=0,
        )
        sums[group % 2] += lax.dot_general(
            left, weights_ref[group], (((1,), (0,)), ((), ())), preferred_element_type=jnp.float32
        )
    total = sums[0] + sums[1]
    total = total[: 2 * ROWS] + total[2 * ROWS :]
    _, _, core = position()
    own = total[:ROWS, :BLOCK]
    other = total[ROWS:, BLOCK:]
    return jnp.where(core == 0, own, other), jnp.where(core == 0, other, own)


def spread(chunk_ref, low, high):
    chips = chunk_ref.shape[0]

    def store(chip, carry):
        chunk_ref[chip, 0] = low
        chunk_ref[chip, 1] = high
        return carry

    lax.fori_loop(0, chips, store, 0, unroll=chips <= 32)


def first_kernel(total, got_ref, pick_ref, weights_ref, chunk_ref, basis_ref, coeff_ref):
    side, _, _ = position()
    owners = got_ref.shape[0] // 2
    port = got_ref[:owners]
    star = got_ref[owners:]
    half = jnp.where(side == 0, port + star, port - star)
    tiles = near(half, pick_ref, weights_ref)
    squares = per_rhs(jnp.sum(port * port + star * star, axis=0)) * (1.0 / total) + EPSILON
    own = dot(half, half) * (0.5 / total)
    scale = lax.rsqrt(jnp.maximum(own, TINY))
    coeff_ref[...] = columns(
        {LENGTH_LANE: jnp.sqrt(squares), START_LANE: jnp.sqrt(own) * lax.rsqrt(squares)}
    )
    basis_ref[...] = half * scale
    spread(chunk_ref, *[tile * scale for tile in tiles])


def in_order(got_ref, shift):
    chips = got_ref.shape[0]
    return jnp.concatenate([got_ref[chips - shift :], got_ref[: chips - shift]], axis=0)


def own_tiles(got_ref, shift):
    _, owner, _ = position()
    chips = got_ref.shape[0]
    chip = lax.rem(owner // 2 + chips - shift, chips)
    return got_ref[chip, 0], got_ref[chip, 1]


def advanced(total, shift, got_refs, basis_refs, pick_ref, weights_ref):
    got = in_order(got_refs[-1], shift).reshape(basis_refs[0].shape)
    tiles = near(got, pick_ref, weights_ref)
    inner = 0.5 / total
    coeffs = [dot(got, ref[...]) * inner for ref in basis_refs]
    rest = got
    for coeff, ref in zip(coeffs, basis_refs):
        rest = rest - coeff * ref[...]
    squares = dot(rest, rest) * inner
    scale = lax.rsqrt(jnp.maximum(squares, TINY))
    owned = [own_tiles(ref, shift) for ref in got_refs]
    parts = []
    for place, value in enumerate(tiles):
        for coeff, earlier in zip(coeffs, owned):
            value = value - coeff * earlier[place]
        parts.append(value * scale)
    return coeffs + [jnp.sqrt(squares)], rest * scale, parts


def middle_kernel(total, shift, got_ref, basis_ref, known_ref, pick_ref, weights_ref,
                  chunk_ref, next_ref, coeff_ref):
    coeffs, next_ref[...], parts = advanced(
        total, shift, [got_ref], [basis_ref], pick_ref, weights_ref
    )
    coeff_ref[...] = columns(dict(enumerate(coeffs))) + known_ref[...]
    spread(chunk_ref, *parts)


def last_kernel(total, shift, first_got_ref, got_ref, zero_ref, one_ref, known_ref, pick_ref,
                weights_ref, chunk_ref, two_ref, coeff_ref, low_ref, high_ref):
    _, owner, core = position()
    refs = [zero_ref, one_ref, two_ref]
    coeffs, two_ref[...], tiles = advanced(
        total, shift, [first_got_ref, got_ref], refs[:2], pick_ref, weights_ref
    )
    base = owner - core
    rhs = iota((ROWS, BLOCK), 0)
    lane = iota((ROWS, BLOCK), 1)
    spots = jnp.zeros((ROWS, BLOCK), jnp.float32)
    for index in range(ITERS + 1):
        if index < ITERS:
            product = tiles[0] * refs[index][base] + tiles[1] * refs[index][base + 1]
        else:
            product = tiles[0] * tiles[0] + tiles[1] * tiles[1]
        column = jnp.sum(product, axis=1, keepdims=True)
        spots = jnp.where(lane == ROWS * index + rhs, column, spots)
    row = jnp.sum(spots, axis=0, keepdims=True)
    chunk_ref[...] = jnp.broadcast_to(row, chunk_ref.shape)
    coeffs = columns({place + ITERS + 1: value for place, value in enumerate(coeffs)})
    coeff_ref[...] = coeffs + known_ref[...]
    low_ref[...] = tiles[0]
    high_ref[...] = tiles[1]


def pack_kernel(zero_ref, one_ref, two_ref, coeff_ref, low_ref, high_ref, mine_ref, theirs_ref):
    _, owner, core = position()
    for out_ref, which in ((mine_ref, core), (theirs_ref, 1 - core)):
        for index, ref in enumerate((zero_ref, one_ref, two_ref)):
            out_ref[index] = ref[owner - core + which]
        out_ref[ITERS] = jnp.where(which == 0, low_ref[...], high_ref[...])
        out_ref[ITERS + 1] = coeff_ref[...]


def over_halves(products):
    return sum(one * other for one, other in products)


def squared(vector):
    return over_halves([(value, value) for half in vector for value in half])


def keep_kernel(mine_ref, partner_ref, across_ref, flipped_ref, mirror_ref, kept_ref, known_ref,
                terms_ref):
    side, _, core = position()
    packed = []
    for index in range(PACKED):
        mine, partner = mine_ref[index], partner_ref[index]
        across, flipped = across_ref[index], flipped_ref[index]
        here = [jnp.where(core == 0, mine, partner), jnp.where(core == 0, partner, mine)]
        there = [jnp.where(core == 0, across, flipped), jnp.where(core == 0, flipped, across)]
        packed.append(
            [
                [jnp.where(side == 0, h, t) for h, t in zip(here, there)],
                [jnp.where(side == 0, t, h) for h, t in zip(here, there)],
            ]
        )
    known = [
        jnp.concatenate([tile[:HALF_RHS] for tile in packed[ITERS + 1][half]], axis=0)
        for half in range(2)
    ]

    def entry(half, j, k):
        place = k * (ITERS + 1) + j
        return known[half][:, place : place + 1]

    halves = range(2)
    length = known[0][:, LENGTH_LANE : LENGTH_LANE + 1]
    start = [known[half][:, START_LANE : START_LANE + 1] for half in halves]
    zero = [[start[half]] for half in halves]
    ahead = [[entry(half, 0, 0) * zero[half][0], entry(half, 1, 0) * zero[half][0]] for half in halves]
    short = [EPSILON / (length * length)]
    product = over_halves([(ahead[half][0], zero[half][0]) for half in halves])
    multiple = product - 0.5 * short[0]
    rest = [[ahead[half][0] - multiple * zero[half][0], ahead[half][1]] for half in halves]
    squares = squared(rest) + EPSILON
    norms = [jnp.sqrt(squares)]
    one = [[value * lax.rsqrt(squares) for value in rest[half]] for half in halves]
    heads = {(0, 0): product + 0.5 * squared(zero), (1, 0): norms[0]}
    short.append(EPSILON / squares)
    cross = heads[0, 0] * short[0] / norms[0]
    ahead = [
        [
            entry(half, 0, 0) * one[half][0] + entry(half, 0, 1) * one[half][1],
            entry(half, 1, 0) * one[half][0] + entry(half, 1, 1) * one[half][1],
            entry(half, 2, 1) * one[half][1],
        ]
        for half in halves
    ]
    product = over_halves([pair for half in halves for pair in zip(ahead[half], one[half])])
    multiples = [
        over_halves([(ahead[half][0], zero[half][0]) for half in halves]) + 0.5 * cross,
        product - 0.5 * short[1],
    ]
    rest = [
        [
            ahead[half][0] - multiples[0] * zero[half][0] - multiples[1] * one[half][0],
            ahead[half][1] - multiples[1] * one[half][1],
            ahead[half][2],
        ]
        for half in halves
    ]
    squares = squared(rest) + EPSILON
    norms.append(jnp.sqrt(squares))
    two = [[value * lax.rsqrt(squares) for value in rest[half]] for half in halves]
    heads.update({(0, 1): multiples[0], (1, 1): product + 0.5 * squared(one), (2, 1): norms[1]})
    short.append(EPSILON / squares)
    crosses = [
        (heads[0, 1] * short[0] - heads[1, 1] * cross) / norms[1],
        (heads[1, 1] * short[1] - heads[0, 1] * cross) / norms[1],
    ]
    ahead = [
        [
            entry(half, 0, 0) * two[half][0] + entry(half, 0, 1) * two[half][1],
            entry(half, 1, 0) * two[half][0] + entry(half, 1, 1) * two[half][1],
            entry(half, 2, 1) * two[half][1],
        ]
        for half in halves
    ]
    known_ref[...] = columns({k * (ITERS + 1) + j: value for (j, k), value in heads.items()})
    terms = [0.5 * crosses[0], 0.5 * crosses[1], -0.5 * short[2]]
    for half in halves:
        terms += zero[half] + one[half] + two[half] + ahead[half]
    for index, value in enumerate(terms):
        terms_ref[index] = jnp.broadcast_to(value, (ROWS, BLOCK))
    for block in range(BLK_DEV):
        rows = slice(block * HALF_RHS, (block + 1) * HALF_RHS)
        vectors = []
        for half in halves:
            parts = [
                jnp.concatenate([tile[rows] for tile in packed[index][half]], axis=0)
                for index in range(ITERS + 1)
            ]
            vectors.append(
                [
                    over_halves(zip(weights, parts))
                    for weights in (
                        zero[half], one[half], two[half], ahead[half] + [two[half][2]]
                    )
                ]
            )
        ports = [0.5 * (sym + anti) for sym, anti in zip(*vectors)]
        stars = [0.5 * (sym - anti) for sym, anti in zip(*vectors)]
        back = exact_dot(
            jnp.concatenate(stars, axis=0), mirror_onehot(mirror_ref, block), ((1,), (1,))
        )
        for index, port in enumerate(ports):
            kept_ref[index, :, block * BLOCK : (block + 1) * BLOCK] = jnp.where(
                side == 0, port, back[index * ROWS : (index + 1) * ROWS]
            )


TERMS = 3 + 2 * 9


def final_kernel(total, got_ref, kept_ref, known_ref, terms_ref, basis_ref, hessenberg_ref):
    inner = 0.5 / total
    got = got_ref[...]
    devices = got.shape[0]
    even = iota((ROWS, BLOCK), 0) % 2 == 0
    rhs = iota((ROWS, BLOCK), 0)
    lane = iota((ROWS, BLOCK), 1)
    halves = range(2)
    values = []
    for half in halves:
        rows = got[half * devices // 2 : (half + 1) * devices // 2]
        sums = jnp.sum(rows.reshape(-1, ROWS, BLOCK), axis=0)
        lower = jnp.sum(jnp.where(even, sums, 0.0), axis=0, keepdims=True)
        upper = jnp.sum(jnp.where(even, 0.0, sums), axis=0, keepdims=True)
        spots = jnp.where(rhs < HALF_RHS, lower, upper) * inner
        values.append(
            [
                jnp.sum(
                    jnp.where(
                        (lane // ROWS == index) & (lane % HALF_RHS == rhs % HALF_RHS), spots, 0.0
                    ),
                    axis=1,
                    keepdims=True,
                )
                for index in range(ITERS + 1)
            ]
        )
    terms = [terms_ref[index] for index in range(TERMS)]
    zero, one, two, ahead = [], [], [], []
    for half in halves:
        own = terms[3 + 9 * half : 12 + 9 * half]
        zero.append(own[0:1])
        one.append(own[1:3])
        two.append(own[3:6])
        ahead.append(
            [known + own[5] * value for known, value in zip(own[6:9], values[half][:ITERS])]
        )
    products = [
        over_halves([pair for half in halves for pair in zip(ahead[half], vector[half])])
        for vector in (zero, one, two)
    ]
    multiples = [product + term for product, term in zip(products, terms[:3])]
    squares = jnp.full((ROWS, BLOCK), EPSILON, jnp.float32)
    for half in halves:
        beyond = values[half][ITERS]
        for value in values[half][:ITERS]:
            beyond = beyond - value * value
        squares = squares + jnp.maximum(beyond, 0.0) * two[half][2] * two[half][2]
        for index in range(ITERS):
            value = ahead[half][index]
            for multiple, vector in zip(multiples, (zero, one, two)):
                if index < len(vector[half]):
                    value = value - multiple * vector[half][index]
            squares = squares + value * value
    scale = lax.rsqrt(squares)
    basis_ref[:ITERS] = kept_ref[:ITERS]
    for block in range(BLK_DEV):
        span = slice(block * BLOCK, (block + 1) * BLOCK)
        rest = kept_ref[ITERS, :, span]
        for j in range(ITERS):
            rest = rest - multiples[j] * kept_ref[j, :, span]
        basis_ref[ITERS, :, span] = rest * scale
    place = 2 * (ITERS + 1)
    coeffs = multiples[:-1] + [products[-1] + 0.5 * squared(two), jnp.sqrt(squares)]
    whole = known_ref[...] + columns({place + index: value for index, value in enumerate(coeffs)})
    turned = whole.T
    for k in range(ITERS):
        hessenberg_ref[k] = turned[k * (ITERS + 1) : (k + 1) * (ITERS + 1), :]


VMEM = pl.BlockSpec(memory_space=pltpu.VMEM)
SMEM = pl.BlockSpec(memory_space=pltpu.SMEM)
HBM = pl.BlockSpec(memory_space=pltpu.HBM)


def shaped(*shape, dtype=jnp.float32):
    return jax.ShapeDtypeStruct(shape, dtype)


def in_hbm(value):
    return pltpu.with_memory_space_constraint(value, pltpu.HBM)


def call(kernel, outs, specs, scratch=(), name=None):
    return pl.pallas_call(
        kernel,
        out_shape=outs,
        in_specs=specs,
        out_specs=[VMEM] * len(outs),
        scratch_shapes=scratch,
        compiler_params=pltpu.CompilerParams(vmem_limit_bytes=VMEM_LIMIT),
        name=name,
    )


def on_device(sources, near_blocks, block_rows, block_cols, mirror):
    devices = lax.axis_size(AXES)
    owners = devices // 2
    chips = devices // 2
    panels = sources.shape[2]
    total = 1.0 * panels * devices
    shift = 5 % (chips // 2)
    groups = [
        [
            2 * (side * (chips // 2) + (chip + shift) % (chips // 2)) + core
            for chip in range(chips // 2)
        ]
        for side in range(2)
        for core in range(2)
    ]
    mirror_rows = mirror.reshape(BLK_DEV, BLOCK)
    blocks = near_blocks[0]
    everything = shaped(devices, ROWS, BLOCK)
    vector = shaped(owners, ROWS, BLOCK)
    chunk = shaped(chips // 2, 2, ROWS, BLOCK)
    tile = shaped(ROWS, BLOCK)

    def swapped(value, bits):
        return lax.ppermute(value, AXES, [(i, i ^ bits) for i in range(devices)])

    def exchanged(chunks):
        return lax.all_to_all(chunks, AXES, 0, 0, axis_index_groups=groups)

    chunks, mirror_rows, places = call(
        start_kernel,
        [
            everything,
            shaped(*mirror_rows.shape, dtype=jnp.int32),
            shaped(2, *block_rows.shape, dtype=jnp.int32),
        ],
        [HBM] * 4,
        [pltpu.VMEM(sources.shape[1:], jnp.float32), pltpu.SemaphoreType.DMA((4,))],
        name="start",
    )(in_hbm(sources[0]), in_hbm(mirror_rows), in_hbm(block_rows), in_hbm(block_cols))
    chunks, blocks = lax.optimization_barrier((chunks, blocks))
    got = lax.all_to_all(chunks, AXES, 0, 0)
    other_blocks = swapped(blocks, 1)
    weights, pick = call(
        prepare_kernel,
        [
            shaped(blocks.shape[0] // 2, 2 * BLOCK, 2 * BLOCK, dtype=blocks.dtype),
            shaped(2 * ROWS * blocks.shape[0], owners * ROWS, dtype=jnp.bfloat16),
        ],
        [HBM, VMEM, SMEM, SMEM],
        [pltpu.VMEM(blocks.shape, blocks.dtype), pltpu.SemaphoreType.DMA],
        name="prepare",
    )(in_hbm(blocks), other_blocks, places, swapped(places, 1))
    near_args = (pick, weights)
    chunks, zero, coeff = call(
        functools.partial(first_kernel, total), [chunk, vector, tile], [VMEM] * 3, name="first"
    )(got, *near_args)
    got = exchanged(chunks)
    chunks, one, coeff = call(
        functools.partial(middle_kernel, total, shift), [chunk, vector, tile], [VMEM] * 5,
        name="middle",
    )(got, zero, coeff, *near_args)
    first_got, got = got, exchanged(chunks)
    chunks, two, coeff, low, high = call(
        functools.partial(last_kernel, total, shift),
        [shaped(devices, BLOCK), vector, tile, tile, tile], [VMEM] * 7, name="last",
    )(first_got, got, zero, one, coeff, *near_args)
    got = lax.all_to_all(chunks.reshape(devices, 1, BLOCK), AXES, 0, 0)
    packed = shaped(PACKED, ROWS, BLOCK)
    mine, theirs = call(pack_kernel, [packed, packed], [VMEM] * 6, name="pack")(
        zero, one, two, coeff, low, high
    )
    kept, known, terms = call(
        keep_kernel,
        [shaped(ITERS + 1, ROWS, panels), tile, shaped(TERMS, ROWS, BLOCK)], [VMEM] * 5,
        name="keep",
    )(
        mine, swapped(theirs, 1), swapped(mine, devices // 2), swapped(theirs, devices // 2 ^ 1),
        mirror_rows,
    )
    basis, hessenberg = call(
        functools.partial(final_kernel, total),
        [shaped(ITERS + 1, ROWS, panels), shaped(ITERS, ITERS + 1, ROWS)], [VMEM] * 4,
        name="final",
    )(got.reshape(devices, BLOCK), kept, known, terms)
    return basis[:, None], hessenberg.transpose(2, 1, 0)


def solution(mesh):
    placed = (
        P("side", None, ("grp", "dev")),
        P("side", ("grp", "dev"), None, None),
        P("side", ("grp", "dev")),
        P("side", ("grp", "dev")),
        P(("grp", "dev")),
    )
    return jax.shard_map(
        on_device,
        mesh=mesh,
        in_specs=placed,
        out_specs=(P(None, "side", None, ("grp", "dev")), P()),
        check_vma=False,
    )
```

```python
import functools

import jax
import jax.numpy as jnp
from jax import lax
from jax.experimental import pallas as pl
from jax.experimental.pallas import tpu as pltpu
from jax.sharding import PartitionSpec as P

BLOCK = 128
BLK_DEV = 2
ITERS = 3
ROWS = 8
HALF_RHS = 4
EPSILON = 1e-06
AXES = ("side", "grp", "dev")
VMEM_LIMIT = 48 * 2**20
LENGTH_LANE = ITERS * (ITERS + 1)
START_LANE = LENGTH_LANE + 1
PACKED = ITERS + 2
TINY = 1e-30


def position():
    side = lax.axis_index("side")
    dev = lax.axis_index("dev")
    owner = lax.axis_index("grp") * lax.axis_size("dev") + dev
    return side, owner, lax.rem(dev, 2)


def iota(shape, axis):
    return lax.broadcasted_iota(jnp.int32, shape, axis)


def per_rhs(tile):
    column = jnp.sum(tile, axis=1, keepdims=True)
    return column + jnp.concatenate([column[HALF_RHS:], column[:HALF_RHS]], axis=0)


def dot(left, right):
    return per_rhs(jnp.sum(left * right, axis=0))


def columns(values):
    lane = iota((ROWS, BLOCK), 1)
    tile = jnp.zeros((ROWS, BLOCK), jnp.float32)
    for index, value in values.items():
        tile = jnp.where(lane == index, value, tile)
    return tile


def mirror_onehot(mirror_ref, block):
    return (iota((BLOCK, BLOCK), 0) == mirror_ref[block : block + 1, :]).astype(jnp.float32)


def exact_dot(left, right, dims):
    return lax.dot_general(
        left, right, (dims, ((), ())),
        precision=lax.Precision.HIGHEST, preferred_element_type=jnp.float32,
    )


def start_kernel(sources_hbm, mirror_hbm, rows_hbm, cols_hbm, chunk_ref, mirror_ref, places_ref,
                 sources_ref, sems):
    copies = [
        pltpu.make_async_copy(sources_hbm, sources_ref, sems.at[0]),
        pltpu.make_async_copy(mirror_hbm, mirror_ref, sems.at[1]),
        pltpu.make_async_copy(rows_hbm, places_ref.at[0], sems.at[2]),
        pltpu.make_async_copy(cols_hbm, places_ref.at[1], sems.at[3]),
    ]
    for copy in copies:
        copy.start()
    for copy in copies:
        copy.wait()
    side, _, _ = position()
    pieces = []
    for block in range(BLK_DEV):
        part = sources_ref[:, block * BLOCK : (block + 1) * BLOCK]
        places = jnp.broadcast_to(mirror_ref[block : block + 1, :], part.shape)
        moved = jnp.take_along_axis(part, places, axis=1, mode="promise_in_bounds")
        pieces.append(jnp.where(side == 0, part, moved))
    tiles = [
        jnp.concatenate([piece[HALF_RHS * c : HALF_RHS * (c + 1)] for piece in pieces], axis=0)
        for c in range(2)
    ]
    chips = chunk_ref.shape[0] // 2

    def store(chip, carry):
        chunk_ref[2 * chip + 1] = tiles[0]
        chunk_ref[2 * chip + 2] = tiles[1]
        return carry

    chunk_ref[0] = tiles[0]
    lax.fori_loop(0, chips - 1, store, 0, unroll=chips <= 32)
    chunk_ref[2 * chips - 1] = tiles[1]


def prepare_kernel(own_hbm, other_ref, own_places, other_places, weights_ref, pick_ref, own_ref,
                   sem):
    copy = pltpu.make_async_copy(own_hbm, own_ref, sem)
    copy.start()
    width = pick_ref.shape[1]
    half_of_row = iota((ROWS, width), 0) // HALF_RHS
    rhs_of_row = iota((ROWS, width), 0) % HALF_RHS
    lane = iota((ROWS, width), 1)
    for entry in range(own_ref.shape[0]):
        picks = []
        for places in (own_places, other_places):
            place = jnp.where(
                half_of_row == places[0, 0, entry], HALF_RHS * places[1, 0, entry] + rhs_of_row, -1
            )
            picks.append((lane == place).astype(jnp.float32))
        first = 2 * ROWS * entry
        pick_ref[first : first + 2 * ROWS, :] = jnp.concatenate(picks, axis=0).astype(jnp.bfloat16)
    for side, ref in ((1, other_ref), (0, own_ref)):
        if side == 0:
            copy.wait()
        for entry in range(own_ref.shape[0]):
            first = entry % 2 * BLOCK
            weights_ref[
                entry // 2, first : first + BLOCK, side * BLOCK : (side + 1) * BLOCK
            ] = ref[entry].T


def near(half, pick_ref, weights_ref):
    flat = half.reshape(-1, BLOCK)
    coarse = flat.astype(jnp.bfloat16)
    fine = (flat - coarse.astype(jnp.float32)).astype(jnp.bfloat16)
    picked = lax.dot_general(
        pick_ref[...], jnp.concatenate([coarse, fine], axis=1), (((1,), (0,)), ((), ())),
        preferred_element_type=jnp.float32,
    ).astype(jnp.bfloat16)
    sums = [jnp.zeros((4 * ROWS, 2 * BLOCK), jnp.float32) for _ in range(2)]
    for group in range(weights_ref.shape[0]):
        rows = [
            slice(2 * ROWS * place, 2 * ROWS * (place + 1)) for place in (2 * group, 2 * group + 1)
        ]
        left = jnp.concatenate(
            [
                jnp.concatenate([picked[rows[0], part], picked[rows[1], part]], axis=1)
                for part in (slice(0, BLOCK), slice(BLOCK, 2 * BLOCK))
            ],
            axis=0,
        )
        sums[group % 2] += lax.dot_general(
            left, weights_ref[group], (((1,), (0,)), ((), ())), preferred_element_type=jnp.float32
        )
    total = sums[0] + sums[1]
    total = total[: 2 * ROWS] + total[2 * ROWS :]
    _, _, core = position()
    own = total[:ROWS, :BLOCK]
    other = total[ROWS:, BLOCK:]
    return jnp.where(core == 0, own, other), jnp.where(core == 0, other, own)


def spread(chunk_ref, low, high):
    chips = chunk_ref.shape[0]

    def store(chip, carry):
        chunk_ref[chip, 0] = low
        chunk_ref[chip, 1] = high
        return carry

    lax.fori_loop(0, chips, store, 0, unroll=chips <= 32)


def first_kernel(total, got_ref, pick_ref, weights_ref, chunk_ref, basis_ref, coeff_ref):
    side, _, _ = position()
    owners = got_ref.shape[0] // 2
    last = 2 * owners - 1
    port = got_ref[1 : owners + 1]
    star = jnp.concatenate([got_ref[owners + 1 : last], got_ref[:1], got_ref[last:]], axis=0)
    half = jnp.where(side == 0, port + star, port - star)
    tiles = near(half, pick_ref, weights_ref)
    squares = per_rhs(jnp.sum(port * port + star * star, axis=0)) * (1.0 / total) + EPSILON
    own = dot(half, half) * (0.5 / total)
    scale = lax.rsqrt(jnp.maximum(own, TINY))
    coeff_ref[...] = columns(
        {LENGTH_LANE: jnp.sqrt(squares), START_LANE: jnp.sqrt(own) * lax.rsqrt(squares)}
    )
    basis_ref[...] = half * scale
    spread(chunk_ref, *[tile * scale for tile in tiles])


def in_order(got_ref, shift):
    chips = got_ref.shape[0]
    return jnp.concatenate([got_ref[chips - shift :], got_ref[: chips - shift]], axis=0)


def own_tiles(got_ref, shift):
    _, owner, _ = position()
    chips = got_ref.shape[0]
    chip = lax.rem(owner // 2 + chips - shift, chips)
    return got_ref[chip, 0], got_ref[chip, 1]


def advanced(total, shift, got_refs, basis_refs, pick_ref, weights_ref):
    got = in_order(got_refs[-1], shift).reshape(basis_refs[0].shape)
    tiles = near(got, pick_ref, weights_ref)
    inner = 0.5 / total
    coeffs = [dot(got, ref[...]) * inner for ref in basis_refs]
    rest = got
    for coeff, ref in zip(coeffs, basis_refs):
        rest = rest - coeff * ref[...]
    squares = dot(rest, rest) * inner
    scale = lax.rsqrt(jnp.maximum(squares, TINY))
    owned = [own_tiles(ref, shift) for ref in got_refs]
    parts = []
    for place, value in enumerate(tiles):
        for coeff, earlier in zip(coeffs, owned):
            value = value - coeff * earlier[place]
        parts.append(value * scale)
    return coeffs + [jnp.sqrt(squares)], rest * scale, parts


def middle_kernel(total, shift, got_ref, basis_ref, known_ref, pick_ref, weights_ref,
                  chunk_ref, next_ref, coeff_ref):
    coeffs, next_ref[...], parts = advanced(
        total, shift, [got_ref], [basis_ref], pick_ref, weights_ref
    )
    coeff_ref[...] = columns(dict(enumerate(coeffs))) + known_ref[...]
    spread(chunk_ref, *parts)


def last_kernel(total, shift, first_got_ref, got_ref, zero_ref, one_ref, known_ref, pick_ref,
                weights_ref, chunk_ref, two_ref, coeff_ref, low_ref, high_ref):
    _, owner, core = position()
    refs = [zero_ref, one_ref, two_ref]
    coeffs, two_ref[...], tiles = advanced(
        total, shift, [first_got_ref, got_ref], refs[:2], pick_ref, weights_ref
    )
    base = owner - core
    rhs = iota((ROWS, BLOCK), 0)
    lane = iota((ROWS, BLOCK), 1)
    spots = jnp.zeros((ROWS, BLOCK), jnp.float32)
    for index in range(ITERS + 1):
        if index < ITERS:
            product = tiles[0] * refs[index][base] + tiles[1] * refs[index][base + 1]
        else:
            product = tiles[0] * tiles[0] + tiles[1] * tiles[1]
        column = jnp.sum(product, axis=1, keepdims=True)
        spots = jnp.where(lane == ROWS * index + rhs, column, spots)
    row = jnp.sum(spots, axis=0, keepdims=True)
    chunk_ref[...] = jnp.broadcast_to(row, chunk_ref.shape)
    coeffs = columns({place + ITERS + 1: value for place, value in enumerate(coeffs)})
    coeff_ref[...] = coeffs + known_ref[...]
    low_ref[...] = tiles[0]
    high_ref[...] = tiles[1]


def pack_kernel(zero_ref, one_ref, two_ref, coeff_ref, low_ref, high_ref, mine_ref, theirs_ref):
    _, owner, core = position()
    for out_ref, which in ((mine_ref, core), (theirs_ref, 1 - core)):
        for index, ref in enumerate((zero_ref, one_ref, two_ref)):
            out_ref[index] = ref[owner - core + which]
        out_ref[ITERS] = jnp.where(which == 0, low_ref[...], high_ref[...])
        out_ref[ITERS + 1] = coeff_ref[...]


def over_halves(products):
    return sum(one * other for one, other in products)


def squared(vector):
    return over_halves([(value, value) for half in vector for value in half])


def keep_kernel(mine_ref, partner_ref, across_ref, flipped_ref, mirror_ref, kept_ref, known_ref,
                terms_ref):
    side, _, core = position()
    packed = []
    for index in range(PACKED):
        mine, partner = mine_ref[index], partner_ref[index]
        across, flipped = across_ref[index], flipped_ref[index]
        here = [jnp.where(core == 0, mine, partner), jnp.where(core == 0, partner, mine)]
        there = [jnp.where(core == 0, across, flipped), jnp.where(core == 0, flipped, across)]
        packed.append(
            [
                [jnp.where(side == 0, h, t) for h, t in zip(here, there)],
                [jnp.where(side == 0, t, h) for h, t in zip(here, there)],
            ]
        )
    known = [
        jnp.concatenate([tile[:HALF_RHS] for tile in packed[ITERS + 1][half]], axis=0)
        for half in range(2)
    ]

    def entry(half, j, k):
        place = k * (ITERS + 1) + j
        return known[half][:, place : place + 1]

    halves = range(2)
    length = known[0][:, LENGTH_LANE : LENGTH_LANE + 1]
    start = [known[half][:, START_LANE : START_LANE + 1] for half in halves]
    zero = [[start[half]] for half in halves]
    ahead = [[entry(half, 0, 0) * zero[half][0], entry(half, 1, 0) * zero[half][0]] for half in halves]
    short = [EPSILON / (length * length)]
    product = over_halves([(ahead[half][0], zero[half][0]) for half in halves])
    multiple = product - 0.5 * short[0]
    rest = [[ahead[half][0] - multiple * zero[half][0], ahead[half][1]] for half in halves]
    squares = squared(rest) + EPSILON
    norms = [jnp.sqrt(squares)]
    one = [[value * lax.rsqrt(squares) for value in rest[half]] for half in halves]
    heads = {(0, 0): product + 0.5 * squared(zero), (1, 0): norms[0]}
    short.append(EPSILON / squares)
    cross = heads[0, 0] * short[0] / norms[0]
    ahead = [
        [
            entry(half, 0, 0) * one[half][0] + entry(half, 0, 1) * one[half][1],
            entry(half, 1, 0) * one[half][0] + entry(half, 1, 1) * one[half][1],
            entry(half, 2, 1) * one[half][1],
        ]
        for half in halves
    ]
    product = over_halves([pair for half in halves for pair in zip(ahead[half], one[half])])
    multiples = [
        over_halves([(ahead[half][0], zero[half][0]) for half in halves]) + 0.5 * cross,
        product - 0.5 * short[1],
    ]
    rest = [
        [
            ahead[half][0] - multiples[0] * zero[half][0] - multiples[1] * one[half][0],
            ahead[half][1] - multiples[1] * one[half][1],
            ahead[half][2],
        ]
        for half in halves
    ]
    squares = squared(rest) + EPSILON
    norms.append(jnp.sqrt(squares))
    two = [[value * lax.rsqrt(squares) for value in rest[half]] for half in halves]
    heads.update({(0, 1): multiples[0], (1, 1): product + 0.5 * squared(one), (2, 1): norms[1]})
    short.append(EPSILON / squares)
    crosses = [
        (heads[0, 1] * short[0] - heads[1, 1] * cross) / norms[1],
        (heads[1, 1] * short[1] - heads[0, 1] * cross) / norms[1],
    ]
    ahead = [
        [
            entry(half, 0, 0) * two[half][0] + entry(half, 0, 1) * two[half][1],
            entry(half, 1, 0) * two[half][0] + entry(half, 1, 1) * two[half][1],
            entry(half, 2, 1) * two[half][1],
        ]
        for half in halves
    ]
    known_ref[...] = columns({k * (ITERS + 1) + j: value for (j, k), value in heads.items()})
    terms = [0.5 * crosses[0], 0.5 * crosses[1], -0.5 * short[2]]
    for half in halves:
        terms += zero[half] + one[half] + two[half] + ahead[half]
    for index, value in enumerate(terms):
        terms_ref[index] = jnp.broadcast_to(value, (ROWS, BLOCK))
    for block in range(BLK_DEV):
        rows = slice(block * HALF_RHS, (block + 1) * HALF_RHS)
        vectors = []
        for half in halves:
            parts = [
                jnp.concatenate([tile[rows] for tile in packed[index][half]], axis=0)
                for index in range(ITERS + 1)
            ]
            vectors.append(
                [
                    over_halves(zip(weights, parts))
                    for weights in (
                        zero[half], one[half], two[half], ahead[half] + [two[half][2]]
                    )
                ]
            )
        ports = [0.5 * (sym + anti) for sym, anti in zip(*vectors)]
        stars = [0.5 * (sym - anti) for sym, anti in zip(*vectors)]
        back = exact_dot(
            jnp.concatenate(stars, axis=0), mirror_onehot(mirror_ref, block), ((1,), (1,))
        )
        for index, port in enumerate(ports):
            kept_ref[index, :, block * BLOCK : (block + 1) * BLOCK] = jnp.where(
                side == 0, port, back[index * ROWS : (index + 1) * ROWS]
            )


TERMS = 3 + 2 * 9


def final_kernel(total, got_ref, kept_ref, known_ref, terms_ref, basis_ref, hessenberg_ref):
    inner = 0.5 / total
    got = got_ref[...]
    devices = got.shape[0]
    place = iota(got.shape, 0)
    device = jnp.where(
        place == 0, devices - 2, jnp.where(place == devices - 1, devices - 1, place - 1)
    )
    rhs = iota((ROWS, BLOCK), 0)
    lane = iota((ROWS, BLOCK), 1)
    halves = range(2)
    values = []
    for half in halves:
        here = (device >= devices // 2) if half == 1 else (device < devices // 2)
        even = device % 2 == 0
        lower = jnp.sum(jnp.where(here & even, got, 0.0), axis=0, keepdims=True)
        upper = jnp.sum(jnp.where(here & ~even, got, 0.0), axis=0, keepdims=True)
        spots = jnp.where(rhs < HALF_RHS, lower, upper) * inner
        values.append(
            [
                jnp.sum(
                    jnp.where(
                        (lane // ROWS == index) & (lane % HALF_RHS == rhs % HALF_RHS), spots, 0.0
                    ),
                    axis=1,
                    keepdims=True,
                )
                for index in range(ITERS + 1)
            ]
        )
    terms = [terms_ref[index] for index in range(TERMS)]
    zero, one, two, ahead = [], [], [], []
    for half in halves:
        own = terms[3 + 9 * half : 12 + 9 * half]
        zero.append(own[0:1])
        one.append(own[1:3])
        two.append(own[3:6])
        ahead.append(
            [known + own[5] * value for known, value in zip(own[6:9], values[half][:ITERS])]
        )
    products = [
        over_halves([pair for half in halves for pair in zip(ahead[half], vector[half])])
        for vector in (zero, one, two)
    ]
    multiples = [product + term for product, term in zip(products, terms[:3])]
    squares = jnp.full((ROWS, BLOCK), EPSILON, jnp.float32)
    for half in halves:
        beyond = values[half][ITERS]
        for value in values[half][:ITERS]:
            beyond = beyond - value * value
        squares = squares + jnp.maximum(beyond, 0.0) * two[half][2] * two[half][2]
        for index in range(ITERS):
            value = ahead[half][index]
            for multiple, vector in zip(multiples, (zero, one, two)):
                if index < len(vector[half]):
                    value = value - multiple * vector[half][index]
            squares = squares + value * value
    scale = lax.rsqrt(squares)
    basis_ref[:ITERS] = kept_ref[:ITERS]
    for block in range(BLK_DEV):
        span = slice(block * BLOCK, (block + 1) * BLOCK)
        rest = kept_ref[ITERS, :, span]
        for j in range(ITERS):
            rest = rest - multiples[j] * kept_ref[j, :, span]
        basis_ref[ITERS, :, span] = rest * scale
    place = 2 * (ITERS + 1)
    coeffs = multiples[:-1] + [products[-1] + 0.5 * squared(two), jnp.sqrt(squares)]
    whole = known_ref[...] + columns({place + index: value for index, value in enumerate(coeffs)})
    turned = whole.T
    for k in range(ITERS):
        hessenberg_ref[k] = turned[k * (ITERS + 1) : (k + 1) * (ITERS + 1), :]


VMEM = pl.BlockSpec(memory_space=pltpu.VMEM)
SMEM = pl.BlockSpec(memory_space=pltpu.SMEM)
HBM = pl.BlockSpec(memory_space=pltpu.HBM)


def shaped(*shape, dtype=jnp.float32):
    return jax.ShapeDtypeStruct(shape, dtype)


def in_hbm(value):
    return pltpu.with_memory_space_constraint(value, pltpu.HBM)


def call(kernel, outs, specs, scratch=(), name=None):
    return pl.pallas_call(
        kernel,
        out_shape=outs,
        in_specs=specs,
        out_specs=[VMEM] * len(outs),
        scratch_shapes=scratch,
        compiler_params=pltpu.CompilerParams(vmem_limit_bytes=VMEM_LIMIT),
        name=name,
    )


def on_device(sources, near_blocks, block_rows, block_cols, mirror):
    devices = lax.axis_size(AXES)
    owners = devices // 2
    chips = devices // 2
    panels = sources.shape[2]
    total = 1.0 * panels * devices
    shift = 5 % (chips // 2)
    groups = [
        [
            2 * (side * (chips // 2) + (chip + shift) % (chips // 2)) + core
            for chip in range(chips // 2)
        ]
        for side in range(2)
        for core in range(2)
    ]
    listed = [[devices - 2, *range(devices - 2), devices - 1]]
    mirror_rows = mirror.reshape(BLK_DEV, BLOCK)
    blocks = near_blocks[0]
    everything = shaped(devices, ROWS, BLOCK)
    vector = shaped(owners, ROWS, BLOCK)
    chunk = shaped(chips // 2, 2, ROWS, BLOCK)
    tile = shaped(ROWS, BLOCK)

    def swapped(value, bits):
        return lax.ppermute(value, AXES, [(i, i ^ bits) for i in range(devices)])

    def exchanged(chunks):
        return lax.all_to_all(chunks, AXES, 0, 0, axis_index_groups=groups)

    chunks, mirror_rows, places = call(
        start_kernel,
        [
            everything,
            shaped(*mirror_rows.shape, dtype=jnp.int32),
            shaped(2, *block_rows.shape, dtype=jnp.int32),
        ],
        [HBM] * 4,
        [pltpu.VMEM(sources.shape[1:], jnp.float32), pltpu.SemaphoreType.DMA((4,))],
        name="start",
    )(in_hbm(sources[0]), in_hbm(mirror_rows), in_hbm(block_rows), in_hbm(block_cols))
    chunks, blocks = lax.optimization_barrier((chunks, blocks))
    got = lax.all_to_all(chunks, AXES, 0, 0, axis_index_groups=listed)
    other_blocks = swapped(blocks, 1)
    weights, pick = call(
        prepare_kernel,
        [
            shaped(blocks.shape[0] // 2, 2 * BLOCK, 2 * BLOCK, dtype=blocks.dtype),
            shaped(2 * ROWS * blocks.shape[0], owners * ROWS, dtype=jnp.bfloat16),
        ],
        [HBM, VMEM, SMEM, SMEM],
        [pltpu.VMEM(blocks.shape, blocks.dtype), pltpu.SemaphoreType.DMA],
        name="prepare",
    )(in_hbm(blocks), other_blocks, places, swapped(places, 1))
    near_args = (pick, weights)
    chunks, zero, coeff = call(
        functools.partial(first_kernel, total), [chunk, vector, tile], [VMEM] * 3, name="first"
    )(got, *near_args)
    got = exchanged(chunks)
    chunks, one, coeff = call(
        functools.partial(middle_kernel, total, shift), [chunk, vector, tile], [VMEM] * 5,
        name="middle",
    )(got, zero, coeff, *near_args)
    first_got, got = got, exchanged(chunks)
    chunks, two, coeff, low, high = call(
        functools.partial(last_kernel, total, shift),
        [shaped(devices, BLOCK), vector, tile, tile, tile], [VMEM] * 7, name="last",
    )(first_got, got, zero, one, coeff, *near_args)
    got = lax.all_to_all(
        chunks.reshape(devices, 1, BLOCK), AXES, 0, 0, axis_index_groups=listed
    )
    packed = shaped(PACKED, ROWS, BLOCK)
    mine, theirs = call(pack_kernel, [packed, packed], [VMEM] * 6, name="pack")(
        zero, one, two, coeff, low, high
    )
    kept, known, terms = call(
        keep_kernel,
        [shaped(ITERS + 1, ROWS, panels), tile, shaped(TERMS, ROWS, BLOCK)], [VMEM] * 5,
        name="keep",
    )(
        mine, swapped(theirs, 1), swapped(mine, devices // 2), swapped(theirs, devices // 2 ^ 1),
        mirror_rows,
    )
    basis, hessenberg = call(
        functools.partial(final_kernel, total),
        [shaped(ITERS + 1, ROWS, panels), shaped(ITERS, ITERS + 1, ROWS)], [VMEM] * 4,
        name="final",
    )(got.reshape(devices, BLOCK), kept, known, terms)
    return basis[:, None], hessenberg.transpose(2, 1, 0)


def solution(mesh):
    placed = (
        P("side", None, ("grp", "dev")),
        P("side", ("grp", "dev"), None, None),
        P("side", ("grp", "dev")),
        P("side", ("grp", "dev")),
        P(("grp", "dev")),
    )
    return jax.shard_map(
        on_device,
        mesh=mesh,
        in_specs=placed,
        out_specs=(P(None, "side", None, ("grp", "dev")), P()),
        check_vma=False,
    )
```

```python
import functools

import jax
import jax.numpy as jnp
from jax import lax
from jax.experimental import pallas as pl
from jax.experimental.pallas import tpu as pltpu
from jax.sharding import PartitionSpec as P

BLOCK = 128
BLK_DEV = 2
ITERS = 3
ROWS = 8
HALF_RHS = 4
EPSILON = 1e-06
AXES = ("side", "grp", "dev")
VMEM_LIMIT = 48 * 2**20
LENGTH_LANE = ITERS * (ITERS + 1)
START_LANE = LENGTH_LANE + 1
PACKED = ITERS + 2
TINY = 1e-30


def position():
    side = lax.axis_index("side")
    dev = lax.axis_index("dev")
    owner = lax.axis_index("grp") * lax.axis_size("dev") + dev
    return side, owner, lax.rem(dev, 2)


def iota(shape, axis):
    return lax.broadcasted_iota(jnp.int32, shape, axis)


def per_rhs(tile):
    column = jnp.sum(tile, axis=1, keepdims=True)
    return column + jnp.concatenate([column[HALF_RHS:], column[:HALF_RHS]], axis=0)


def dot(left, right):
    return per_rhs(jnp.sum(left * right, axis=0))


def columns(values):
    lane = iota((ROWS, BLOCK), 1)
    tile = jnp.zeros((ROWS, BLOCK), jnp.float32)
    for index, value in values.items():
        tile = jnp.where(lane == index, value, tile)
    return tile


def mirror_onehot(mirror_ref, block):
    return (iota((BLOCK, BLOCK), 0) == mirror_ref[block : block + 1, :]).astype(jnp.float32)


def exact_dot(left, right, dims):
    return lax.dot_general(
        left, right, (dims, ((), ())),
        precision=lax.Precision.HIGHEST, preferred_element_type=jnp.float32,
    )


def start_kernel(sources_hbm, mirror_hbm, rows_hbm, cols_hbm, chunk_ref, mirror_ref, places_ref,
                 sources_ref, sems):
    copies = [
        pltpu.make_async_copy(sources_hbm, sources_ref, sems.at[0]),
        pltpu.make_async_copy(mirror_hbm, mirror_ref, sems.at[1]),
        pltpu.make_async_copy(rows_hbm, places_ref.at[0], sems.at[2]),
        pltpu.make_async_copy(cols_hbm, places_ref.at[1], sems.at[3]),
    ]
    for copy in copies:
        copy.start()
    for copy in copies:
        copy.wait()
    side, _, _ = position()
    pieces = []
    for block in range(BLK_DEV):
        part = sources_ref[:, block * BLOCK : (block + 1) * BLOCK]
        places = jnp.broadcast_to(mirror_ref[block : block + 1, :], part.shape)
        moved = jnp.take_along_axis(part, places, axis=1, mode="promise_in_bounds")
        pieces.append(jnp.where(side == 0, part, moved))
    tiles = [
        jnp.concatenate([piece[HALF_RHS * c : HALF_RHS * (c + 1)] for piece in pieces], axis=0)
        for c in range(2)
    ]
    chips = chunk_ref.shape[0] // 2

    def store(chip, carry):
        chunk_ref[2 * chip + 1] = tiles[0]
        chunk_ref[2 * chip + 2] = tiles[1]
        return carry

    chunk_ref[0] = tiles[0]
    lax.fori_loop(0, chips - 1, store, 0, unroll=chips <= 32)
    chunk_ref[2 * chips - 1] = tiles[1]


def prepare_kernel(own_hbm, other_ref, own_places, other_places, weights_ref, pick_ref, own_ref,
                   sem):
    copy = pltpu.make_async_copy(own_hbm, own_ref, sem)
    copy.start()
    width = pick_ref.shape[1]
    half_of_row = iota((ROWS, width), 0) // HALF_RHS
    rhs_of_row = iota((ROWS, width), 0) % HALF_RHS
    lane = iota((ROWS, width), 1)
    for entry in range(own_ref.shape[0]):
        picks = []
        for places in (own_places, other_places):
            place = jnp.where(
                half_of_row == places[0, 0, entry], HALF_RHS * places[1, 0, entry] + rhs_of_row, -1
            )
            picks.append((lane == place).astype(jnp.float32))
        first = 2 * ROWS * entry
        pick_ref[first : first + 2 * ROWS, :] = jnp.concatenate(picks, axis=0).astype(jnp.bfloat16)
    for side, ref in ((1, other_ref), (0, own_ref)):
        if side == 0:
            copy.wait()
        for entry in range(own_ref.shape[0]):
            first = entry % 2 * BLOCK
            weights_ref[
                entry // 2, first : first + BLOCK, side * BLOCK : (side + 1) * BLOCK
            ] = ref[entry].T


def near(half, pick_ref, weights_ref):
    flat = half.reshape(-1, BLOCK)
    coarse = flat.astype(jnp.bfloat16)
    fine = (flat - coarse.astype(jnp.float32)).astype(jnp.bfloat16)
    picked = lax.dot_general(
        pick_ref[...], jnp.concatenate([coarse, fine], axis=1), (((1,), (0,)), ((), ())),
        preferred_element_type=jnp.float32,
    ).astype(jnp.bfloat16)
    sums = [jnp.zeros((4 * ROWS, 2 * BLOCK), jnp.float32) for _ in range(4)]
    for group in range(weights_ref.shape[0]):
        rows = [
            slice(2 * ROWS * place, 2 * ROWS * (place + 1)) for place in (2 * group, 2 * group + 1)
        ]
        left = jnp.concatenate(
            [
                jnp.concatenate([picked[rows[0], part], picked[rows[1], part]], axis=1)
                for part in (slice(0, BLOCK), slice(BLOCK, 2 * BLOCK))
            ],
            axis=0,
        )
        sums[group % 4] += lax.dot_general(
            left, weights_ref[group], (((1,), (0,)), ((), ())), preferred_element_type=jnp.float32
        )
    total = (sums[0] + sums[1]) + (sums[2] + sums[3])
    total = total[: 2 * ROWS] + total[2 * ROWS :]
    _, _, core = position()
    own = total[:ROWS, :BLOCK]
    other = total[ROWS:, BLOCK:]
    return jnp.where(core == 0, own, other), jnp.where(core == 0, other, own)


def spread(chunk_ref, low, high):
    chips = chunk_ref.shape[0]

    def store(chip, carry):
        chunk_ref[chip, 0] = low
        chunk_ref[chip, 1] = high
        return carry

    lax.fori_loop(0, chips, store, 0, unroll=chips <= 32)


def first_kernel(total, got_ref, pick_ref, weights_ref, chunk_ref, basis_ref, coeff_ref):
    side, _, _ = position()
    owners = got_ref.shape[0] // 2
    last = 2 * owners - 1
    port = got_ref[1 : owners + 1]
    star = jnp.concatenate([got_ref[owners + 1 : last], got_ref[:1], got_ref[last:]], axis=0)
    half = jnp.where(side == 0, port + star, port - star)
    tiles = near(half, pick_ref, weights_ref)
    squares = per_rhs(jnp.sum(port * port + star * star, axis=0)) * (1.0 / total) + EPSILON
    own = dot(half, half) * (0.5 / total)
    scale = lax.rsqrt(jnp.maximum(own, TINY))
    coeff_ref[...] = columns(
        {LENGTH_LANE: jnp.sqrt(squares), START_LANE: jnp.sqrt(own) * lax.rsqrt(squares)}
    )
    basis_ref[...] = half * scale
    spread(chunk_ref, *[tile * scale for tile in tiles])


def in_order(got_ref, shift):
    chips = got_ref.shape[0]
    return jnp.concatenate([got_ref[chips - shift :], got_ref[: chips - shift]], axis=0)


def own_tiles(got_ref, shift):
    _, owner, _ = position()
    chips = got_ref.shape[0]
    chip = lax.rem(owner // 2 + chips - shift, chips)
    return got_ref[chip, 0], got_ref[chip, 1]


def advanced(total, shift, got_refs, basis_refs, pick_ref, weights_ref):
    got = in_order(got_refs[-1], shift).reshape(basis_refs[0].shape)
    tiles = near(got, pick_ref, weights_ref)
    inner = 0.5 / total
    coeffs = [dot(got, ref[...]) * inner for ref in basis_refs]
    rest = got
    for coeff, ref in zip(coeffs, basis_refs):
        rest = rest - coeff * ref[...]
    squares = dot(rest, rest) * inner
    scale = lax.rsqrt(jnp.maximum(squares, TINY))
    owned = [own_tiles(ref, shift) for ref in got_refs]
    parts = []
    for place, value in enumerate(tiles):
        for coeff, earlier in zip(coeffs, owned):
            value = value - coeff * earlier[place]
        parts.append(value * scale)
    return coeffs + [jnp.sqrt(squares)], rest * scale, parts


def middle_kernel(total, shift, got_ref, basis_ref, known_ref, pick_ref, weights_ref,
                  chunk_ref, next_ref, coeff_ref):
    coeffs, next_ref[...], parts = advanced(
        total, shift, [got_ref], [basis_ref], pick_ref, weights_ref
    )
    coeff_ref[...] = columns(dict(enumerate(coeffs))) + known_ref[...]
    spread(chunk_ref, *parts)


def last_kernel(total, shift, first_got_ref, got_ref, zero_ref, one_ref, known_ref, pick_ref,
                weights_ref, chunk_ref, two_ref, coeff_ref, low_ref, high_ref):
    _, owner, core = position()
    refs = [zero_ref, one_ref, two_ref]
    coeffs, two_ref[...], tiles = advanced(
        total, shift, [first_got_ref, got_ref], refs[:2], pick_ref, weights_ref
    )
    base = owner - core
    rhs = iota((ROWS, BLOCK), 0)
    lane = iota((ROWS, BLOCK), 1)
    spots = jnp.zeros((ROWS, BLOCK), jnp.float32)
    for index in range(ITERS + 1):
        if index < ITERS:
            product = tiles[0] * refs[index][base] + tiles[1] * refs[index][base + 1]
        else:
            product = tiles[0] * tiles[0] + tiles[1] * tiles[1]
        column = jnp.sum(product, axis=1, keepdims=True)
        spots = jnp.where(lane == ROWS * index + rhs, column, spots)
    row = jnp.sum(spots, axis=0, keepdims=True)
    chunk_ref[...] = jnp.broadcast_to(row, chunk_ref.shape)
    coeffs = columns({place + ITERS + 1: value for place, value in enumerate(coeffs)})
    coeff_ref[...] = coeffs + known_ref[...]
    low_ref[...] = tiles[0]
    high_ref[...] = tiles[1]


def pack_kernel(zero_ref, one_ref, two_ref, coeff_ref, low_ref, high_ref, mine_ref, theirs_ref):
    _, owner, core = position()
    for out_ref, which in ((mine_ref, core), (theirs_ref, 1 - core)):
        for index, ref in enumerate((zero_ref, one_ref, two_ref)):
            out_ref[index] = ref[owner - core + which]
        out_ref[ITERS] = jnp.where(which == 0, low_ref[...], high_ref[...])
        out_ref[ITERS + 1] = coeff_ref[...]


def over_halves(products):
    return sum(one * other for one, other in products)


def squared(vector):
    return over_halves([(value, value) for half in vector for value in half])


def keep_kernel(mine_ref, partner_ref, across_ref, flipped_ref, mirror_ref, kept_ref, known_ref,
                terms_ref):
    side, _, core = position()
    packed = []
    for index in range(PACKED):
        mine, partner = mine_ref[index], partner_ref[index]
        across, flipped = across_ref[index], flipped_ref[index]
        here = [jnp.where(core == 0, mine, partner), jnp.where(core == 0, partner, mine)]
        there = [jnp.where(core == 0, across, flipped), jnp.where(core == 0, flipped, across)]
        packed.append(
            [
                [jnp.where(side == 0, h, t) for h, t in zip(here, there)],
                [jnp.where(side == 0, t, h) for h, t in zip(here, there)],
            ]
        )
    known = [
        jnp.concatenate([tile[:HALF_RHS] for tile in packed[ITERS + 1][half]], axis=0)
        for half in range(2)
    ]

    def entry(half, j, k):
        place = k * (ITERS + 1) + j
        return known[half][:, place : place + 1]

    halves = range(2)
    length = known[0][:, LENGTH_LANE : LENGTH_LANE + 1]
    start = [known[half][:, START_LANE : START_LANE + 1] for half in halves]
    zero = [[start[half]] for half in halves]
    ahead = [[entry(half, 0, 0) * zero[half][0], entry(half, 1, 0) * zero[half][0]] for half in halves]
    short = [EPSILON / (length * length)]
    product = over_halves([(ahead[half][0], zero[half][0]) for half in halves])
    multiple = product - 0.5 * short[0]
    rest = [[ahead[half][0] - multiple * zero[half][0], ahead[half][1]] for half in halves]
    squares = squared(rest) + EPSILON
    norms = [jnp.sqrt(squares)]
    one = [[value * lax.rsqrt(squares) for value in rest[half]] for half in halves]
    heads = {(0, 0): product + 0.5 * squared(zero), (1, 0): norms[0]}
    short.append(EPSILON / squares)
    cross = heads[0, 0] * short[0] / norms[0]
    ahead = [
        [
            entry(half, 0, 0) * one[half][0] + entry(half, 0, 1) * one[half][1],
            entry(half, 1, 0) * one[half][0] + entry(half, 1, 1) * one[half][1],
            entry(half, 2, 1) * one[half][1],
        ]
        for half in halves
    ]
    product = over_halves([pair for half in halves for pair in zip(ahead[half], one[half])])
    multiples = [
        over_halves([(ahead[half][0], zero[half][0]) for half in halves]) + 0.5 * cross,
        product - 0.5 * short[1],
    ]
    rest = [
        [
            ahead[half][0] - multiples[0] * zero[half][0] - multiples[1] * one[half][0],
            ahead[half][1] - multiples[1] * one[half][1],
            ahead[half][2],
        ]
        for half in halves
    ]
    squares = squared(rest) + EPSILON
    norms.append(jnp.sqrt(squares))
    two = [[value * lax.rsqrt(squares) for value in rest[half]] for half in halves]
    heads.update({(0, 1): multiples[0], (1, 1): product + 0.5 * squared(one), (2, 1): norms[1]})
    short.append(EPSILON / squares)
    crosses = [
        (heads[0, 1] * short[0] - heads[1, 1] * cross) / norms[1],
        (heads[1, 1] * short[1] - heads[0, 1] * cross) / norms[1],
    ]
    ahead = [
        [
            entry(half, 0, 0) * two[half][0] + entry(half, 0, 1) * two[half][1],
            entry(half, 1, 0) * two[half][0] + entry(half, 1, 1) * two[half][1],
            entry(half, 2, 1) * two[half][1],
        ]
        for half in halves
    ]
    known_ref[...] = columns({k * (ITERS + 1) + j: value for (j, k), value in heads.items()})
    terms = [0.5 * crosses[0], 0.5 * crosses[1], -0.5 * short[2]]
    for half in halves:
        terms += zero[half] + one[half] + two[half] + ahead[half]
    for index, value in enumerate(terms):
        terms_ref[index] = jnp.broadcast_to(value, (ROWS, BLOCK))
    for block in range(BLK_DEV):
        rows = slice(block * HALF_RHS, (block + 1) * HALF_RHS)
        vectors = []
        for half in halves:
            parts = [
                jnp.concatenate([tile[rows] for tile in packed[index][half]], axis=0)
                for index in range(ITERS + 1)
            ]
            vectors.append(
                [
                    over_halves(zip(weights, parts))
                    for weights in (
                        zero[half], one[half], two[half], ahead[half] + [two[half][2]]
                    )
                ]
            )
        ports = [0.5 * (sym + anti) for sym, anti in zip(*vectors)]
        stars = [0.5 * (sym - anti) for sym, anti in zip(*vectors)]
        back = exact_dot(
            jnp.concatenate(stars, axis=0), mirror_onehot(mirror_ref, block), ((1,), (1,))
        )
        for index, port in enumerate(ports):
            kept_ref[index, :, block * BLOCK : (block + 1) * BLOCK] = jnp.where(
                side == 0, port, back[index * ROWS : (index + 1) * ROWS]
            )


TERMS = 3 + 2 * 9


def final_kernel(total, got_ref, kept_ref, known_ref, terms_ref, basis_ref, hessenberg_ref):
    inner = 0.5 / total
    got = got_ref[...]
    devices = got.shape[0]
    place = iota(got.shape, 0)
    device = jnp.where(
        place == 0, devices - 2, jnp.where(place == devices - 1, devices - 1, place - 1)
    )
    rhs = iota((ROWS, BLOCK), 0)
    lane = iota((ROWS, BLOCK), 1)
    halves = range(2)
    values = []
    for half in halves:
        here = (device >= devices // 2) if half == 1 else (device < devices // 2)
        even = device % 2 == 0
        lower = jnp.sum(jnp.where(here & even, got, 0.0), axis=0, keepdims=True)
        upper = jnp.sum(jnp.where(here & ~even, got, 0.0), axis=0, keepdims=True)
        spots = jnp.where(rhs < HALF_RHS, lower, upper) * inner
        values.append(
            [
                jnp.sum(
                    jnp.where(
                        (lane // ROWS == index) & (lane % HALF_RHS == rhs % HALF_RHS), spots, 0.0
                    ),
                    axis=1,
                    keepdims=True,
                )
                for index in range(ITERS + 1)
            ]
        )
    terms = [terms_ref[index] for index in range(TERMS)]
    zero, one, two, ahead = [], [], [], []
    for half in halves:
        own = terms[3 + 9 * half : 12 + 9 * half]
        zero.append(own[0:1])
        one.append(own[1:3])
        two.append(own[3:6])
        ahead.append(
            [known + own[5] * value for known, value in zip(own[6:9], values[half][:ITERS])]
        )
    products = [
        over_halves([pair for half in halves for pair in zip(ahead[half], vector[half])])
        for vector in (zero, one, two)
    ]
    multiples = [product + term for product, term in zip(products, terms[:3])]
    squares = jnp.full((ROWS, BLOCK), EPSILON, jnp.float32)
    for half in halves:
        beyond = values[half][ITERS]
        for value in values[half][:ITERS]:
            beyond = beyond - value * value
        squares = squares + jnp.maximum(beyond, 0.0) * two[half][2] * two[half][2]
        for index in range(ITERS):
            value = ahead[half][index]
            for multiple, vector in zip(multiples, (zero, one, two)):
                if index < len(vector[half]):
                    value = value - multiple * vector[half][index]
            squares = squares + value * value
    scale = lax.rsqrt(squares)
    basis_ref[:ITERS] = kept_ref[:ITERS]
    for block in range(BLK_DEV):
        span = slice(block * BLOCK, (block + 1) * BLOCK)
        rest = kept_ref[ITERS, :, span]
        for j in range(ITERS):
            rest = rest - multiples[j] * kept_ref[j, :, span]
        basis_ref[ITERS, :, span] = rest * scale
    place = 2 * (ITERS + 1)
    coeffs = multiples[:-1] + [products[-1] + 0.5 * squared(two), jnp.sqrt(squares)]
    whole = known_ref[...] + columns({place + index: value for index, value in enumerate(coeffs)})
    turned = whole.T
    for k in range(ITERS):
        hessenberg_ref[k] = turned[k * (ITERS + 1) : (k + 1) * (ITERS + 1), :]


VMEM = pl.BlockSpec(memory_space=pltpu.VMEM)
SMEM = pl.BlockSpec(memory_space=pltpu.SMEM)
HBM = pl.BlockSpec(memory_space=pltpu.HBM)


def shaped(*shape, dtype=jnp.float32):
    return jax.ShapeDtypeStruct(shape, dtype)


def in_hbm(value):
    return pltpu.with_memory_space_constraint(value, pltpu.HBM)


def call(kernel, outs, specs, scratch=(), name=None):
    return pl.pallas_call(
        kernel,
        out_shape=outs,
        in_specs=specs,
        out_specs=[VMEM] * len(outs),
        scratch_shapes=scratch,
        compiler_params=pltpu.CompilerParams(vmem_limit_bytes=VMEM_LIMIT),
        name=name,
    )


def on_device(sources, near_blocks, block_rows, block_cols, mirror):
    devices = lax.axis_size(AXES)
    owners = devices // 2
    chips = devices // 2
    panels = sources.shape[2]
    total = 1.0 * panels * devices
    shift = 5 % (chips // 2)
    groups = [
        [
            2 * (side * (chips // 2) + (chip + shift) % (chips // 2)) + core
            for chip in range(chips // 2)
        ]
        for side in range(2)
        for core in range(2)
    ]
    listed = [[devices - 2, *range(devices - 2), devices - 1]]
    mirror_rows = mirror.reshape(BLK_DEV, BLOCK)
    blocks = near_blocks[0]
    everything = shaped(devices, ROWS, BLOCK)
    vector = shaped(owners, ROWS, BLOCK)
    chunk = shaped(chips // 2, 2, ROWS, BLOCK)
    tile = shaped(ROWS, BLOCK)

    def swapped(value, bits):
        return lax.ppermute(value, AXES, [(i, i ^ bits) for i in range(devices)])

    def exchanged(chunks):
        return lax.all_to_all(chunks, AXES, 0, 0, axis_index_groups=groups)

    chunks, mirror_rows, places = call(
        start_kernel,
        [
            everything,
            shaped(*mirror_rows.shape, dtype=jnp.int32),
            shaped(2, *block_rows.shape, dtype=jnp.int32),
        ],
        [HBM] * 4,
        [pltpu.VMEM(sources.shape[1:], jnp.float32), pltpu.SemaphoreType.DMA((4,))],
        name="start",
    )(in_hbm(sources[0]), in_hbm(mirror_rows), in_hbm(block_rows), in_hbm(block_cols))
    chunks, blocks = lax.optimization_barrier((chunks, blocks))
    got = lax.all_to_all(chunks, AXES, 0, 0, axis_index_groups=listed)
    other_blocks = swapped(blocks, 1)
    weights, pick = call(
        prepare_kernel,
        [
            shaped(blocks.shape[0] // 2, 2 * BLOCK, 2 * BLOCK, dtype=blocks.dtype),
            shaped(2 * ROWS * blocks.shape[0], owners * ROWS, dtype=jnp.bfloat16),
        ],
        [HBM, VMEM, SMEM, SMEM],
        [pltpu.VMEM(blocks.shape, blocks.dtype), pltpu.SemaphoreType.DMA],
        name="prepare",
    )(in_hbm(blocks), other_blocks, places, swapped(places, 1))
    near_args = (pick, weights)
    chunks, zero, coeff = call(
        functools.partial(first_kernel, total), [chunk, vector, tile], [VMEM] * 3, name="first"
    )(got, *near_args)
    got = exchanged(chunks)
    chunks, one, coeff = call(
        functools.partial(middle_kernel, total, shift), [chunk, vector, tile], [VMEM] * 5,
        name="middle",
    )(got, zero, coeff, *near_args)
    first_got, got = got, exchanged(chunks)
    chunks, two, coeff, low, high = call(
        functools.partial(last_kernel, total, shift),
        [shaped(devices, BLOCK), vector, tile, tile, tile], [VMEM] * 7, name="last",
    )(first_got, got, zero, one, coeff, *near_args)
    got = lax.all_to_all(
        chunks.reshape(devices, 1, BLOCK), AXES, 0, 0, axis_index_groups=listed
    )
    packed = shaped(PACKED, ROWS, BLOCK)
    mine, theirs = call(pack_kernel, [packed, packed], [VMEM] * 6, name="pack")(
        zero, one, two, coeff, low, high
    )
    kept, known, terms = call(
        keep_kernel,
        [shaped(ITERS + 1, ROWS, panels), tile, shaped(TERMS, ROWS, BLOCK)], [VMEM] * 5,
        name="keep",
    )(
        mine, swapped(theirs, 1), swapped(mine, devices // 2), swapped(theirs, devices // 2 ^ 1),
        mirror_rows,
    )
    basis, hessenberg = call(
        functools.partial(final_kernel, total),
        [shaped(ITERS + 1, ROWS, panels), shaped(ITERS, ITERS + 1, ROWS)], [VMEM] * 4,
        name="final",
    )(got.reshape(devices, BLOCK), kept, known, terms)
    return basis[:, None], hessenberg.transpose(2, 1, 0)


def solution(mesh):
    placed = (
        P("side", None, ("grp", "dev")),
        P("side", ("grp", "dev"), None, None),
        P("side", ("grp", "dev")),
        P("side", ("grp", "dev")),
        P(("grp", "dev")),
    )
    return jax.shard_map(
        on_device,
        mesh=mesh,
        in_specs=placed,
        out_specs=(P(None, "side", None, ("grp", "dev")), P()),
        check_vma=False,
    )
```
